32 devices in a mesh: groups: 2 (over y), seq: 4 (over z), dp: 4 (over x, core).
Axes of the slice: x: 2, y: 2, z: 4, core: 2. Of those that a mesh axis runs over, the one named last changes fastest.
Arguments:
- x_raw: bfloat16 [1024, 8192], P(('groups', 'seq'), 'dp'), parts along dimension 0, may hold values from -6 to 6
- bc_raw: bfloat16 [1024, 2048], P(('groups', 'seq'), 'dp'), parts along dimension 0, may hold values from -6 to 6
- z_gate: bfloat16 [1024, 8192], P(('groups', 'seq'), 'dp'), parts along dimension 0, may hold values from -6 to 6
- dt_raw: float32 [1024, 128], P(('groups', 'seq'), 'dp'), parts along dimension 0, may hold values from -3 to 6
- conv_x_weight: float32 [4, 8192], P(None, 'dp'), may hold values from -3 to 3
- conv_x_bias: float32 [8192], P('dp'), may hold values from -3 to 3
- conv_bc_weight: float32 [4, 2048], P(None, 'dp'), may hold values from -3 to 3
- conv_bc_bias: float32 [2048], P('dp'), may hold values from -3 to 3
- dt_bias: float32 [128], P('dp'), may hold values from -1 to 1
- a_log: float32 [128], P('dp')
- skip_d: float32 [128], P('dp'), may hold values from 0.5 to 1.5
- norm_gain: float32 [8192], P('dp'), may hold values from 0.5 to 1.5
- queries: bfloat16 [1024, 4096], P(('groups', 'seq'), 'dp'), parts along dimension 0, may hold values from -6 to 6
- keys: bfloat16 [1024, 1024], P(('groups', 'seq'), 'dp'), parts along dimension 0, may hold values from -6 to 6
- values: bfloat16 [1024, 1024], P(('groups', 'seq'), 'dp'), parts along dimension 0, may hold values from -6 to 6
- doc_lens: int32 [8], P('groups'), parts along dimension 0, may hold values from 1 to 256, 512 in all
Outputs:
- mamba_out: bfloat16 [1024, 8192], P(('groups', 'seq'), 'dp'), parts along dimension 0
- attn_out: bfloat16 [1024, 4096], P(('groups', 'seq'), 'dp'), parts along dimension 0
The draws below stay inside these ranges and needn't reach their ends.
There are 2 independent parts, one for each index of `groups`. The reference program is written for one: setup_inputs(seed, part) draws one part's arguments, and reference() takes and returns one part's arrays. A program takes and returns all parts, laid end to end along the dimension named above; an argument that names none is the same for every part. Nothing has to cross between parts.
Inputs may be any that keep to these rules, and one draw needn't show every extreme that they name: doc_lens holds 4 document lengths that sum to 512; the longest is exactly 256.
All inputs are finite; a program needn't handle non-finite values.
Results may differ from the reference program's by a relative error of at most 0.018.
Values may be sent and summed in bfloat16 or wider, within the bound.
A program may use at most 128 MiB of HBM per device.

```python
import math
import jax
import jax.numpy as jnp
import numpy as np
from jax import lax

HEADS = 128
HDIM = 64
STATE = 128
GROUPS = 8
CONV = 4
QHEADS = 32
KVHEADS = 8
ADIM = 128
TOK_DEV = 128
DOCS = 4
STREAM_LENGTH = 512


def draw_queries(key, part):
    noise_key = jax.random.fold_in(key, 1)
    field = jnp.clip(jax.random.normal(noise_key, (STREAM_LENGTH, QHEADS * ADIM), jnp.float32), -6.0, 6.0)
    return field.astype(jnp.bfloat16)


def draw_keys(key, part):
    noise_key = jax.random.fold_in(key, 2)
    field = jnp.clip(jax.random.normal(noise_key, (STREAM_LENGTH, KVHEADS * ADIM), jnp.float32), -6.0, 6.0)
    return field.astype(jnp.bfloat16)


def draw_dt_raw(key, part):
    noise_key = jax.random.fold_in(key, 3)
    cluster_prng_seed = jax.random.fold_in(key, 4)
    field = jnp.clip(0.5 * jax.random.normal(noise_key, (STREAM_LENGTH, HEADS), jnp.float32), -3.0, 3.0)
    flagged_spots = jax.random.randint(cluster_prng_seed, (8,), 0, STREAM_LENGTH)
    field = field.at[flagged_spots].add(3.0)
    return jnp.clip(field, -3.0, 6.0)


def draw_a_log(key, part):
    marker_random_key = jax.random.fold_in(key, 5)
    level_key = jax.random.fold_in(key, 6)
    slow = jax.random.bernoulli(marker_random_key, 0.5, (HEADS,))
    level = jax.random.uniform(level_key, (HEADS,), jnp.float32, 0.0, 1.0)
    slow_rate = jnp.exp(jnp.log(0.2 / STREAM_LENGTH) + level * jnp.log(10.0))
    fast_rate = jnp.exp(jnp.log(1.0 / 400.0) + level * jnp.log(400.0 / 30.0))
    return jnp.log(jnp.where(slow, slow_rate, fast_rate) / 0.7)


def shard_levels(stream_key, extent, pieces, least, top_value):
    loudness = 1.0
    for axis_at, blocks in pieces:
        draws = jax.random.uniform(jax.random.fold_in(jax.random.fold_in(stream_key, 6), axis_at), (blocks,), jnp.float32, least / len(pieces), top_value / len(pieces))
        loudness = loudness * jnp.repeat(jnp.exp(draws), extent[axis_at] // blocks).reshape((-1,) + (1,) * (len(extent) - 1 - axis_at))
    return loudness


def profile(number_of, total, reach, lean):
    loads = [(1 << 20) // math.isqrt(grade ** lean) + 1 for grade in range(2, number_of + 1)]
    spare, counts = total - reach - (number_of - 1), [1] * (number_of - 1)
    while spare > 0:
        free = [i for i in range(number_of - 1) if counts[i] < reach]
        whole, budget = sum([loads[i] for i in free]), spare
        for i in free:
            addition = min(reach - counts[i], max(1, budget * loads[i] // whole), spare)
            counts[i] = counts[i] + addition
            spare = spare - addition
    return np.array([reach] + counts)


def uneven_parts(stream_key, number_of, total, bound, skew):
    if number_of == 2:
        one = jax.random.randint(stream_key, (), max(1, total - bound), min(bound, total - 1) + 1)
        return jnp.stack([one, total - one])
    tallies = jnp.asarray(profile(number_of, total, bound, skew), jnp.int32)
    pairs = (number_of - 1) // 2
    donor, taker = tallies[1:1 + 2 * pairs:2], tallies[2:2 + 2 * pairs:2]
    margin = jnp.minimum(donor - 1, bound - taker)
    shifted = jax.random.randint(jax.random.fold_in(stream_key, 1), (pairs,), 0, 1 << 20) % (margin + 1)
    tallies = tallies.at[1:1 + 2 * pairs:2].set(donor - shifted).at[2:2 + 2 * pairs:2].set(taker + shifted)
    return tallies[jax.random.permutation(jax.random.fold_in(stream_key, 2), number_of)]


def bell_draw(own_key, dims, scale, limit, cuts=(), kind=jnp.bfloat16):
    array = scale * jax.random.normal(own_key, dims, jnp.float32)
    if cuts:
        array = array * shard_levels(own_key, dims, cuts, -0.22, 0.18)
    return jnp.clip(array, -limit, limit).astype(kind)


def setup_inputs(seed: int = 0, part: int = 0) -> dict:
    key_of = jax.random.split(jax.random.key(seed), 17)
    part_splits = jax.random.split(jax.random.fold_in(key_of[16], part), 17)
    return {
        "x_raw": bell_draw(part_splits[0], (STREAM_LENGTH, HEADS * HDIM), 1.0, 6.0, ((0, 4), (1, 4))),
        "bc_raw": bell_draw(part_splits[1], (STREAM_LENGTH, 2 * GROUPS * STATE), 1.0, 6.0, ((0, 4), (1, 4))),
        "z_gate": bell_draw(part_splits[2], (STREAM_LENGTH, HEADS * HDIM), 1.0, 6.0, ((0, 4), (1, 4))),
        "dt_raw": draw_dt_raw(jax.random.fold_in(jax.random.fold_in(key_of[16], part), 71), part),
        "conv_x_weight": bell_draw(key_of[4], (CONV, HEADS * HDIM), CONV ** -0.5, 3.0, ((1, 4),), jnp.float32),
        "conv_x_bias": bell_draw(key_of[5], (HEADS * HDIM,), 0.5, 3.0, ((0, 4),), jnp.float32),
        "conv_bc_weight": bell_draw(key_of[6], (CONV, 2 * GROUPS * STATE), CONV ** -0.5, 3.0, ((1, 4),), jnp.float32),
        "conv_bc_bias": bell_draw(key_of[7], (2 * GROUPS * STATE,), 0.5, 3.0, ((0, 4),), jnp.float32),
        "dt_bias": jnp.clip(jax.random.uniform(key_of[8], (HEADS,), jnp.float32, -1.0, 1.0) * shard_levels(key_of[8], (HEADS,), ((0, 4),), -0.4, 0.0), -1.0, 1.0),
        "a_log": draw_a_log(jax.random.fold_in(key_of[16], 71), part),
        "skip_d": jnp.clip(0.5 + 1.0 * jax.random.uniform(key_of[10], (HEADS,), jnp.float32) ** shard_levels(key_of[10], (HEADS,), ((0, 4),), -0.2, 0.2), 0.5, 1.5),
        "norm_gain": jnp.clip(1.0 + 0.1 * jax.random.normal(key_of[11], (HEADS * HDIM,), jnp.float32), 0.5, 1.5),
        "queries": draw_queries(jax.random.fold_in(jax.random.fold_in(key_of[16], part), 71), part),
        "keys": draw_keys(jax.random.fold_in(jax.random.fold_in(key_of[16], part), 71), part),
        "values": bell_draw(part_splits[14], (STREAM_LENGTH, KVHEADS * ADIM), 1.0, 6.0, ((0, 4), (1, 4))),
        "doc_lens": uneven_parts(part_splits[15], DOCS, STREAM_LENGTH, STREAM_LENGTH // 2, 2).astype(jnp.int32),
    }


EPSILON = 1e-05
NEGATIVE = -1e+30
HIGHEST = lax.Precision.HIGHEST

def doc_starts(doc_lens):
    ends = jnp.cumsum(doc_lens).astype(jnp.int32)
    return (ends - doc_lens).astype(jnp.int32)

def doc_index(positions, starts):
    inside = (starts[None, :] <= positions[:, None]).astype(jnp.int32)
    return (lax.optimization_barrier(jnp.sum(inside, axis=1)) - 1).astype(jnp.int32)

def causal_conv(padded, pad_docs, docs, weight, bias):
    count = docs.shape[0]
    total = jnp.zeros((count, bias.shape[0]), jnp.float32) + bias[None, :]
    for lag in range(weight.shape[0]):
        term = padded[lag:lag + count].astype(jnp.float32) * weight[lag][None, :]
        same = pad_docs[lag:lag + count] == docs
        total = total + jnp.where(same[:, None], term, 0.0)
    return jax.nn.silu(total).astype(jnp.bfloat16)

def ssd_terms(head_values, b_groups, c_groups, step_size, log_decay, begins):
    rows, heads, width = head_values.shape
    group_total_count = b_groups.shape[1]
    per_group = heads // group_total_count
    running = jnp.cumsum(log_decay, axis=0)
    segment = jnp.cumsum(begins.astype(jnp.int32), axis=0).astype(jnp.int32)
    order = jnp.arange(rows, dtype=jnp.int32)
    linked = (segment[:, None] == segment[None, :]) & (order[:, None] >= order[None, :])
    spread = running.T[:, :, None] - running.T[:, None, :]
    multiplier = jnp.where(linked[None], jnp.exp(jnp.where(linked[None], spread, 0.0)), 0.0)
    intersection = jnp.einsum('ign,jgn->gij', c_groups, b_groups, preferred_element_type=jnp.float32)
    intersection = jnp.repeat(intersection, per_group, axis=0)
    scaled = head_values.astype(jnp.float32) * step_size[:, :, None]
    output = jnp.einsum('hij,jhp->ihp', multiplier * intersection, scaled, precision=HIGHEST)
    entry = jnp.where((segment == 0)[:, None], jnp.exp(running), 0.0)
    tail_weight = jnp.where((segment == segment[-1])[:, None], jnp.exp(running[-1][None, :] - running), 0.0)
    weighted = (scaled * tail_weight[:, :, None]).reshape(rows, group_total_count, per_group, width)
    local_state = jnp.einsum('jgqp,jgn->gqpn', weighted, b_groups.astype(jnp.float32), precision=HIGHEST)
    local_state = local_state.reshape(heads, width, -1)
    through = jnp.where(segment[-1] == 0, jnp.exp(running[-1]), 0.0)
    return (output, entry, local_state, through)

def apply_state(c_groups, state):
    heads, width, size = state.shape
    group_total_count = c_groups.shape[1]
    grouped = state.reshape(group_total_count, heads // group_total_count, width, size)
    result = jnp.einsum('ign,gqpn->igqp', c_groups.astype(jnp.float32), grouped, precision=HIGHEST)
    return result.reshape(c_groups.shape[0], heads, width)

def gated_norm(mixed, z_gate, norm_gain, group_total_count):
    count = mixed.shape[0]
    gated = mixed * jax.nn.silu(z_gate.astype(jnp.float32)).reshape(mixed.shape)
    grouped = gated.reshape(count, group_total_count, -1)
    multiplier = lax.rsqrt(lax.optimization_barrier(jnp.mean(grouped * grouped, axis=-1, keepdims=True)) + EPSILON)
    return ((grouped * multiplier).reshape(count, -1) * norm_gain[None, :]).astype(jnp.bfloat16)

def reference(x_raw, bc_raw, z_gate, dt_raw, conv_x_weight, conv_x_bias, conv_bc_weight, conv_bc_bias, dt_bias, a_log, skip_d, norm_gain, queries, keys, values, doc_lens):
    starts = doc_starts(doc_lens)
    positions = jnp.arange(STREAM_LENGTH, dtype=jnp.int32)
    docs = doc_index(positions, starts)
    pad_positions = jnp.arange(STREAM_LENGTH + CONV - 1, dtype=jnp.int32) - (CONV - 1)
    pad_docs = doc_index(pad_positions, starts)
    begins = jnp.any(starts[None, :] == positions[:, None], axis=1)
    x_pad = jnp.concatenate([jnp.zeros((CONV - 1, x_raw.shape[1]), x_raw.dtype), x_raw], axis=0)
    bc_pad = jnp.concatenate([jnp.zeros((CONV - 1, bc_raw.shape[1]), bc_raw.dtype), bc_raw], axis=0)
    x_conv = causal_conv(x_pad, pad_docs, docs, conv_x_weight, conv_x_bias)
    bc_conv = causal_conv(bc_pad, pad_docs, docs, conv_bc_weight, conv_bc_bias)
    step_size = jax.nn.softplus(dt_raw + dt_bias[None, :])
    log_decay = -step_size * jnp.exp(a_log)[None, :]
    blocks = STREAM_LENGTH // TOK_DEV
    value_blocks = x_conv.reshape(blocks, TOK_DEV, HEADS, HDIM)
    paired = bc_conv.reshape(blocks, TOK_DEV, GROUPS, 2, STATE)

    def advance(state, block):
        head_values, pair_block, steps, logs, starts_here = block
        b_groups = pair_block[:, :, 0]
        c_groups = pair_block[:, :, 1]
        output, entry, local_state, through = ssd_terms(head_values, b_groups, c_groups, steps, logs, starts_here)
        output = output + apply_state(c_groups, state) * entry[:, :, None]
        return (state * through[:, None, None] + local_state, output)
    initial = jnp.zeros((HEADS, HDIM, STATE), jnp.float32)
    _, outputs = lax.scan(advance, initial, (value_blocks, paired, step_size.reshape(blocks, TOK_DEV, HEADS), log_decay.reshape(blocks, TOK_DEV, HEADS), begins.reshape(blocks, TOK_DEV)))
    mixed = outputs.reshape(STREAM_LENGTH, HEADS, HDIM) + skip_d[None, :, None] * x_conv.reshape(STREAM_LENGTH, HEADS, HDIM).astype(jnp.float32)
    mamba_out = gated_norm(mixed, z_gate, norm_gain, GROUPS)
    share = QHEADS // KVHEADS
    scale = ADIM ** (-0.5)
    query_heads = queries.reshape(STREAM_LENGTH, KVHEADS, share, ADIM).transpose(1, 0, 2, 3)
    key_heads = keys.reshape(STREAM_LENGTH, KVHEADS, ADIM).transpose(1, 0, 2)
    value_heads = values.reshape(STREAM_LENGTH, KVHEADS, ADIM).transpose(1, 0, 2)

    def head_attend(operands):
        asking_head_index, key_head, value_head = operands

        def block_attend(block_index):
            query_block = lax.dynamic_slice_in_dim(asking_head_index, block_index * TOK_DEV, TOK_DEV, 0)
            row_positions = block_index * TOK_DEV + jnp.arange(TOK_DEV, dtype=jnp.int32)
            row_docs = lax.dynamic_slice_in_dim(docs, block_index * TOK_DEV, TOK_DEV, 0)
            scores = jnp.einsum('tga,ja->gtj', query_block.astype(jnp.float32), key_head.astype(jnp.float32), precision=HIGHEST) * scale
            permitted_mask = (positions[None, :] <= row_positions[:, None]) & (docs[None, :] == row_docs[:, None])
            scores = jnp.where(permitted_mask[None], scores, NEGATIVE)
            peak = lax.optimization_barrier(jnp.max(scores, axis=-1, keepdims=True))
            expo = jnp.where(permitted_mask[None], jnp.exp(scores - peak), 0.0)
            probs = expo.astype(jnp.bfloat16)
            total = lax.optimization_barrier(jnp.sum(expo, axis=-1))
            summed = jnp.einsum('gtj,ja->gta', probs.astype(jnp.float32), value_head.astype(jnp.float32), precision=HIGHEST)
            return (summed / total[:, :, None]).transpose(1, 0, 2)
        return lax.map(block_attend, jnp.arange(blocks, dtype=jnp.int32))
    attended = lax.map(head_attend, (query_heads, key_heads, value_heads))
    attn_out = attended.transpose(1, 2, 0, 3, 4).reshape(STREAM_LENGTH, QHEADS * ADIM).astype(jnp.bfloat16)
    return (mamba_out, attn_out)
```

```python
import functools
import jax
import jax.numpy as jnp
from jax import lax
from jax.experimental import pallas as pl
from jax.experimental.pallas import tpu as pltpu
from jax.sharding import PartitionSpec as P

HDIM = 64
STATE = 128
QHEADS = 32
KVHEADS = 8
ADIM = 128
EPSILON = 1e-05
NEGATIVE = -1e30
LOG2E = 1.4426950408889634
HIGHEST = lax.Precision.HIGHEST
F32 = jnp.float32
BF16 = jnp.bfloat16
CHUNK = 256
NT = (((1,), (1,)), ((), ()))


def silu(value):
    half = 0.5 * value
    return half + half * jnp.tanh(half)


def dot(a, b):
    return jnp.dot(a, b, preferred_element_type=F32)


def wide(tile, width):
    return jnp.concatenate([tile] * (width // tile.shape[1]), axis=1)


def relay_kernel(
    n,
    reach,
    x_hbm, bc_hbm, z_hbm, dt_hbm, cxw_hbm, cxb_hbm, cbw_hbm, cbb_hbm,
    dtb_hbm, alog_hbm, skip_hbm, gain_hbm, q_hbm, k_hbm, v_hbm, lens_hbm,
    mamba_ref,
    attn_ref,
    halo_out,
    halo_in,
    kv,
    state_in,
    state_out,
    xf,
    bcf,
    xc,
    gated,
    gate_entry,
    small_send,
    small_recv,
    kv_send,
    kv_recv,
    st_send,
    st_recv,
    fetch_sem,
    x_tail,
    x_ref, bc_ref, z_ref, dt_ref, cxw_ref, cxb_ref, cbw_ref, cbb_ref,
    dtb_ref, alog_ref, skip_ref, gain_ref, q_ref, k_ref, v_ref, lens_ref,
):
    here = lax.axis_index("seq")
    rows, width = x_ref.shape
    fetches = [
        pltpu.make_async_copy(source, target, fetch_sem.at[i])
        for i, (source, target) in enumerate(
            (
                (x_hbm.at[pl.ds(rows - 16, 16), :], x_tail),
                (bc_hbm, bc_ref),
                (lens_hbm, lens_ref),
                (dt_hbm, dt_ref),
                (dtb_hbm, dtb_ref),
                (alog_hbm, alog_ref),
                (skip_hbm, skip_ref),
                (cbw_hbm, cbw_ref),
                (cbb_hbm, cbb_ref),
                (cxw_hbm, cxw_ref),
                (cxb_hbm, cxb_ref),
                (x_hbm, x_ref),
                (z_hbm, z_ref),
                (k_hbm, k_ref),
                (v_hbm, v_ref),
                (q_hbm, q_ref),
                (gain_hbm, gain_ref),
            )
        )
    ]
    for fetch in fetches:
        fetch.start()
    bc_width = bc_ref.shape[1]
    heads = dt_ref.shape[0]
    groups = bc_width // (2 * STATE)
    chunks = width // CHUNK
    group_width = width // groups
    taps = cxw_ref.shape[0]
    margin = taps - 1
    has_left = here > 0
    has_right = here < n - 1
    right = {"seq": here + 1}

    def remote(src, dst, send, recv):
        return pltpu.make_async_remote_copy(
            src_ref=src,
            dst_ref=dst,
            send_sem=send,
            recv_sem=recv,
            device_id=right,
            device_id_type=pl.DeviceIdType.MESH,
        )

    barrier = pltpu.get_barrier_semaphore()

    @pl.when(has_left)
    def _():
        pl.semaphore_signal(
            barrier, inc=1, device_id={"seq": here - 1}, device_id_type=pl.DeviceIdType.MESH
        )

    @pl.when(has_right)
    def _():
        pl.semaphore_signal(
            barrier, inc=1, device_id={"seq": here + 1}, device_id_type=pl.DeviceIdType.MESH
        )

    fetches[0].wait()
    fetches[1].wait()
    blocks = width // bc_width
    tail_x = x_tail[...].astype(F32)[16 - margin :]
    tail_bc = bc_ref[rows - 16 :, :].astype(F32)[16 - margin :]
    pieces = [tail_x[:, b * bc_width : (b + 1) * bc_width] for b in range(blocks)] + [tail_bc]
    pieces.append(jnp.zeros((16 - margin * (blocks + 1), bc_width), F32))
    halo_out[...] = jnp.concatenate(pieces, axis=0).astype(BF16)

    @pl.when(has_left & has_right)
    def _():
        pl.semaphore_wait(barrier, 2)

    @pl.when(jnp.logical_not(has_left & has_right))
    def _():
        pl.semaphore_wait(barrier, 1)

    halo_copy = remote(halo_out, halo_in, small_send, small_recv)
    own_k = remote(k_hbm, kv.at[0, 0], kv_send.at[0, 0], kv_recv.at[0, 0])
    own_v = remote(v_hbm, kv.at[0, 1], kv_send.at[0, 1], kv_recv.at[0, 1])

    @pl.when(has_right)
    def _():
        halo_copy.start()
        own_k.start()
        own_v.start()

    for fetch in fetches[2:11]:
        fetch.wait()
    first = here * rows
    starts = []
    running_start = jnp.int32(0)
    for d in range(lens_ref.shape[0]):
        starts.append(running_start)
        running_start = running_start + lens_ref[d]

    def doc_of(positions):
        total = jnp.full(positions.shape, -1, jnp.int32)
        for start in starts:
            total = total + jnp.where(start <= positions, 1, 0)
        return total

    square = (rows, 128)
    pos_i = first + lax.broadcasted_iota(jnp.int32, square, 0)
    pos_j = first + lax.broadcasted_iota(jnp.int32, (rows, rows), 1)
    doc_i = doc_of(pos_i)
    doc_j = doc_of(pos_j)
    linked = (doc_i == doc_j) & (pos_i >= pos_j)
    before = doc_of(jnp.full((1, 128), first - 1, jnp.int32))
    last = doc_of(jnp.full((1, 128), first + rows - 1, jnp.int32))
    same = [
        jnp.where(doc_of(pos_i - (margin - lag)) == doc_i, 1.0, 0.0) for lag in range(margin)
    ]

    raw = dt_ref[...].T + dtb_ref[...]
    step = jnp.maximum(raw, 0.0) + jnp.log1p(jnp.exp(-jnp.abs(raw)))
    decay = step * (jnp.exp(alog_ref[...]) * (-LOG2E))
    order_i = lax.broadcasted_iota(jnp.int32, (rows, rows), 0)
    order_j = lax.broadcasted_iota(jnp.int32, (rows, rows), 1)
    lower = jnp.where(order_i >= order_j, 1.0, 0.0)
    running = jnp.dot(lower, decay, precision=HIGHEST, preferred_element_type=F32)
    final = running[rows - 1 : rows]
    row_of = (running - jnp.log2(step)).T
    tail = jnp.where(
        (doc_i == last)[:, :heads], jnp.exp2(final - running) * step, 0.0
    )
    entry = jnp.where((doc_i == before)[:, :heads], jnp.exp2(running), 0.0)
    through = jnp.where((last == before)[:, :heads], jnp.exp2(final), 0.0)
    stack = jnp.concatenate(
        [
            tail,
            entry,
            jnp.broadcast_to(through, (8, heads)),
            jnp.broadcast_to(skip_ref[...], (8, heads)),
        ],
        axis=0,
    )
    high = stack.astype(BF16)
    low = (stack - high.astype(F32)).astype(BF16)

    @pl.when(has_left)
    def _():
        halo_copy.wait_recv()

    @pl.when(here == 0)
    def _():
        halo_in[...] = jnp.zeros_like(halo_in)
        state_in[...] = jnp.zeros_like(state_in)

    for s in range(reach):
        @pl.when(here < s + 1)
        def _(s=s):
            kv[s] = jnp.zeros_like(kv[s])

    halo = halo_in[...].astype(F32)
    for b in range(blocks):
        xf[8 - margin : 8, b * bc_width : (b + 1) * bc_width] = halo[
            b * margin : (b + 1) * margin
        ]
    bcf[8 - margin : 8, :] = halo[blocks * margin : (blocks + 1) * margin]
    bcf[8:, :] = bc_ref[...].astype(F32)

    def conv(source, weight_ref, bias_ref, at, size):
        total = source[8 : 8 + rows, at : at + size] * weight_ref[margin : margin + 1, at : at + size]
        total = total + bias_ref[:, at : at + size]
        for lag in range(margin):
            moved = source[8 - margin + lag : 8 - margin + lag + rows, at : at + size]
            total = total + moved * weight_ref[lag : lag + 1, at : at + size] * wide(
                same[lag], size
            )
        return silu(total).astype(BF16)

    b_turned, c_groups, crossed = [], [], []
    for g in range(groups):
        b_here = conv(bcf, cbw_ref, cbb_ref, 2 * g * STATE, STATE)
        c_here = conv(bcf, cbw_ref, cbb_ref, (2 * g + 1) * STATE, STATE)
        b_turned.append(b_here.astype(F32).T.astype(BF16))
        c_groups.append(c_here)
        crossed.append(lax.dot_general(c_here, b_here, NT, preferred_element_type=F32))

    def state_copy(c):
        return remote(state_out.at[c], state_in.at[c], st_send.at[c], st_recv.at[c])

    lane_head = lax.broadcasted_iota(jnp.int32, (heads, CHUNK), 1) // HDIM
    head_row = lax.broadcasted_iota(jnp.int32, (heads, CHUNK), 0)
    per_chunk = CHUNK // HDIM
    low_half = lax.broadcasted_iota(jnp.int32, (rows, 128), 1) < HDIM

    fetches[11].wait()
    carried = []
    for c in range(chunks):
        at = c * CHUNK
        g = at // group_width
        xf[8:, at : at + CHUNK] = x_ref[:, at : at + CHUNK].astype(F32)
        x_here = conv(xf, cxw_ref, cxb_ref, at, CHUNK)
        xc[:, at : at + CHUNK] = x_here
        spread = jnp.where(head_row == lane_head + c * per_chunk, 1.0, 0.0).astype(BF16)
        expanded = dot(high, spread) + dot(low, spread)
        x32 = x_here.astype(F32)
        local = dot(b_turned[g], (x32 * expanded[:rows]).astype(BF16))
        gate_entry[:, at : at + CHUNK] = expanded[rows : 2 * rows]
        gated[:, at : at + CHUNK] = x32 * expanded[2 * rows + 8 : 2 * rows + 9]
        carried.append(expanded[2 * rows : 2 * rows + 1])
        state_out[c] = local.astype(BF16)

        @pl.when(here == 0)
        def _(c=c):
            state_copy(c).start()

    for s in range(1, reach):
        @pl.when(here >= s)
        def _(s=s):
            for i in range(2):
                remote(
                    kv.at[s - 1, i], kv.at[s - 1, i], kv_send.at[s - 1, i], kv_recv.at[s - 1, i]
                ).wait_recv()

        @pl.when((here >= s) & has_right)
        def _(s=s):
            for i in range(2):
                remote(
                    kv.at[s - 1, i], kv.at[s, i], kv_send.at[s, i], kv_recv.at[s, i]
                ).start()

    for fetch in fetches[12:]:
        fetch.wait()

    kv_local = k_ref.shape[1] // ADIM
    share = q_ref.shape[1] // (ADIM * kv_local)
    scale = ADIM**-0.5 * LOG2E
    key_count = (reach + 1) * rows
    key_pos = (
        first - reach * rows + lax.broadcasted_iota(jnp.int32, (rows, key_count), 1)
    )
    key_docs = doc_of(key_pos)
    permitted = (key_docs == wide(doc_i, key_count)) & (key_pos <= wide(pos_i, key_count))

    def attend(head):
        g = head // share
        cols = slice(g * ADIM, (g + 1) * ADIM)
        keys = jnp.concatenate(
            [kv[s, 0, :, cols] for s in reversed(range(reach))] + [k_ref[:, cols]], axis=0
        )
        values = jnp.concatenate(
            [kv[s, 1, :, cols] for s in reversed(range(reach))] + [v_ref[:, cols]], axis=0
        )
        query = q_ref[:, head * ADIM : (head + 1) * ADIM]
        scores = lax.dot_general(query, keys, NT, preferred_element_type=F32)
        scores = jnp.where(permitted, scores, NEGATIVE)
        peak = jnp.max(scores, axis=1, keepdims=True)
        expo = jnp.exp2((scores - peak) * scale)
        total = jnp.sum(expo, axis=1, keepdims=True)
        summed = dot(expo.astype(BF16), values)
        attn_ref[:, head * ADIM : (head + 1) * ADIM] = (summed / total).astype(BF16)

    q_heads = kv_local * share
    early = chunks // 4
    for c in range(chunks):
        at = c * CHUNK
        g = at // group_width
        gate = silu(z_ref[:, at : at + CHUNK].astype(F32))
        for pair in range(CHUNK // 128):
            col = at + pair * 128
            head = col // HDIM
            parts = []
            for h in (head, head + 1):
                exponent = running[:, h : h + 1] - row_of[h : h + 1, :]
                parts.append(
                    (jnp.exp2(jnp.where(linked, exponent, NEGATIVE)) * crossed[g]).astype(BF16)
                )
            x_pair = xc[:, col : col + 128]
            zero = jnp.zeros_like(x_pair)
            stacked = jnp.concatenate(
                [jnp.where(low_half, x_pair, zero), jnp.where(low_half, zero, x_pair)], axis=0
            )
            inside = dot(jnp.concatenate(parts, axis=1), stacked)
            gated[:, col : col + 128] = (gated[:, col : col + 128] + inside) * gate[
                :, pair * 128 : (pair + 1) * 128
            ]
        gate_entry[:, at : at + CHUNK] = gate_entry[:, at : at + CHUNK] * gate

        @pl.when(has_left)
        def _(c=c):
            state_copy(c).wait_recv()

        @pl.when(has_left & has_right)
        def _(c=c):
            state_out[c] = (
                state_out[c].astype(F32) + state_in[c].astype(F32) * carried[c]
            ).astype(BF16)
            state_copy(c).start()

        if c == early:
            @pl.when(here >= reach)
            def _():
                for i in range(2):
                    remote(
                        kv.at[reach - 1, i],
                        kv.at[reach - 1, i],
                        kv_send.at[reach - 1, i],
                        kv_recv.at[reach - 1, i],
                    ).wait_recv()

        if early <= c < chunks - 1:
            span = chunks - early - 1
            for head in range((c - early) * q_heads // span, (c - early + 1) * q_heads // span):
                attend(head)

        gated[:, at : at + CHUNK] = (
            gated[:, at : at + CHUNK]
            + dot(c_groups[g], state_in[c]) * gate_entry[:, at : at + CHUNK]
        )
        if (at + CHUNK) % group_width == 0:
            left = at + CHUNK - group_width
            value = gated[:, left : left + group_width]
            mean = jnp.sum(value * value, axis=1, keepdims=True) * (1.0 / group_width)
            mamba_ref[:, left : left + group_width] = (
                value * lax.rsqrt(mean + EPSILON) * gain_ref[:, left : left + group_width]
            ).astype(BF16)

    @pl.when(has_right)
    def _():
        halo_copy.wait_send()
        own_k.wait_send()
        own_v.wait_send()
        for c in range(chunks):
            state_copy(c).wait_send()

    for s in range(1, reach):
        @pl.when((here >= s) & has_right)
        def _(s=s):
            for i in range(2):
                remote(
                    kv.at[s - 1, i], kv.at[s, i], kv_send.at[s, i], kv_recv.at[s, i]
                ).wait_send()


SUB = 128


def packed_kernel(
    n,
    x_hbm, bc_hbm, z_hbm, dt_hbm, cxw_hbm, cxb_hbm, cbw_hbm, cbb_hbm,
    dtb_hbm, alog_hbm, skip_hbm, gain_hbm, q_hbm, k_hbm, v_hbm, lens_hbm,
    mamba_ref,
    attn_ref,
    halo_out,
    halo_in,
    kv,
    state_in,
    state_out,
    c_mine,
    c_next,
    xf,
    bcf,
    xc,
    gated,
    gate_entry,
    small_send,
    small_recv,
    kv_send,
    kv_recv,
    st_send,
    st_recv,
    c_sem,
    fetch_sem,
    x_tail,
    x_ref, bc_ref, z_ref, dt_ref, cxw_ref, cxb_ref, cbw_ref, cbb_ref,
    dtb_ref, alog_ref, skip_ref, gain_ref, q_ref, k_ref, v_ref, lens_ref,
):
    here = lax.axis_index("seq")
    rows, width = x_ref.shape
    fetches = [
        pltpu.make_async_copy(source, target, fetch_sem.at[i])
        for i, (source, target) in enumerate(
            (
                (x_hbm.at[pl.ds(rows - 16, 16), :], x_tail),
                (bc_hbm, bc_ref),
                (lens_hbm, lens_ref),
                (dt_hbm, dt_ref),
                (dtb_hbm, dtb_ref),
                (alog_hbm, alog_ref),
                (skip_hbm, skip_ref),
                (cbw_hbm, cbw_ref),
                (cbb_hbm, cbb_ref),
                (cxw_hbm, cxw_ref),
                (cxb_hbm, cxb_ref),
                (x_hbm, x_ref),
                (z_hbm, z_ref),
                (k_hbm, k_ref),
                (v_hbm, v_ref),
                (q_hbm, q_ref),
                (gain_hbm, gain_ref),
            )
        )
    ]
    for fetch in fetches:
        fetch.start()
    bc_width = bc_ref.shape[1]
    heads = dt_ref.shape[0]
    groups = bc_width // (2 * STATE)
    chunks = width // CHUNK
    per = CHUNK // SUB
    group_width = width // groups
    taps = cxw_ref.shape[0]
    margin = taps - 1
    has_left = here > 0
    has_right = here < n - 1
    middle = has_left & has_right

    def remote(src, dst, send, recv, to=1):
        return pltpu.make_async_remote_copy(
            src_ref=src,
            dst_ref=dst,
            send_sem=send,
            recv_sem=recv,
            device_id={"seq": here + to},
            device_id_type=pl.DeviceIdType.MESH,
        )

    barrier = pltpu.get_barrier_semaphore()

    @pl.when(has_left)
    def _():
        pl.semaphore_signal(
            barrier, inc=1, device_id={"seq": here - 1}, device_id_type=pl.DeviceIdType.MESH
        )

    @pl.when(has_right)
    def _():
        pl.semaphore_signal(
            barrier, inc=1, device_id={"seq": here + 1}, device_id_type=pl.DeviceIdType.MESH
        )

    fetches[0].wait()
    fetches[1].wait()
    blocks = width // bc_width
    tail_x = x_tail[...].astype(F32)[16 - margin :]
    tail_bc = bc_ref[rows - 16 :, :].astype(F32)[16 - margin :]
    pieces = [tail_x[:, b * bc_width : (b + 1) * bc_width] for b in range(blocks)] + [tail_bc]
    pieces.append(jnp.zeros((16 - margin * (blocks + 1), bc_width), F32))
    halo_out[...] = jnp.concatenate(pieces, axis=0).astype(BF16)

    @pl.when(middle)
    def _():
        pl.semaphore_wait(barrier, 2)

    @pl.when(jnp.logical_not(middle))
    def _():
        pl.semaphore_wait(barrier, 1)

    halo_copy = remote(halo_out, halo_in, small_send, small_recv)
    own_k = remote(k_hbm, kv.at[0], kv_send.at[0], kv_recv.at[0])
    own_v = remote(v_hbm, kv.at[1], kv_send.at[1], kv_recv.at[1])
    c_back = remote(c_mine, c_next, c_sem.at[0], c_sem.at[1], -1)

    @pl.when(has_right)
    def _():
        halo_copy.start()
        own_k.start()
        own_v.start()

    for fetch in fetches[2:11]:
        fetch.wait()
    first = here * rows
    starts = []
    running_start = jnp.int32(0)
    for d in range(lens_ref.shape[0]):
        starts.append(running_start)
        running_start = running_start + lens_ref[d]

    def doc_of(positions):
        total = jnp.full(positions.shape, -1, jnp.int32)
        for start in starts:
            total = total + jnp.where(start <= positions, 1, 0)
        return total

    def doc_at(position):
        return doc_of(jnp.full((1, 128), position, jnp.int32))

    square = (rows, 128)
    pos_i = first + lax.broadcasted_iota(jnp.int32, square, 0)
    pos_j = first + lax.broadcasted_iota(jnp.int32, (rows, rows), 1)
    doc_i = doc_of(pos_i)
    doc_j = doc_of(pos_j)
    linked = (doc_i == doc_j) & (pos_i >= pos_j)
    before = doc_at(first - 1)
    last = doc_at(first + rows - 1)
    same = [
        jnp.where(doc_of(pos_i - (margin - lag)) == doc_i, 1.0, 0.0) for lag in range(margin)
    ]
    ahead = doc_of(pos_i + rows) == before
    spare = (doc_at(first + rows) == before) & jnp.logical_not(ahead)
    rows_came = doc_at(first - rows - 1) == doc_at(first)

    raw = dt_ref[...].T + dtb_ref[...]
    step = jnp.maximum(raw, 0.0) + jnp.log1p(jnp.exp(-jnp.abs(raw)))
    decay = step * (jnp.exp(alog_ref[...]) * (-LOG2E))
    order_i = lax.broadcasted_iota(jnp.int32, (rows, rows), 0)
    order_j = lax.broadcasted_iota(jnp.int32, (rows, rows), 1)
    unit = jnp.where(order_i == order_j, 1.0, 0.0)
    lower = jnp.where(order_i >= order_j, 1.0, 0.0)
    running = jnp.dot(lower, decay, precision=HIGHEST, preferred_element_type=F32)
    final = running[rows - 1 : rows]
    row_of = (running - jnp.log2(step)).T
    tail = jnp.where(
        (doc_i == last)[:, :heads], jnp.exp2(final - running) * step, 0.0
    )
    entry = jnp.where((doc_i == before)[:, :heads], jnp.exp2(running), 0.0)
    through = jnp.where((last == before)[:, :heads], jnp.exp2(final), 0.0)
    stack = jnp.concatenate(
        [
            tail,
            entry,
            jnp.broadcast_to(through, (8, heads)),
            jnp.broadcast_to(skip_ref[...], (8, heads)),
        ],
        axis=0,
    )
    high = stack.astype(BF16)
    low = (stack - high.astype(F32)).astype(BF16)

    @pl.when(has_left)
    def _():
        halo_copy.wait_recv()

    @pl.when(here == 0)
    def _():
        halo_in[...] = jnp.zeros_like(halo_in)
        state_in[...] = jnp.zeros_like(state_in)
        kv[...] = jnp.zeros_like(kv)

    halo = halo_in[...].astype(F32)
    for b in range(blocks):
        xf[8 - margin : 8, b * bc_width : (b + 1) * bc_width] = halo[
            b * margin : (b + 1) * margin
        ]
    bcf[8 - margin : 8, :] = halo[blocks * margin : (blocks + 1) * margin]
    bcf[8:, :] = bc_ref[...].astype(F32)

    def conv(source, weight_ref, bias_ref, at, size):
        total = source[8 : 8 + rows, at : at + size] * weight_ref[margin : margin + 1, at : at + size]
        total = total + bias_ref[:, at : at + size]
        for lag in range(margin):
            moved = source[8 - margin + lag : 8 - margin + lag + rows, at : at + size]
            total = total + moved * weight_ref[lag : lag + 1, at : at + size] * wide(
                same[lag], size
            )
        return silu(total).astype(BF16)

    b_turned, c_groups, crossed = [], [], []
    for g in range(groups):
        b_here = conv(bcf, cbw_ref, cbb_ref, 2 * g * STATE, STATE)
        c_here = conv(bcf, cbw_ref, cbb_ref, (2 * g + 1) * STATE, STATE)
        b_turned.append(b_here.astype(F32).T.astype(BF16))
        c_mine[g] = c_here
        c_groups.append(jnp.where(rows_came, unit, c_here.astype(F32)).astype(BF16))
        crossed.append(lax.dot_general(c_here, b_here, NT, preferred_element_type=F32))

    @pl.when(here >= 2)
    def _():
        c_back.start()

    def state_copy(i):
        return remote(state_out.at[i], state_in.at[i], st_send.at[i], st_recv.at[i])

    kv_local = k_ref.shape[1] // ADIM
    lane_head = lax.broadcasted_iota(jnp.int32, (heads, CHUNK), 1) // HDIM
    head_row = lax.broadcasted_iota(jnp.int32, (heads, CHUNK), 0)
    per_chunk = CHUNK // HDIM
    low_half = lax.broadcasted_iota(jnp.int32, (rows, 128), 1) < HDIM
    carried = []

    def make_local(c):
        at = c * CHUNK
        g = at // group_width
        xf[8:, at : at + CHUNK] = x_ref[:, at : at + CHUNK].astype(F32)
        x_here = conv(xf, cxw_ref, cxb_ref, at, CHUNK)
        xc[:, at : at + CHUNK] = x_here
        spread = jnp.where(head_row == lane_head + c * per_chunk, 1.0, 0.0).astype(BF16)
        expanded = dot(high, spread) + dot(low, spread)
        x32 = x_here.astype(F32)
        local = dot(b_turned[g], (x32 * expanded[:rows]).astype(BF16)).astype(BF16)
        gate_entry[:, at : at + CHUNK] = expanded[rows : 2 * rows]
        gated[:, at : at + CHUNK] = x32 * expanded[2 * rows + 8 : 2 * rows + 9]
        carried.append(expanded[2 * rows : 2 * rows + 1])
        for i in range(per):
            state_out[c * per + i] = local[:, i * SUB : (i + 1) * SUB]

        @pl.when(here == 0)
        def _():
            for i in range(per):
                state_copy(c * per + i).start()

    def pass_on(c):
        g = c * CHUNK // group_width

        @pl.when(middle)
        def _():
            for i in range(per):
                at = c * per + i
                state_copy(at).wait_recv()
                state = state_out[at].astype(F32) + state_in[at].astype(F32) * carried[c][
                    :, i * SUB : (i + 1) * SUB
                ]
                sent = dot(c_next[g], state.astype(BF16))
                if at < 2 * kv_local:
                    col = at % kv_local * ADIM
                    sent = jnp.where(
                        spare, kv[at // kv_local, :, col : col + ADIM].astype(F32), sent
                    )
                state_out[at] = sent.astype(BF16)
                state_copy(at).start()

    def arrive(c):
        @pl.when(here == n - 1)
        def _():
            for i in range(per):
                state_copy(c * per + i).wait_recv()

    share = q_ref.shape[1] // (ADIM * kv_local)
    q_heads = kv_local * share
    scale = ADIM**-0.5 * LOG2E

    def permitted_keys():
        count = 3 * rows
        key_pos = first - 2 * rows + lax.broadcasted_iota(jnp.int32, (rows, count), 1)
        return (doc_of(key_pos) == wide(doc_i, count)) & (key_pos <= wide(pos_i, count))

    def attend(head, permitted):
        g = head // share
        cols = slice(g * ADIM, (g + 1) * ADIM)
        keys = jnp.concatenate([state_in[g], kv[0, :, cols], k_ref[:, cols]], axis=0)
        values = jnp.concatenate([state_in[kv_local + g], kv[1, :, cols], v_ref[:, cols]], axis=0)
        query = q_ref[:, head * ADIM : (head + 1) * ADIM]
        scores = lax.dot_general(query, keys, NT, preferred_element_type=F32)
        scores = jnp.where(permitted, scores, NEGATIVE)
        peak = jnp.max(scores, axis=1, keepdims=True)
        expo = jnp.exp2((scores - peak) * scale)
        total = jnp.sum(expo, axis=1, keepdims=True)
        summed = dot(expo.astype(BF16), values)
        attn_ref[:, head * ADIM : (head + 1) * ADIM] = (summed / total).astype(BF16)

    def inside(c):
        at = c * CHUNK
        g = at // group_width
        gate = silu(z_ref[:, at : at + CHUNK].astype(F32))
        for pair in range(CHUNK // 128):
            col = at + pair * 128
            head = col // HDIM
            parts = []
            for h in (head, head + 1):
                exponent = running[:, h : h + 1] - row_of[h : h + 1, :]
                parts.append(
                    (jnp.exp2(jnp.where(linked, exponent, NEGATIVE)) * crossed[g]).astype(BF16)
                )
            x_pair = xc[:, col : col + 128]
            zero = jnp.zeros_like(x_pair)
            stacked = jnp.concatenate(
                [jnp.where(low_half, x_pair, zero), jnp.where(low_half, zero, x_pair)], axis=0
            )
            within = dot(jnp.concatenate(parts, axis=1), stacked)
            gated[:, col : col + 128] = (gated[:, col : col + 128] + within) * gate[
                :, pair * 128 : (pair + 1) * 128
            ]
        gate_entry[:, at : at + CHUNK] = gate_entry[:, at : at + CHUNK] * gate

    def finish(c):
        at = c * CHUNK
        g = at // group_width
        came = jnp.concatenate([state_in[c * per + i] for i in range(per)], axis=1)
        gated[:, at : at + CHUNK] = (
            gated[:, at : at + CHUNK]
            + dot(c_groups[g], came) * gate_entry[:, at : at + CHUNK]
        )
        if (at + CHUNK) % group_width == 0:
            left = at + CHUNK - group_width
            value = gated[:, left : left + group_width]
            mean = jnp.sum(value * value, axis=1, keepdims=True) * (1.0 / group_width)
            mamba_ref[:, left : left + group_width] = (
                value * lax.rsqrt(mean + EPSILON) * gain_ref[:, left : left + group_width]
            ).astype(BF16)

    fetches[11].wait()
    lag = chunks // 2
    for c in range(chunks):
        make_local(c)
        if c == lag - 1:
            @pl.when(has_left)
            def _():
                own_k.wait_recv()
                own_v.wait_recv()

            @pl.when(middle)
            def _():
                c_back.wait_recv()
                for g in range(groups):
                    c_next[g] = jnp.where(ahead, c_next[g].astype(F32), unit).astype(BF16)
        if c >= lag:
            pass_on(c - lag)

    for fetch in fetches[12:]:
        fetch.wait()
    left_over = list(range(chunks - lag, chunks))
    for c in range(chunks):
        inside(c)
        if c % 4 == 1 and len(left_over) > 2:
            pass_on(left_over.pop(0))
    arrive(0)
    arrive(1)
    permitted = permitted_keys()
    for head in range(q_heads):
        attend(head, permitted)
        if head % 4 == 3 and left_over:
            pass_on(left_over.pop(0))
    for c in left_over:
        pass_on(c)
    for c in range(chunks):
        if c > 1:
            arrive(c)
        finish(c)

    @pl.when(has_right)
    def _():
        halo_copy.wait_send()
        own_k.wait_send()
        own_v.wait_send()
        for i in range(chunks * per):
            state_copy(i).wait_send()

    @pl.when(here >= 2)
    def _():
        c_back.wait_send()


def write_out(mamba_ref, attn_ref, mamba_hbm, attn_hbm, sems):
    copies = [
        pltpu.make_async_copy(mamba_ref, mamba_hbm, sems.at[0]),
        pltpu.make_async_copy(attn_ref, attn_hbm, sems.at[1]),
    ]
    for copy in copies:
        copy.start()
    for copy in copies:
        copy.wait()


def shards(n, *args):
    (
        x_raw, bc_raw, z_gate, dt_raw, cxw, cxb, cbw, cbb, dtb, a_log, skip_d, gain, queries, keys,
        values, doc_lens,
    ) = args
    operands = (
        x_raw, bc_raw, z_gate, dt_raw.T, cxw, cxb[None], cbw, cbb[None], dtb[None], a_log[None],
        skip_d[None], gain[None], queries, keys, values, doc_lens,
    )
    rows, width = x_raw.shape
    bc_width = bc_raw.shape[1]
    chunks = width // CHUNK
    reach = max(1, n // 2)
    vmem = pl.BlockSpec(memory_space=pltpu.VMEM)
    dma = pltpu.SemaphoreType.DMA
    if reach == 2 and rows == STATE and keys.shape[1] == CHUNK and 2 * CHUNK <= width:
        subs = width // SUB
        state = pltpu.VMEM((subs, STATE, SUB), BF16)
        turned = pltpu.VMEM((bc_width // (2 * STATE), rows, STATE), BF16)
        body = functools.partial(packed_kernel, n)
        buffers = [pltpu.VMEM((2,) + keys.shape, BF16), state, state, turned, turned]
        sems = [dma((2,)), dma((2,)), dma((subs,)), dma((subs,)), dma((2,))]
    else:
        state = pltpu.VMEM((chunks, STATE, CHUNK), BF16)
        body = functools.partial(relay_kernel, n, reach)
        buffers = [pltpu.VMEM((reach, 2) + keys.shape, BF16), state, state]
        sems = [dma((reach, 2)), dma((reach, 2)), dma((chunks,)), dma((chunks,))]
    results = pl.pallas_call(
        body,
        out_shape=(pltpu.VMEM((rows, width), BF16), pltpu.VMEM(queries.shape, BF16)),
        in_specs=[pl.BlockSpec(memory_space=pltpu.HBM)] * 16,
        out_specs=(vmem, vmem),
        scratch_shapes=[
            pltpu.VMEM((16, bc_width), BF16),
            pltpu.VMEM((16, bc_width), BF16),
        ]
        + buffers
        + [
            pltpu.VMEM((rows + 8, width), F32),
            pltpu.VMEM((rows + 8, bc_width), F32),
            pltpu.VMEM((rows, width), BF16),
            pltpu.VMEM((rows, width), F32),
            pltpu.VMEM((rows, width), F32),
            dma,
            dma,
        ]
        + sems
        + [dma((17,)), pltpu.VMEM((16, width), BF16)]
        + [pltpu.VMEM(a.shape, a.dtype) for a in operands[:-1]]
        + [pltpu.SMEM(doc_lens.shape, jnp.int32)],
        compiler_params=pltpu.CompilerParams(
            collective_id=0, has_side_effects=True, vmem_limit_bytes=60 * 1024 * 1024
        ),
    )(*operands)
    hbm = pl.BlockSpec(memory_space=pltpu.HBM)
    return pl.pallas_call(
        write_out,
        out_shape=(
            jax.ShapeDtypeStruct((rows, width), BF16),
            jax.ShapeDtypeStruct(queries.shape, BF16),
        ),
        in_specs=[vmem, vmem],
        out_specs=(hbm, hbm),
        scratch_shapes=[dma((2,))],
    )(*[pltpu.with_memory_space_constraint(r, pltpu.VMEM) for r in results])


def solution(mesh):
    both = P(("groups", "seq"), "dp")
    placed = (
        both, both, both, both, P(None, "dp"), P("dp"), P(None, "dp"), P("dp"), P("dp"), P("dp"),
        P("dp"), P("dp"), both, both, both, P("groups"),
    )
    return jax.shard_map(
        functools.partial(shards, mesh.shape["seq"]),
        mesh=mesh,
        in_specs=placed,
        out_specs=(both, both),
        check_vma=False,
    )
```

```python
import functools
import jax
import jax.numpy as jnp
from jax import lax
from jax.experimental import pallas as pl
from jax.experimental.pallas import tpu as pltpu
from jax.sharding import PartitionSpec as P

HDIM = 64
STATE = 128
QHEADS = 32
KVHEADS = 8
ADIM = 128
EPSILON = 1e-05
NEGATIVE = -1e30
LOG2E = 1.4426950408889634
HIGHEST = lax.Precision.HIGHEST
F32 = jnp.float32
BF16 = jnp.bfloat16
CHUNK = 256
NT = (((1,), (1,)), ((), ()))


def silu(value):
    half = 0.5 * value
    return half + half * jnp.tanh(half)


def dot(a, b):
    return jnp.dot(a, b, preferred_element_type=F32)


def wide(tile, width):
    return jnp.concatenate([tile] * (width // tile.shape[1]), axis=1)


def relay_kernel(
    n,
    reach,
    x_hbm, bc_hbm, z_hbm, dt_hbm, cxw_hbm, cxb_hbm, cbw_hbm, cbb_hbm,
    dtb_hbm, alog_hbm, skip_hbm, gain_hbm, q_hbm, k_hbm, v_hbm, lens_hbm,
    mamba_ref,
    attn_ref,
    halo_out,
    halo_in,
    kv,
    state_in,
    state_out,
    xf,
    bcf,
    xc,
    gated,
    gate_entry,
    small_send,
    small_recv,
    kv_send,
    kv_recv,
    st_send,
    st_recv,
    fetch_sem,
    x_tail,
    x_ref, bc_ref, z_ref, dt_ref, cxw_ref, cxb_ref, cbw_ref, cbb_ref,
    dtb_ref, alog_ref, skip_ref, gain_ref, q_ref, k_ref, v_ref, lens_ref,
):
    here = lax.axis_index("seq")
    rows, width = x_ref.shape
    fetches = [
        pltpu.make_async_copy(source, target, fetch_sem.at[i])
        for i, (source, target) in enumerate(
            (
                (x_hbm.at[pl.ds(rows - 16, 16), :], x_tail),
                (bc_hbm, bc_ref),
                (lens_hbm, lens_ref),
                (dt_hbm, dt_ref),
                (dtb_hbm, dtb_ref),
                (alog_hbm, alog_ref),
                (skip_hbm, skip_ref),
                (cbw_hbm, cbw_ref),
                (cbb_hbm, cbb_ref),
                (cxw_hbm, cxw_ref),
                (cxb_hbm, cxb_ref),
                (x_hbm, x_ref),
                (z_hbm, z_ref),
                (k_hbm, k_ref),
                (v_hbm, v_ref),
                (q_hbm, q_ref),
                (gain_hbm, gain_ref),
            )
        )
    ]
    for fetch in fetches:
        fetch.start()
    bc_width = bc_ref.shape[1]
    heads = dt_ref.shape[0]
    groups = bc_width // (2 * STATE)
    chunks = width // CHUNK
    group_width = width // groups
    taps = cxw_ref.shape[0]
    margin = taps - 1
    has_left = here > 0
    has_right = here < n - 1
    right = {"seq": here + 1}

    def remote(src, dst, send, recv):
        return pltpu.make_async_remote_copy(
            src_ref=src,
            dst_ref=dst,
            send_sem=send,
            recv_sem=recv,
            device_id=right,
            device_id_type=pl.DeviceIdType.MESH,
        )

    barrier = pltpu.get_barrier_semaphore()

    @pl.when(has_left)
    def _():
        pl.semaphore_signal(
            barrier, inc=1, device_id={"seq": here - 1}, device_id_type=pl.DeviceIdType.MESH
        )

    @pl.when(has_right)
    def _():
        pl.semaphore_signal(
            barrier, inc=1, device_id={"seq": here + 1}, device_id_type=pl.DeviceIdType.MESH
        )

    fetches[0].wait()
    fetches[1].wait()
    blocks = width // bc_width
    tail_x = x_tail[...].astype(F32)[16 - margin :]
    tail_bc = bc_ref[rows - 16 :, :].astype(F32)[16 - margin :]
    pieces = [tail_x[:, b * bc_width : (b + 1) * bc_width] for b in range(blocks)] + [tail_bc]
    pieces.append(jnp.zeros((16 - margin * (blocks + 1), bc_width), F32))
    halo_out[...] = jnp.concatenate(pieces, axis=0).astype(BF16)

    @pl.when(has_left & has_right)
    def _():
        pl.semaphore_wait(barrier, 2)

    @pl.when(jnp.logical_not(has_left & has_right))
    def _():
        pl.semaphore_wait(barrier, 1)

    halo_copy = remote(halo_out, halo_in, small_send, small_recv)
    own_k = remote(k_hbm, kv.at[0, 0], kv_send.at[0, 0], kv_recv.at[0, 0])
    own_v = remote(v_hbm, kv.at[0, 1], kv_send.at[0, 1], kv_recv.at[0, 1])

    @pl.when(has_right)
    def _():
        halo_copy.start()
        own_k.start()
        own_v.start()

    for fetch in fetches[2:11]:
        fetch.wait()
    first = here * rows
    starts = []
    running_start = jnp.int32(0)
    for d in range(lens_ref.shape[0]):
        starts.append(running_start)
        running_start = running_start + lens_ref[d]

    def doc_of(positions):
        total = jnp.full(positions.shape, -1, jnp.int32)
        for start in starts:
            total = total + jnp.where(start <= positions, 1, 0)
        return total

    square = (rows, 128)
    pos_i = first + lax.broadcasted_iota(jnp.int32, square, 0)
    pos_j = first + lax.broadcasted_iota(jnp.int32, (rows, rows), 1)
    doc_i = doc_of(pos_i)
    doc_j = doc_of(pos_j)
    linked = (doc_i == doc_j) & (pos_i >= pos_j)
    before = doc_of(jnp.full((1, 128), first - 1, jnp.int32))
    last = doc_of(jnp.full((1, 128), first + rows - 1, jnp.int32))
    same = [
        jnp.where(doc_of(pos_i - (margin - lag)) == doc_i, 1.0, 0.0) for lag in range(margin)
    ]

    raw = dt_ref[...].T + dtb_ref[...]
    step = jnp.maximum(raw, 0.0) + jnp.log1p(jnp.exp(-jnp.abs(raw)))
    decay = step * (jnp.exp(alog_ref[...]) * (-LOG2E))
    order_i = lax.broadcasted_iota(jnp.int32, (rows, rows), 0)
    order_j = lax.broadcasted_iota(jnp.int32, (rows, rows), 1)
    lower = jnp.where(order_i >= order_j, 1.0, 0.0)
    running = jnp.dot(lower, decay, precision=HIGHEST, preferred_element_type=F32)
    final = running[rows - 1 : rows]
    row_of = (running - jnp.log2(step)).T
    tail = jnp.where(
        (doc_i == last)[:, :heads], jnp.exp2(final - running) * step, 0.0
    )
    entry = jnp.where((doc_i == before)[:, :heads], jnp.exp2(running), 0.0)
    through = jnp.where((last == before)[:, :heads], jnp.exp2(final), 0.0)
    stack = jnp.concatenate(
        [
            tail,
            entry,
            jnp.broadcast_to(through, (8, heads)),
            jnp.broadcast_to(skip_ref[...], (8, heads)),
        ],
        axis=0,
    )
    high = stack.astype(BF16)
    low = (stack - high.astype(F32)).astype(BF16)

    @pl.when(has_left)
    def _():
        halo_copy.wait_recv()

    @pl.when(here == 0)
    def _():
        halo_in[...] = jnp.zeros_like(halo_in)
        state_in[...] = jnp.zeros_like(state_in)

    for s in range(reach):
        @pl.when(here < s + 1)
        def _(s=s):
            kv[s] = jnp.zeros_like(kv[s])

    halo = halo_in[...].astype(F32)
    for b in range(blocks):
        xf[8 - margin : 8, b * bc_width : (b + 1) * bc_width] = halo[
            b * margin : (b + 1) * margin
        ]
    bcf[8 - margin : 8, :] = halo[blocks * margin : (blocks + 1) * margin]
    bcf[8:, :] = bc_ref[...].astype(F32)

    def conv(source, weight_ref, bias_ref, at, size):
        total = source[8 : 8 + rows, at : at + size] * weight_ref[margin : margin + 1, at : at + size]
        total = total + bias_ref[:, at : at + size]
        for lag in range(margin):
            moved = source[8 - margin + lag : 8 - margin + lag + rows, at : at + size]
            total = total + moved * weight_ref[lag : lag + 1, at : at + size] * wide(
                same[lag], size
            )
        return silu(total).astype(BF16)

    b_turned, c_groups, crossed = [], [], []
    for g in range(groups):
        b_here = conv(bcf, cbw_ref, cbb_ref, 2 * g * STATE, STATE)
        c_here = conv(bcf, cbw_ref, cbb_ref, (2 * g + 1) * STATE, STATE)
        b_turned.append(b_here.astype(F32).T.astype(BF16))
        c_groups.append(c_here)
        crossed.append(lax.dot_general(c_here, b_here, NT, preferred_element_type=F32))

    def state_copy(c):
        return remote(state_out.at[c], state_in.at[c], st_send.at[c], st_recv.at[c])

    lane_head = lax.broadcasted_iota(jnp.int32, (heads, CHUNK), 1) // HDIM
    head_row = lax.broadcasted_iota(jnp.int32, (heads, CHUNK), 0)
    per_chunk = CHUNK // HDIM
    low_half = lax.broadcasted_iota(jnp.int32, (rows, 128), 1) < HDIM

    fetches[11].wait()
    carried = []
    for c in range(chunks):
        at = c * CHUNK
        g = at // group_width
        xf[8:, at : at + CHUNK] = x_ref[:, at : at + CHUNK].astype(F32)
        x_here = conv(xf, cxw_ref, cxb_ref, at, CHUNK)
        xc[:, at : at + CHUNK] = x_here
        spread = jnp.where(head_row == lane_head + c * per_chunk, 1.0, 0.0).astype(BF16)
        expanded = dot(high, spread) + dot(low, spread)
        x32 = x_here.astype(F32)
        local = dot(b_turned[g], (x32 * expanded[:rows]).astype(BF16))
        gate_entry[:, at : at + CHUNK] = expanded[rows : 2 * rows]
        gated[:, at : at + CHUNK] = x32 * expanded[2 * rows + 8 : 2 * rows + 9]
        carried.append(expanded[2 * rows : 2 * rows + 1])
        state_out[c] = local.astype(BF16)

        @pl.when(here == 0)
        def _(c=c):
            state_copy(c).start()

    for s in range(1, reach):
        @pl.when(here >= s)
        def _(s=s):
            for i in range(2):
                remote(
                    kv.at[s - 1, i], kv.at[s - 1, i], kv_send.at[s - 1, i], kv_recv.at[s - 1, i]
                ).wait_recv()

        @pl.when((here >= s) & has_right)
        def _(s=s):
            for i in range(2):
                remote(
                    kv.at[s - 1, i], kv.at[s, i], kv_send.at[s, i], kv_recv.at[s, i]
                ).start()

    for fetch in fetches[12:]:
        fetch.wait()

    kv_local = k_ref.shape[1] // ADIM
    share = q_ref.shape[1] // (ADIM * kv_local)
    scale = ADIM**-0.5 * LOG2E
    key_count = (reach + 1) * rows
    key_pos = (
        first - reach * rows + lax.broadcasted_iota(jnp.int32, (rows, key_count), 1)
    )
    key_docs = doc_of(key_pos)
    permitted = (key_docs == wide(doc_i, key_count)) & (key_pos <= wide(pos_i, key_count))

    def attend(head):
        g = head // share
        cols = slice(g * ADIM, (g + 1) * ADIM)
        keys = jnp.concatenate(
            [kv[s, 0, :, cols] for s in reversed(range(reach))] + [k_ref[:, cols]], axis=0
        )
        values = jnp.concatenate(
            [kv[s, 1, :, cols] for s in reversed(range(reach))] + [v_ref[:, cols]], axis=0
        )
        query = q_ref[:, head * ADIM : (head + 1) * ADIM]
        scores = lax.dot_general(query, keys, NT, preferred_element_type=F32)
        scores = jnp.where(permitted, scores, NEGATIVE)
        peak = jnp.max(scores, axis=1, keepdims=True)
        expo = jnp.exp2((scores - peak) * scale)
        total = jnp.sum(expo, axis=1, keepdims=True)
        summed = dot(expo.astype(BF16), values)
        attn_ref[:, head * ADIM : (head + 1) * ADIM] = (summed / total).astype(BF16)

    q_heads = kv_local * share
    early = chunks // 4
    for c in range(chunks):
        at = c * CHUNK
        g = at // group_width
        gate = silu(z_ref[:, at : at + CHUNK].astype(F32))
        for pair in range(CHUNK // 128):
            col = at + pair * 128
            head = col // HDIM
            parts = []
            for h in (head, head + 1):
                exponent = running[:, h : h + 1] - row_of[h : h + 1, :]
                parts.append(
                    (jnp.exp2(jnp.where(linked, exponent, NEGATIVE)) * crossed[g]).astype(BF16)
                )
            x_pair = xc[:, col : col + 128]
            zero = jnp.zeros_like(x_pair)
            stacked = jnp.concatenate(
                [jnp.where(low_half, x_pair, zero), jnp.where(low_half, zero, x_pair)], axis=0
            )
            inside = dot(jnp.concatenate(parts, axis=1), stacked)
            gated[:, col : col + 128] = (gated[:, col : col + 128] + inside) * gate[
                :, pair * 128 : (pair + 1) * 128
            ]
        gate_entry[:, at : at + CHUNK] = gate_entry[:, at : at + CHUNK] * gate

        @pl.when(has_left)
        def _(c=c):
            state_copy(c).wait_recv()

        @pl.when(has_left & has_right)
        def _(c=c):
            state_out[c] = (
                state_out[c].astype(F32) + state_in[c].astype(F32) * carried[c]
            ).astype(BF16)
            state_copy(c).start()

        if c == early:
            @pl.when(here >= reach)
            def _():
                for i in range(2):
                    remote(
                        kv.at[reach - 1, i],
                        kv.at[reach - 1, i],
                        kv_send.at[reach - 1, i],
                        kv_recv.at[reach - 1, i],
                    ).wait_recv()

        if early <= c < chunks - 1:
            span = chunks - early - 1
            for head in range((c - early) * q_heads // span, (c - early + 1) * q_heads // span):
                attend(head)

        gated[:, at : at + CHUNK] = (
            gated[:, at : at + CHUNK]
            + dot(c_groups[g], state_in[c]) * gate_entry[:, at : at + CHUNK]
        )
        if (at + CHUNK) % group_width == 0:
            left = at + CHUNK - group_width
            value = gated[:, left : left + group_width]
            mean = jnp.sum(value * value, axis=1, keepdims=True) * (1.0 / group_width)
            mamba_ref[:, left : left + group_width] = (
                value * lax.rsqrt(mean + EPSILON) * gain_ref[:, left : left + group_width]
            ).astype(BF16)

    @pl.when(has_right)
    def _():
        halo_copy.wait_send()
        own_k.wait_send()
        own_v.wait_send()
        for c in range(chunks):
            state_copy(c).wait_send()

    for s in range(1, reach):
        @pl.when((here >= s) & has_right)
        def _(s=s):
            for i in range(2):
                remote(
                    kv.at[s - 1, i], kv.at[s, i], kv_send.at[s, i], kv_recv.at[s, i]
                ).wait_send()


SUB = 128
ORDER = (
    ("l", 0, 6),
    ("k", 0, 1),
    ("t", 0, 1),
    ("l", 6, 8),
    ("p", 0, 1),
    ("w", 0, 1),
    ("i", 0, 4),
    ("p", 1, 2),
    ("i", 4, 8),
    ("p", 2, 3),
    ("r", 0, 2),
    ("a", 0, 3),
    ("p", 3, 4),
    ("a", 3, 6),
    ("p", 4, 5),
    ("a", 6, 8),
    ("p", 5, 8),
    ("f", 0, 2),
    ("r", 2, 3),
    ("f", 2, 3),
    ("r", 3, 4),
    ("f", 3, 4),
    ("r", 4, 5),
    ("f", 4, 5),
    ("r", 5, 6),
    ("f", 5, 6),
    ("r", 6, 7),
    ("f", 6, 7),
    ("r", 7, 8),
    ("f", 7, 8),
)


def packed_kernel(
    n,
    x_hbm, bc_hbm, z_hbm, dt_hbm, cxw_hbm, cxb_hbm, cbw_hbm, cbb_hbm,
    dtb_hbm, alog_hbm, skip_hbm, gain_hbm, q_hbm, k_hbm, v_hbm, lens_hbm,
    mamba_ref,
    attn_ref,
    halo_out,
    halo_in,
    kv,
    state_in,
    state_out,
    c_mine,
    c_next,
    xf,
    bcf,
    xc,
    gated,
    gate_entry,
    small_send,
    small_recv,
    kv_send,
    kv_recv,
    st_send,
    st_recv,
    c_sem,
    fetch_sem,
    x_tail,
    x_ref, bc_ref, z_ref, dt_ref, cxw_ref, cxb_ref, cbw_ref, cbb_ref,
    dtb_ref, alog_ref, skip_ref, gain_ref, q_ref, k_ref, v_ref, lens_ref,
):
    here = lax.axis_index("seq")
    rows, width = x_ref.shape
    fetches = [
        pltpu.make_async_copy(source, target, fetch_sem.at[i])
        for i, (source, target) in enumerate(
            (
                (x_hbm.at[pl.ds(rows - 16, 16), :], x_tail),
                (bc_hbm, bc_ref),
                (lens_hbm, lens_ref),
                (dt_hbm, dt_ref),
                (dtb_hbm, dtb_ref),
                (alog_hbm, alog_ref),
                (skip_hbm, skip_ref),
                (cbw_hbm, cbw_ref),
                (cbb_hbm, cbb_ref),
                (cxw_hbm, cxw_ref),
                (cxb_hbm, cxb_ref),
                (x_hbm, x_ref),
                (z_hbm, z_ref),
                (k_hbm, k_ref),
                (v_hbm, v_ref),
                (q_hbm, q_ref),
                (gain_hbm, gain_ref),
            )
        )
    ]
    for fetch in fetches:
        fetch.start()
    bc_width = bc_ref.shape[1]
    heads = dt_ref.shape[0]
    groups = bc_width // (2 * STATE)
    chunks = width // CHUNK
    per = CHUNK // SUB
    group_width = width // groups
    taps = cxw_ref.shape[0]
    margin = taps - 1
    has_left = here > 0
    has_right = here < n - 1
    middle = has_left & has_right

    def remote(src, dst, send, recv, to=1):
        return pltpu.make_async_remote_copy(
            src_ref=src,
            dst_ref=dst,
            send_sem=send,
            recv_sem=recv,
            device_id={"seq": here + to},
            device_id_type=pl.DeviceIdType.MESH,
        )

    barrier = pltpu.get_barrier_semaphore()

    @pl.when(has_left)
    def _():
        pl.semaphore_signal(
            barrier, inc=1, device_id={"seq": here - 1}, device_id_type=pl.DeviceIdType.MESH
        )

    @pl.when(has_right)
    def _():
        pl.semaphore_signal(
            barrier, inc=1, device_id={"seq": here + 1}, device_id_type=pl.DeviceIdType.MESH
        )

    fetches[0].wait()
    fetches[1].wait()
    blocks = width // bc_width
    tail_x = x_tail[...].astype(F32)[16 - margin :]
    tail_bc = bc_ref[rows - 16 :, :].astype(F32)[16 - margin :]
    pieces = [tail_x[:, b * bc_width : (b + 1) * bc_width] for b in range(blocks)] + [tail_bc]
    pieces.append(jnp.zeros((16 - margin * (blocks + 1), bc_width), F32))
    halo_out[...] = jnp.concatenate(pieces, axis=0).astype(BF16)

    @pl.when(middle)
    def _():
        pl.semaphore_wait(barrier, 2)

    @pl.when(jnp.logical_not(middle))
    def _():
        pl.semaphore_wait(barrier, 1)

    halo_copy = remote(halo_out, halo_in, small_send, small_recv)
    own_k = remote(k_hbm, kv.at[0], kv_send.at[0], kv_recv.at[0])
    own_v = remote(v_hbm, kv.at[1], kv_send.at[1], kv_recv.at[1])
    c_back = remote(c_mine, c_next, c_sem.at[0], c_sem.at[1], -1)

    @pl.when(has_right)
    def _():
        halo_copy.start()
        own_k.start()
        own_v.start()

    for fetch in fetches[2:11]:
        fetch.wait()
    first = here * rows
    starts = []
    running_start = jnp.int32(0)
    for d in range(lens_ref.shape[0]):
        starts.append(running_start)
        running_start = running_start + lens_ref[d]

    def doc_of(positions):
        total = jnp.full(positions.shape, -1, jnp.int32)
        for start in starts:
            total = total + jnp.where(start <= positions, 1, 0)
        return total

    def doc_at(position):
        return doc_of(jnp.full((1, 128), position, jnp.int32))

    square = (rows, 128)
    pos_i = first + lax.broadcasted_iota(jnp.int32, square, 0)
    pos_j = first + lax.broadcasted_iota(jnp.int32, (rows, rows), 1)
    doc_i = doc_of(pos_i)
    doc_j = doc_of(pos_j)
    linked = (doc_i == doc_j) & (pos_i >= pos_j)
    before = doc_at(first - 1)
    last = doc_at(first + rows - 1)
    same = [
        jnp.where(doc_of(pos_i - (margin - lag)) == doc_i, 1.0, 0.0) for lag in range(margin)
    ]
    ahead = doc_of(pos_i + rows) == before
    spare = (doc_at(first + rows) == before) & jnp.logical_not(ahead)
    rows_came = doc_at(first - rows - 1) == doc_at(first)

    raw = dt_ref[...].T + dtb_ref[...]
    step = jnp.maximum(raw, 0.0) + jnp.log1p(jnp.exp(-jnp.abs(raw)))
    decay = step * (jnp.exp(alog_ref[...]) * (-LOG2E))
    order_i = lax.broadcasted_iota(jnp.int32, (rows, rows), 0)
    order_j = lax.broadcasted_iota(jnp.int32, (rows, rows), 1)
    unit = jnp.where(order_i == order_j, 1.0, 0.0)
    lower = jnp.where(order_i >= order_j, 1.0, 0.0)
    running = jnp.dot(lower, decay, precision=HIGHEST, preferred_element_type=F32)
    final = running[rows - 1 : rows]
    row_of = (running - jnp.log2(step)).T
    tail = jnp.where(
        (doc_i == last)[:, :heads], jnp.exp2(final - running) * step, 0.0
    )
    entry = jnp.where((doc_i == before)[:, :heads], jnp.exp2(running), 0.0)
    through = jnp.where((last == before)[:, :heads], jnp.exp2(final), 0.0)
    stack = jnp.concatenate(
        [
            tail,
            entry,
            jnp.broadcast_to(through, (8, heads)),
            jnp.broadcast_to(skip_ref[...], (8, heads)),
        ],
        axis=0,
    )
    high = stack.astype(BF16)
    low = (stack - high.astype(F32)).astype(BF16)

    @pl.when(has_left)
    def _():
        halo_copy.wait_recv()

    @pl.when(here == 0)
    def _():
        halo_in[...] = jnp.zeros_like(halo_in)
        state_in[...] = jnp.zeros_like(state_in)
        kv[...] = jnp.zeros_like(kv)

    halo = halo_in[...].astype(F32)
    for b in range(blocks):
        xf[8 - margin : 8, b * bc_width : (b + 1) * bc_width] = halo[
            b * margin : (b + 1) * margin
        ]
    bcf[8 - margin : 8, :] = halo[blocks * margin : (blocks + 1) * margin]
    bcf[8:, :] = bc_ref[...].astype(F32)

    def conv(source, weight_ref, bias_ref, at, size):
        total = source[8 : 8 + rows, at : at + size] * weight_ref[margin : margin + 1, at : at + size]
        total = total + bias_ref[:, at : at + size]
        for lag in range(margin):
            moved = source[8 - margin + lag : 8 - margin + lag + rows, at : at + size]
            total = total + moved * weight_ref[lag : lag + 1, at : at + size] * wide(
                same[lag], size
            )
        return silu(total).astype(BF16)

    b_turned, c_groups, crossed = [], [], []
    for g in range(groups):
        b_here = conv(bcf, cbw_ref, cbb_ref, 2 * g * STATE, STATE)
        c_here = conv(bcf, cbw_ref, cbb_ref, (2 * g + 1) * STATE, STATE)
        b_turned.append(b_here.astype(F32).T.astype(BF16))
        c_mine[g] = c_here
        c_groups.append(jnp.where(rows_came, unit, c_here.astype(F32)).astype(BF16))
        crossed.append(lax.dot_general(c_here, b_here, NT, preferred_element_type=F32))

    @pl.when(here >= 2)
    def _():
        c_back.start()

    def state_copy(i):
        return remote(state_out.at[i], state_in.at[i], st_send.at[i], st_recv.at[i])

    kv_local = k_ref.shape[1] // ADIM
    lane_head = lax.broadcasted_iota(jnp.int32, (heads, CHUNK), 1) // HDIM
    head_row = lax.broadcasted_iota(jnp.int32, (heads, CHUNK), 0)
    per_chunk = CHUNK // HDIM
    low_half = lax.broadcasted_iota(jnp.int32, (rows, 128), 1) < HDIM
    carried = []

    def make_local(c):
        at = c * CHUNK
        g = at // group_width
        xf[8:, at : at + CHUNK] = x_ref[:, at : at + CHUNK].astype(F32)
        x_here = conv(xf, cxw_ref, cxb_ref, at, CHUNK)
        xc[:, at : at + CHUNK] = x_here
        spread = jnp.where(head_row == lane_head + c * per_chunk, 1.0, 0.0).astype(BF16)
        expanded = dot(high, spread) + dot(low, spread)
        x32 = x_here.astype(F32)
        local = dot(b_turned[g], (x32 * expanded[:rows]).astype(BF16)).astype(BF16)
        gate_entry[:, at : at + CHUNK] = expanded[rows : 2 * rows]
        gated[:, at : at + CHUNK] = x32 * expanded[2 * rows + 8 : 2 * rows + 9]
        carried.append(expanded[2 * rows : 2 * rows + 1])
        for i in range(per):
            state_out[c * per + i] = local[:, i * SUB : (i + 1) * SUB]

        @pl.when(here == 0)
        def _():
            for i in range(per):
                state_copy(c * per + i).start()

    def pass_on(c):
        g = c * CHUNK // group_width

        @pl.when(middle)
        def _():
            for i in range(per):
                at = c * per + i
                state_copy(at).wait_recv()
                state = state_out[at].astype(F32) + state_in[at].astype(F32) * carried[c][
                    :, i * SUB : (i + 1) * SUB
                ]
                sent = dot(c_next[g], state.astype(BF16))
                if at < 2 * kv_local:
                    col = at % kv_local * ADIM
                    sent = jnp.where(
                        spare, kv[at // kv_local, :, col : col + ADIM].astype(F32), sent
                    )
                state_out[at] = sent.astype(BF16)
                state_copy(at).start()

    def arrive(c):
        @pl.when(here == n - 1)
        def _():
            for i in range(per):
                state_copy(c * per + i).wait_recv()

    share = q_ref.shape[1] // (ADIM * kv_local)
    q_heads = kv_local * share
    scale = ADIM**-0.5 * LOG2E

    def permitted_keys():
        count = 3 * rows
        key_pos = first - 2 * rows + lax.broadcasted_iota(jnp.int32, (rows, count), 1)
        return (doc_of(key_pos) == wide(doc_i, count)) & (key_pos <= wide(pos_i, count))

    def attend(head, permitted):
        g = head // share
        cols = slice(g * ADIM, (g + 1) * ADIM)
        keys = jnp.concatenate([state_in[g], kv[0, :, cols], k_ref[:, cols]], axis=0)
        values = jnp.concatenate([state_in[kv_local + g], kv[1, :, cols], v_ref[:, cols]], axis=0)
        query = q_ref[:, head * ADIM : (head + 1) * ADIM]
        scores = lax.dot_general(query, keys, NT, preferred_element_type=F32)
        scores = jnp.where(permitted, scores, NEGATIVE)
        peak = jnp.max(scores, axis=1, keepdims=True)
        expo = jnp.exp2((scores - peak) * scale)
        total = jnp.sum(expo, axis=1, keepdims=True)
        summed = dot(expo.astype(BF16), values)
        attn_ref[:, head * ADIM : (head + 1) * ADIM] = (summed / total).astype(BF16)

    def inside(c):
        at = c * CHUNK
        g = at // group_width
        gate = silu(z_ref[:, at : at + CHUNK].astype(F32))
        for pair in range(CHUNK // 128):
            col = at + pair * 128
            head = col // HDIM
            parts = []
            for h in (head, head + 1):
                exponent = running[:, h : h + 1] - row_of[h : h + 1, :]
                parts.append(
                    (jnp.exp2(jnp.where(linked, exponent, NEGATIVE)) * crossed[g]).astype(BF16)
                )
            x_pair = xc[:, col : col + 128]
            zero = jnp.zeros_like(x_pair)
            stacked = jnp.concatenate(
                [jnp.where(low_half, x_pair, zero), jnp.where(low_half, zero, x_pair)], axis=0
            )
            within = dot(jnp.concatenate(parts, axis=1), stacked)
            gated[:, col : col + 128] = (gated[:, col : col + 128] + within) * gate[
                :, pair * 128 : (pair + 1) * 128
            ]
        gate_entry[:, at : at + CHUNK] = gate_entry[:, at : at + CHUNK] * gate

    def finish(c):
        at = c * CHUNK
        g = at // group_width
        came = jnp.concatenate([state_in[c * per + i] for i in range(per)], axis=1)
        gated[:, at : at + CHUNK] = (
            gated[:, at : at + CHUNK]
            + dot(c_groups[g], came) * gate_entry[:, at : at + CHUNK]
        )
        if (at + CHUNK) % group_width == 0:
            left = at + CHUNK - group_width
            value = gated[:, left : left + group_width]
            mean = jnp.sum(value * value, axis=1, keepdims=True) * (1.0 / group_width)
            mamba_ref[:, left : left + group_width] = (
                value * lax.rsqrt(mean + EPSILON) * gain_ref[:, left : left + group_width]
            ).astype(BF16)

    fetches[11].wait()

    def take_keys():
        @pl.when(has_left)
        def _():
            own_k.wait_recv()
            own_v.wait_recv()

    def take_turned():
        @pl.when(middle)
        def _():
            c_back.wait_recv()
            for g in range(groups):
                c_next[g] = jnp.where(ahead, c_next[g].astype(F32), unit).astype(BF16)

    def take_rest():
        for fetch in fetches[12:]:
            fetch.wait()

    held = []

    def attend_next(head):
        if not held:
            held.append(permitted_keys())
        attend(head, held[0])

    steps = {
        "l": make_local, "p": pass_on, "r": arrive, "i": inside, "a": attend_next, "f": finish,
        "k": lambda _: take_keys(), "t": lambda _: take_turned(), "w": lambda _: take_rest(),
    }
    for name, low_end, high_end in ORDER:
        for at in range(low_end, high_end):
            steps[name](at)

    @pl.when(has_right)
    def _():
        halo_copy.wait_send()
        own_k.wait_send()
        own_v.wait_send()
        for i in range(chunks * per):
            state_copy(i).wait_send()

    @pl.when(here >= 2)
    def _():
        c_back.wait_send()


def write_out(mamba_ref, attn_ref, mamba_hbm, attn_hbm, sems):
    copies = [
        pltpu.make_async_copy(mamba_ref, mamba_hbm, sems.at[0]),
        pltpu.make_async_copy(attn_ref, attn_hbm, sems.at[1]),
    ]
    for copy in copies:
        copy.start()
    for copy in copies:
        copy.wait()


def shards(n, *args):
    (
        x_raw, bc_raw, z_gate, dt_raw, cxw, cxb, cbw, cbb, dtb, a_log, skip_d, gain, queries, keys,
        values, doc_lens,
    ) = args
    operands = (
        x_raw, bc_raw, z_gate, dt_raw.T, cxw, cxb[None], cbw, cbb[None], dtb[None], a_log[None],
        skip_d[None], gain[None], queries, keys, values, doc_lens,
    )
    rows, width = x_raw.shape
    bc_width = bc_raw.shape[1]
    chunks = width // CHUNK
    reach = max(1, n // 2)
    vmem = pl.BlockSpec(memory_space=pltpu.VMEM)
    dma = pltpu.SemaphoreType.DMA
    if reach == 2 and rows == STATE and keys.shape[1] == CHUNK and width == 8 * CHUNK and (
        queries.shape[1] == 8 * ADIM
    ):
        subs = width // SUB
        state = pltpu.VMEM((subs, STATE, SUB), BF16)
        turned = pltpu.VMEM((bc_width // (2 * STATE), rows, STATE), BF16)
        body = functools.partial(packed_kernel, n)
        buffers = [pltpu.VMEM((2,) + keys.shape, BF16), state, state, turned, turned]
        sems = [dma((2,)), dma((2,)), dma((subs,)), dma((subs,)), dma((2,))]
    else:
        state = pltpu.VMEM((chunks, STATE, CHUNK), BF16)
        body = functools.partial(relay_kernel, n, reach)
        buffers = [pltpu.VMEM((reach, 2) + keys.shape, BF16), state, state]
        sems = [dma((reach, 2)), dma((reach, 2)), dma((chunks,)), dma((chunks,))]
    results = pl.pallas_call(
        body,
        out_shape=(pltpu.VMEM((rows, width), BF16), pltpu.VMEM(queries.shape, BF16)),
        in_specs=[pl.BlockSpec(memory_space=pltpu.HBM)] * 16,
        out_specs=(vmem, vmem),
        scratch_shapes=[
            pltpu.VMEM((16, bc_width), BF16),
            pltpu.VMEM((16, bc_width), BF16),
        ]
        + buffers
        + [
            pltpu.VMEM((rows + 8, width), F32),
            pltpu.VMEM((rows + 8, bc_width), F32),
            pltpu.VMEM((rows, width), BF16),
            pltpu.VMEM((rows, width), F32),
            pltpu.VMEM((rows, width), F32),
            dma,
            dma,
        ]
        + sems
        + [dma((17,)), pltpu.VMEM((16, width), BF16)]
        + [pltpu.VMEM(a.shape, a.dtype) for a in operands[:-1]]
        + [pltpu.SMEM(doc_lens.shape, jnp.int32)],
        compiler_params=pltpu.CompilerParams(
            collective_id=0, has_side_effects=True, vmem_limit_bytes=60 * 1024 * 1024
        ),
    )(*operands)
    hbm = pl.BlockSpec(memory_space=pltpu.HBM)
    return pl.pallas_call(
        write_out,
        out_shape=(
            jax.ShapeDtypeStruct((rows, width), BF16),
            jax.ShapeDtypeStruct(queries.shape, BF16),
        ),
        in_specs=[vmem, vmem],
        out_specs=(hbm, hbm),
        scratch_shapes=[dma((2,))],
    )(*[pltpu.with_memory_space_constraint(r, pltpu.VMEM) for r in results])


def solution(mesh):
    both = P(("groups", "seq"), "dp")
    placed = (
        both, both, both, both, P(None, "dp"), P("dp"), P(None, "dp"), P("dp"), P("dp"), P("dp"),
        P("dp"), P("dp"), both, both, both, P("groups"),
    )
    return jax.shard_map(
        functools.partial(shards, mesh.shape["seq"]),
        mesh=mesh,
        in_specs=placed,
        out_specs=(both, both),
        check_vma=False,
    )
```

```python
import functools
import jax
import jax.numpy as jnp
from jax import lax
from jax.experimental import pallas as pl
from jax.experimental.pallas import tpu as pltpu
from jax.sharding import PartitionSpec as P

HDIM = 64
STATE = 128
QHEADS = 32
KVHEADS = 8
ADIM = 128
EPSILON = 1e-05
NEGATIVE = -1e30
LOG2E = 1.4426950408889634
HIGHEST = lax.Precision.HIGHEST
F32 = jnp.float32
BF16 = jnp.bfloat16
CHUNK = 256
NT = (((1,), (1,)), ((), ()))


def silu(value):
    half = 0.5 * value
    return half + half * jnp.tanh(half)


def dot(a, b):
    return jnp.dot(a, b, preferred_element_type=F32)


def wide(tile, width):
    return jnp.concatenate([tile] * (width // tile.shape[1]), axis=1)


def relay_kernel(
    n,
    reach,
    x_hbm, bc_hbm, z_hbm, dt_hbm, cxw_hbm, cxb_hbm, cbw_hbm, cbb_hbm,
    dtb_hbm, alog_hbm, skip_hbm, gain_hbm, q_hbm, k_hbm, v_hbm, lens_hbm,
    mamba_ref,
    attn_ref,
    halo_out,
    halo_in,
    kv,
    state_in,
    state_out,
    xf,
    bcf,
    xc,
    gated,
    gate_entry,
    small_send,
    small_recv,
    kv_send,
    kv_recv,
    st_send,
    st_recv,
    fetch_sem,
    x_tail,
    x_ref, bc_ref, z_ref, dt_ref, cxw_ref, cxb_ref, cbw_ref, cbb_ref,
    dtb_ref, alog_ref, skip_ref, gain_ref, q_ref, k_ref, v_ref, lens_ref,
):
    here = lax.axis_index("seq")
    rows, width = x_ref.shape
    fetches = [
        pltpu.make_async_copy(source, target, fetch_sem.at[i])
        for i, (source, target) in enumerate(
            (
                (x_hbm.at[pl.ds(rows - 16, 16), :], x_tail),
                (bc_hbm, bc_ref),
                (lens_hbm, lens_ref),
                (dt_hbm, dt_ref),
                (dtb_hbm, dtb_ref),
                (alog_hbm, alog_ref),
                (skip_hbm, skip_ref),
                (cbw_hbm, cbw_ref),
                (cbb_hbm, cbb_ref),
                (cxw_hbm, cxw_ref),
                (cxb_hbm, cxb_ref),
                (x_hbm, x_ref),
                (z_hbm, z_ref),
                (k_hbm, k_ref),
                (v_hbm, v_ref),
                (q_hbm, q_ref),
                (gain_hbm, gain_ref),
            )
        )
    ]
    for fetch in fetches:
        fetch.start()
    bc_width = bc_ref.shape[1]
    heads = dt_ref.shape[0]
    groups = bc_width // (2 * STATE)
    chunks = width // CHUNK
    group_width = width // groups
    taps = cxw_ref.shape[0]
    margin = taps - 1
    has_left = here > 0
    has_right = here < n - 1
    right = {"seq": here + 1}

    def remote(src, dst, send, recv):
        return pltpu.make_async_remote_copy(
            src_ref=src,
            dst_ref=dst,
            send_sem=send,
            recv_sem=recv,
            device_id=right,
            device_id_type=pl.DeviceIdType.MESH,
        )

    barrier = pltpu.get_barrier_semaphore()

    @pl.when(has_left)
    def _():
        pl.semaphore_signal(
            barrier, inc=1, device_id={"seq": here - 1}, device_id_type=pl.DeviceIdType.MESH
        )

    @pl.when(has_right)
    def _():
        pl.semaphore_signal(
            barrier, inc=1, device_id={"seq": here + 1}, device_id_type=pl.DeviceIdType.MESH
        )

    fetches[0].wait()
    fetches[1].wait()
    blocks = width // bc_width
    tail_x = x_tail[...].astype(F32)[16 - margin :]
    tail_bc = bc_ref[rows - 16 :, :].astype(F32)[16 - margin :]
    pieces = [tail_x[:, b * bc_width : (b + 1) * bc_width] for b in range(blocks)] + [tail_bc]
    pieces.append(jnp.zeros((16 - margin * (blocks + 1), bc_width), F32))
    halo_out[...] = jnp.concatenate(pieces, axis=0).astype(BF16)

    @pl.when(has_left & has_right)
    def _():
        pl.semaphore_wait(barrier, 2)

    @pl.when(jnp.logical_not(has_left & has_right))
    def _():
        pl.semaphore_wait(barrier, 1)

    halo_copy = remote(halo_out, halo_in, small_send, small_recv)
    own_k = remote(k_hbm, kv.at[0, 0], kv_send.at[0, 0], kv_recv.at[0, 0])
    own_v = remote(v_hbm, kv.at[0, 1], kv_send.at[0, 1], kv_recv.at[0, 1])

    @pl.when(has_right)
    def _():
        halo_copy.start()
        own_k.start()
        own_v.start()

    for fetch in fetches[2:11]:
        fetch.wait()
    first = here * rows
    starts = []
    running_start = jnp.int32(0)
    for d in range(lens_ref.shape[0]):
        starts.append(running_start)
        running_start = running_start + lens_ref[d]

    def doc_of(positions):
        total = jnp.full(positions.shape, -1, jnp.int32)
        for start in starts:
            total = total + jnp.where(start <= positions, 1, 0)
        return total

    square = (rows, 128)
    pos_i = first + lax.broadcasted_iota(jnp.int32, square, 0)
    pos_j = first + lax.broadcasted_iota(jnp.int32, (rows, rows), 1)
    doc_i = doc_of(pos_i)
    doc_j = doc_of(pos_j)
    linked = (doc_i == doc_j) & (pos_i >= pos_j)
    before = doc_of(jnp.full((1, 128), first - 1, jnp.int32))
    last = doc_of(jnp.full((1, 128), first + rows - 1, jnp.int32))
    same = [
        jnp.where(doc_of(pos_i - (margin - lag)) == doc_i, 1.0, 0.0) for lag in range(margin)
    ]

    raw = dt_ref[...].T + dtb_ref[...]
    step = jnp.maximum(raw, 0.0) + jnp.log1p(jnp.exp(-jnp.abs(raw)))
    decay = step * (jnp.exp(alog_ref[...]) * (-LOG2E))
    order_i = lax.broadcasted_iota(jnp.int32, (rows, rows), 0)
    order_j = lax.broadcasted_iota(jnp.int32, (rows, rows), 1)
    lower = jnp.where(order_i >= order_j, 1.0, 0.0)
    running = jnp.dot(lower, decay, precision=HIGHEST, preferred_element_type=F32)
    final = running[rows - 1 : rows]
    row_of = (running - jnp.log2(step)).T
    tail = jnp.where(
        (doc_i == last)[:, :heads], jnp.exp2(final - running) * step, 0.0
    )
    entry = jnp.where((doc_i == before)[:, :heads], jnp.exp2(running), 0.0)
    through = jnp.where((last == before)[:, :heads], jnp.exp2(final), 0.0)
    stack = jnp.concatenate(
        [
            tail,
            entry,
            jnp.broadcast_to(through, (8, heads)),
            jnp.broadcast_to(skip_ref[...], (8, heads)),
        ],
        axis=0,
    )
    high = stack.astype(BF16)
    low = (stack - high.astype(F32)).astype(BF16)

    @pl.when(has_left)
    def _():
        halo_copy.wait_recv()

    @pl.when(here == 0)
    def _():
        halo_in[...] = jnp.zeros_like(halo_in)
        state_in[...] = jnp.zeros_like(state_in)

    for s in range(reach):
        @pl.when(here < s + 1)
        def _(s=s):
            kv[s] = jnp.zeros_like(kv[s])

    halo = halo_in[...].astype(F32)
    for b in range(blocks):
        xf[8 - margin : 8, b * bc_width : (b + 1) * bc_width] = halo[
            b * margin : (b + 1) * margin
        ]
    bcf[8 - margin : 8, :] = halo[blocks * margin : (blocks + 1) * margin]
    bcf[8:, :] = bc_ref[...].astype(F32)

    def conv(source, weight_ref, bias_ref, at, size):
        total = source[8 : 8 + rows, at : at + size] * weight_ref[margin : margin + 1, at : at + size]
        total = total + bias_ref[:, at : at + size]
        for lag in range(margin):
            moved = source[8 - margin + lag : 8 - margin + lag + rows, at : at + size]
            total = total + moved * weight_ref[lag : lag + 1, at : at + size] * wide(
                same[lag], size
            )
        return silu(total).astype(BF16)

    b_turned, c_groups, crossed = [], [], []
    for g in range(groups):
        b_here = conv(bcf, cbw_ref, cbb_ref, 2 * g * STATE, STATE)
        c_here = conv(bcf, cbw_ref, cbb_ref, (2 * g + 1) * STATE, STATE)
        b_turned.append(b_here.astype(F32).T.astype(BF16))
        c_groups.append(c_here)
        crossed.append(lax.dot_general(c_here, b_here, NT, preferred_element_type=F32))

    def state_copy(c):
        return remote(state_out.at[c], state_in.at[c], st_send.at[c], st_recv.at[c])

    lane_head = lax.broadcasted_iota(jnp.int32, (heads, CHUNK), 1) // HDIM
    head_row = lax.broadcasted_iota(jnp.int32, (heads, CHUNK), 0)
    per_chunk = CHUNK // HDIM
    low_half = lax.broadcasted_iota(jnp.int32, (rows, 128), 1) < HDIM

    fetches[11].wait()
    carried = []
    for c in range(chunks):
        at = c * CHUNK
        g = at // group_width
        xf[8:, at : at + CHUNK] = x_ref[:, at : at + CHUNK].astype(F32)
        x_here = conv(xf, cxw_ref, cxb_ref, at, CHUNK)
        xc[:, at : at + CHUNK] = x_here
        spread = jnp.where(head_row == lane_head + c * per_chunk, 1.0, 0.0).astype(BF16)
        expanded = dot(high, spread) + dot(low, spread)
        x32 = x_here.astype(F32)
        local = dot(b_turned[g], (x32 * expanded[:rows]).astype(BF16))
        gate_entry[:, at : at + CHUNK] = expanded[rows : 2 * rows]
        gated[:, at : at + CHUNK] = x32 * expanded[2 * rows + 8 : 2 * rows + 9]
        carried.append(expanded[2 * rows : 2 * rows + 1])
        state_out[c] = local.astype(BF16)

        @pl.when(here == 0)
        def _(c=c):
            state_copy(c).start()

    for s in range(1, reach):
        @pl.when(here >= s)
        def _(s=s):
            for i in range(2):
                remote(
                    kv.at[s - 1, i], kv.at[s - 1, i], kv_send.at[s - 1, i], kv_recv.at[s - 1, i]
                ).wait_recv()

        @pl.when((here >= s) & has_right)
        def _(s=s):
            for i in range(2):
                remote(
                    kv.at[s - 1, i], kv.at[s, i], kv_send.at[s, i], kv_recv.at[s, i]
                ).start()

    for fetch in fetches[12:]:
        fetch.wait()

    kv_local = k_ref.shape[1] // ADIM
    share = q_ref.shape[1] // (ADIM * kv_local)
    scale = ADIM**-0.5 * LOG2E
    key_count = (reach + 1) * rows
    key_pos = (
        first - reach * rows + lax.broadcasted_iota(jnp.int32, (rows, key_count), 1)
    )
    key_docs = doc_of(key_pos)
    permitted = (key_docs == wide(doc_i, key_count)) & (key_pos <= wide(pos_i, key_count))

    def attend(head):
        g = head // share
        cols = slice(g * ADIM, (g + 1) * ADIM)
        keys = jnp.concatenate(
            [kv[s, 0, :, cols] for s in reversed(range(reach))] + [k_ref[:, cols]], axis=0
        )
        values = jnp.concatenate(
            [kv[s, 1, :, cols] for s in reversed(range(reach))] + [v_ref[:, cols]], axis=0
        )
        query = q_ref[:, head * ADIM : (head + 1) * ADIM]
        scores = lax.dot_general(query, keys, NT, preferred_element_type=F32)
        scores = jnp.where(permitted, scores, NEGATIVE)
        peak = jnp.max(scores, axis=1, keepdims=True)
        expo = jnp.exp2((scores - peak) * scale)
        total = jnp.sum(expo, axis=1, keepdims=True)
        summed = dot(expo.astype(BF16), values)
        attn_ref[:, head * ADIM : (head + 1) * ADIM] = (summed / total).astype(BF16)

    q_heads = kv_local * share
    early = chunks // 4
    for c in range(chunks):
        at = c * CHUNK
        g = at // group_width
        gate = silu(z_ref[:, at : at + CHUNK].astype(F32))
        for pair in range(CHUNK // 128):
            col = at + pair * 128
            head = col // HDIM
            parts = []
            for h in (head, head + 1):
                exponent = running[:, h : h + 1] - row_of[h : h + 1, :]
                parts.append(
                    (jnp.exp2(jnp.where(linked, exponent, NEGATIVE)) * crossed[g]).astype(BF16)
                )
            x_pair = xc[:, col : col + 128]
            zero = jnp.zeros_like(x_pair)
            stacked = jnp.concatenate(
                [jnp.where(low_half, x_pair, zero), jnp.where(low_half, zero, x_pair)], axis=0
            )
            inside = dot(jnp.concatenate(parts, axis=1), stacked)
            gated[:, col : col + 128] = (gated[:, col : col + 128] + inside) * gate[
                :, pair * 128 : (pair + 1) * 128
            ]
        gate_entry[:, at : at + CHUNK] = gate_entry[:, at : at + CHUNK] * gate

        @pl.when(has_left)
        def _(c=c):
            state_copy(c).wait_recv()

        @pl.when(has_left & has_right)
        def _(c=c):
            state_out[c] = (
                state_out[c].astype(F32) + state_in[c].astype(F32) * carried[c]
            ).astype(BF16)
            state_copy(c).start()

        if c == early:
            @pl.when(here >= reach)
            def _():
                for i in range(2):
                    remote(
                        kv.at[reach - 1, i],
                        kv.at[reach - 1, i],
                        kv_send.at[reach - 1, i],
                        kv_recv.at[reach - 1, i],
                    ).wait_recv()

        if early <= c < chunks - 1:
            span = chunks - early - 1
            for head in range((c - early) * q_heads // span, (c - early + 1) * q_heads // span):
                attend(head)

        gated[:, at : at + CHUNK] = (
            gated[:, at : at + CHUNK]
            + dot(c_groups[g], state_in[c]) * gate_entry[:, at : at + CHUNK]
        )
        if (at + CHUNK) % group_width == 0:
            left = at + CHUNK - group_width
            value = gated[:, left : left + group_width]
            mean = jnp.sum(value * value, axis=1, keepdims=True) * (1.0 / group_width)
            mamba_ref[:, left : left + group_width] = (
                value * lax.rsqrt(mean + EPSILON) * gain_ref[:, left : left + group_width]
            ).astype(BF16)

    @pl.when(has_right)
    def _():
        halo_copy.wait_send()
        own_k.wait_send()
        own_v.wait_send()
        for c in range(chunks):
            state_copy(c).wait_send()

    for s in range(1, reach):
        @pl.when((here >= s) & has_right)
        def _(s=s):
            for i in range(2):
                remote(
                    kv.at[s - 1, i], kv.at[s, i], kv_send.at[s, i], kv_recv.at[s, i]
                ).wait_send()


SUB = 128
ORDER = (
    ("l", 7, 8),
    ("e", 0, 1),
    ("l", 0, 7),
    ("o", 0, 1),
    ("k", 0, 1),
    ("t", 0, 1),
    ("q", 0, 4),
    ("x", 0, 1),
    ("p", 0, 1),
    ("w", 0, 1),
    ("i", 0, 4),
    ("p", 1, 2),
    ("i", 4, 8),
    ("p", 2, 3),
    ("r", 0, 2),
    ("a", 0, 3),
    ("p", 3, 4),
    ("a", 3, 6),
    ("p", 4, 5),
    ("a", 6, 8),
    ("p", 5, 7),
    ("f", 0, 2),
    ("r", 2, 3),
    ("f", 2, 3),
    ("r", 3, 4),
    ("f", 3, 4),
    ("n", 0, 1),
    ("y", 0, 1),
    ("r", 4, 5),
    ("f", 4, 5),
    ("r", 5, 6),
    ("f", 5, 6),
    ("r", 7, 8),
    ("f", 7, 8),
    ("r", 6, 7),
    ("f", 6, 7),
    ("n", 1, 2),
)


def packed_kernel(
    n,
    x_hbm, bc_hbm, z_hbm, dt_hbm, cxw_hbm, cxb_hbm, cbw_hbm, cbb_hbm,
    dtb_hbm, alog_hbm, skip_hbm, gain_hbm, q_hbm, k_hbm, v_hbm, lens_hbm,
    mamba_ref,
    attn_ref,
    halo_out,
    halo_in,
    kv,
    state_in,
    state_out,
    c_mine,
    c_next,
    c_ahead,
    ready,
    extra,
    xf,
    bcf,
    xc,
    gated,
    gate_entry,
    small_send,
    small_recv,
    kv_send,
    kv_recv,
    st_send,
    st_recv,
    c_sem,
    extra_sem,
    fetch_sem,
    x_tail,
    x_ref, bc_ref, z_ref, dt_ref, cxw_ref, cxb_ref, cbw_ref, cbb_ref,
    dtb_ref, alog_ref, skip_ref, gain_ref, q_ref, k_ref, v_ref, lens_ref,
):
    here = lax.axis_index("seq")
    has_left = here > 0
    has_right = here < n - 1
    middle = has_left & has_right
    barrier = pltpu.get_barrier_semaphore()

    @pl.when(has_left)
    def _():
        pl.semaphore_signal(
            barrier, inc=1, device_id={"seq": here - 1}, device_id_type=pl.DeviceIdType.MESH
        )

    @pl.when(has_right)
    def _():
        pl.semaphore_signal(
            barrier, inc=1, device_id={"seq": here + 1}, device_id_type=pl.DeviceIdType.MESH
        )

    rows, width = x_ref.shape
    fetches = [
        pltpu.make_async_copy(source, target, fetch_sem.at[i])
        for i, (source, target) in enumerate(
            (
                (x_hbm.at[pl.ds(rows - 16, 16), :], x_tail),
                (bc_hbm, bc_ref),
                (lens_hbm, lens_ref),
                (dt_hbm, dt_ref),
                (dtb_hbm, dtb_ref),
                (alog_hbm, alog_ref),
                (skip_hbm, skip_ref),
                (cbw_hbm, cbw_ref),
                (cbb_hbm, cbb_ref),
                (cxw_hbm, cxw_ref),
                (cxb_hbm, cxb_ref),
                (x_hbm, x_ref),
                (z_hbm, z_ref),
                (k_hbm, k_ref),
                (v_hbm, v_ref),
                (q_hbm, q_ref),
                (gain_hbm, gain_ref),
            )
        )
    ]
    for fetch in fetches:
        fetch.start()
    bc_width = bc_ref.shape[1]
    heads = dt_ref.shape[0]
    groups = bc_width // (2 * STATE)
    chunks = width // CHUNK
    per = CHUNK // SUB
    group_width = width // groups
    taps = cxw_ref.shape[0]
    margin = taps - 1

    def remote(src, dst, send, recv, to=1):
        return pltpu.make_async_remote_copy(
            src_ref=src,
            dst_ref=dst,
            send_sem=send,
            recv_sem=recv,
            device_id={"seq": here + to},
            device_id_type=pl.DeviceIdType.MESH,
        )

    fetches[0].wait()
    fetches[1].wait()
    blocks = width // bc_width
    tail_x = x_tail[...].astype(F32)[16 - margin :]
    tail_bc = bc_ref[rows - 16 :, :].astype(F32)[16 - margin :]
    pieces = [tail_x[:, b * bc_width : (b + 1) * bc_width] for b in range(blocks)] + [tail_bc]
    pieces.append(jnp.zeros((16 - margin * (blocks + 1), bc_width), F32))
    halo_out[...] = jnp.concatenate(pieces, axis=0).astype(BF16)

    @pl.when(middle)
    def _():
        pl.semaphore_wait(barrier, 2)

    @pl.when(jnp.logical_not(middle))
    def _():
        pl.semaphore_wait(barrier, 1)

    halo_copy = remote(halo_out, halo_in, small_send, small_recv)
    own_k = remote(k_hbm, kv.at[0], kv_send.at[0], kv_recv.at[0])
    own_v = remote(v_hbm, kv.at[1], kv_send.at[1], kv_recv.at[1])
    c_back = remote(c_mine, c_next, c_sem.at[0], c_sem.at[1], -1)

    @pl.when(has_right)
    def _():
        halo_copy.start()
        own_k.start()
        own_v.start()

    for fetch in fetches[2:11]:
        fetch.wait()
    first = here * rows
    starts = []
    running_start = jnp.int32(0)
    for d in range(lens_ref.shape[0]):
        starts.append(running_start)
        running_start = running_start + lens_ref[d]

    def doc_of(positions):
        total = jnp.full(positions.shape, -1, jnp.int32)
        for start in starts:
            total = total + jnp.where(start <= positions, 1, 0)
        return total

    def doc_at(position):
        return doc_of(jnp.full((1, 128), position, jnp.int32))

    square = (rows, 128)
    pos_i = first + lax.broadcasted_iota(jnp.int32, square, 0)
    pos_j = first + lax.broadcasted_iota(jnp.int32, (rows, rows), 1)
    doc_i = doc_of(pos_i)
    doc_j = doc_of(pos_j)
    linked = (doc_i == doc_j) & (pos_i >= pos_j)
    before = doc_at(first - 1)
    last = doc_at(first + rows - 1)
    same = [
        jnp.where(doc_of(pos_i - (margin - lag)) == doc_i, 1.0, 0.0) for lag in range(margin)
    ]
    ahead = doc_of(pos_i + rows) == before
    spare = (doc_at(first + rows) == before) & jnp.logical_not(ahead)
    rows_came = doc_at(first - rows - 1) == doc_at(first)

    raw = dt_ref[...].T + dtb_ref[...]
    step = jnp.maximum(raw, 0.0) + jnp.log1p(jnp.exp(-jnp.abs(raw)))
    decay = step * (jnp.exp(alog_ref[...]) * (-LOG2E))
    order_i = lax.broadcasted_iota(jnp.int32, (rows, rows), 0)
    order_j = lax.broadcasted_iota(jnp.int32, (rows, rows), 1)
    unit = jnp.where(order_i == order_j, 1.0, 0.0)
    lower = jnp.where(order_i >= order_j, 1.0, 0.0)
    running = jnp.dot(lower, decay, precision=HIGHEST, preferred_element_type=F32)
    final = running[rows - 1 : rows]
    row_of = (running - jnp.log2(step)).T
    tail = jnp.where(
        (doc_i == last)[:, :heads], jnp.exp2(final - running) * step, 0.0
    )
    entry = jnp.where((doc_i == before)[:, :heads], jnp.exp2(running), 0.0)
    through = jnp.where((last == before)[:, :heads], jnp.exp2(final), 0.0)
    stack = jnp.concatenate(
        [
            tail,
            entry,
            jnp.broadcast_to(through, (8, heads)),
            jnp.broadcast_to(skip_ref[...], (8, heads)),
        ],
        axis=0,
    )
    high = stack.astype(BF16)
    low = (stack - high.astype(F32)).astype(BF16)

    @pl.when(has_left)
    def _():
        halo_copy.wait_recv()

    @pl.when(here == 0)
    def _():
        halo_in[...] = jnp.zeros_like(halo_in)
        state_in[...] = jnp.zeros_like(state_in)
        kv[...] = jnp.zeros_like(kv)

    @pl.when(here != 2)
    def _():
        extra[...] = jnp.zeros_like(extra)

    halo = halo_in[...].astype(F32)
    for b in range(blocks):
        xf[8 - margin : 8, b * bc_width : (b + 1) * bc_width] = halo[
            b * margin : (b + 1) * margin
        ]
    bcf[8 - margin : 8, :] = halo[blocks * margin : (blocks + 1) * margin]
    bcf[8:, :] = bc_ref[...].astype(F32)

    def conv(source, weight_ref, bias_ref, at, size):
        total = source[8 : 8 + rows, at : at + size] * weight_ref[margin : margin + 1, at : at + size]
        total = total + bias_ref[:, at : at + size]
        for lag in range(margin):
            moved = source[8 - margin + lag : 8 - margin + lag + rows, at : at + size]
            total = total + moved * weight_ref[lag : lag + 1, at : at + size] * wide(
                same[lag], size
            )
        return silu(total).astype(BF16)

    b_turned, c_groups, crossed, c_own = [], [], [], []
    for g in range(groups):
        b_here = conv(bcf, cbw_ref, cbb_ref, 2 * g * STATE, STATE)
        c_here = conv(bcf, cbw_ref, cbb_ref, (2 * g + 1) * STATE, STATE)
        b_turned.append(b_here.astype(F32).T.astype(BF16))
        c_mine[g] = c_here
        c_own.append(c_here)
        c_groups.append(jnp.where(rows_came, unit, c_here.astype(F32)).astype(BF16))
        crossed.append(lax.dot_general(c_here, b_here, NT, preferred_element_type=F32))

    @pl.when(here >= 2)
    def _():
        c_back.start()

    def state_copy(i):
        return remote(state_out.at[i], state_in.at[i], st_send.at[i], st_recv.at[i])

    kv_local = k_ref.shape[1] // ADIM
    lane_head = lax.broadcasted_iota(jnp.int32, (heads, CHUNK), 1) // HDIM
    head_row = lax.broadcasted_iota(jnp.int32, (heads, CHUNK), 0)
    per_chunk = CHUNK // HDIM
    low_half = lax.broadcasted_iota(jnp.int32, (rows, 128), 1) < HDIM
    carried = {}

    def make_local(c):
        at = c * CHUNK
        g = at // group_width
        xf[8:, at : at + CHUNK] = x_ref[:, at : at + CHUNK].astype(F32)
        x_here = conv(xf, cxw_ref, cxb_ref, at, CHUNK)
        xc[:, at : at + CHUNK] = x_here
        spread = jnp.where(head_row == lane_head + c * per_chunk, 1.0, 0.0).astype(BF16)
        expanded = dot(high, spread) + dot(low, spread)
        x32 = x_here.astype(F32)
        local = dot(b_turned[g], (x32 * expanded[:rows]).astype(BF16)).astype(BF16)
        gate_entry[:, at : at + CHUNK] = expanded[rows : 2 * rows]
        gated[:, at : at + CHUNK] = x32 * expanded[2 * rows + 8 : 2 * rows + 9]
        carried[c] = expanded[2 * rows : 2 * rows + 1]
        for i in range(per):
            state_out[c * per + i] = local[:, i * SUB : (i + 1) * SUB]

        if c < chunks - 1:
            first_send(c)

    def first_send(c):
        @pl.when(here == 0)
        def _():
            for i in range(per):
                state_copy(c * per + i).start()

    extra_copy = remote(
        state_out.at[pl.ds((chunks - 1) * per, per)], extra, extra_sem.at[0], extra_sem.at[1]
    )

    def early_send():
        @pl.when(here == 1)
        def _():
            extra_copy.start()

    def early_pass():
        c = chunks - 1
        g = c * CHUNK // group_width

        @pl.when(here == 2)
        def _():
            extra_copy.wait_recv()
            for i in range(per):
                at = c * per + i
                state_out[at] = (
                    ready[at] + dot(c_ahead[g], extra[i]) * carried[c][:, i * SUB : (i + 1) * SUB]
                ).astype(BF16)
                state_copy(at).start()

    def late_pass():
        c = chunks - 1
        g = c * CHUNK // group_width

        @pl.when(here == 1)
        def _():
            extra_copy.wait_send()
            for i in range(per):
                at = c * per + i
                state_copy(at).wait_recv()
                state_out[at] = (
                    dot(c_ahead[g], state_in[at]) * carried[c][:, i * SUB : (i + 1) * SUB]
                ).astype(BF16)
                state_copy(at).start()

    def make_ready(cs):
        @pl.when(middle)
        def _():
            for c in cs:
                g = c * CHUNK // group_width
                for i in range(per):
                    at = c * per + i
                    sent = dot(c_next[g], state_out[at])
                    if at < 2 * kv_local:
                        col = at % kv_local * ADIM
                        sent = jnp.where(
                            spare, kv[at // kv_local, :, col : col + ADIM].astype(F32), sent
                        )
                    ready[at] = sent

    def pass_on(c):
        g = c * CHUNK // group_width

        @pl.when(middle)
        def _():
            for i in range(per):
                at = c * per + i
                state_copy(at).wait_recv()
                state_out[at] = (
                    ready[at]
                    + dot(c_ahead[g], state_in[at]) * carried[c][:, i * SUB : (i + 1) * SUB]
                ).astype(BF16)
                state_copy(at).start()

    def arrive(c):
        @pl.when(here >= (2 if c == chunks - 1 else n - 1))
        def _():
            for i in range(per):
                state_copy(c * per + i).wait_recv()

    share = q_ref.shape[1] // (ADIM * kv_local)
    q_heads = kv_local * share
    scale = ADIM**-0.5 * LOG2E

    def permitted_keys():
        count = 3 * rows
        key_pos = first - 2 * rows + lax.broadcasted_iota(jnp.int32, (rows, count), 1)
        return (doc_of(key_pos) == wide(doc_i, count)) & (key_pos <= wide(pos_i, count))

    def attend(head, permitted):
        g = head // share
        cols = slice(g * ADIM, (g + 1) * ADIM)
        keys = jnp.concatenate([state_in[g], kv[0, :, cols], k_ref[:, cols]], axis=0)
        values = jnp.concatenate([state_in[kv_local + g], kv[1, :, cols], v_ref[:, cols]], axis=0)
        query = q_ref[:, head * ADIM : (head + 1) * ADIM]
        scores = lax.dot_general(query, keys, NT, preferred_element_type=F32)
        scores = jnp.where(permitted, scores, NEGATIVE)
        peak = jnp.max(scores, axis=1, keepdims=True)
        expo = jnp.exp2((scores - peak) * scale)
        total = jnp.sum(expo, axis=1, keepdims=True)
        summed = dot(expo.astype(BF16), values)
        attn_ref[:, head * ADIM : (head + 1) * ADIM] = (summed / total).astype(BF16)

    def inside(c):
        at = c * CHUNK
        g = at // group_width
        gate = silu(z_ref[:, at : at + CHUNK].astype(F32))
        for pair in range(CHUNK // 128):
            col = at + pair * 128
            head = col // HDIM
            parts = []
            for h in (head, head + 1):
                exponent = running[:, h : h + 1] - row_of[h : h + 1, :]
                parts.append(
                    (jnp.exp2(jnp.where(linked, exponent, NEGATIVE)) * crossed[g]).astype(BF16)
                )
            x_pair = xc[:, col : col + 128]
            zero = jnp.zeros_like(x_pair)
            stacked = jnp.concatenate(
                [jnp.where(low_half, x_pair, zero), jnp.where(low_half, zero, x_pair)], axis=0
            )
            within = dot(jnp.concatenate(parts, axis=1), stacked)
            gated[:, col : col + 128] = (gated[:, col : col + 128] + within) * gate[
                :, pair * 128 : (pair + 1) * 128
            ]
        gate_entry[:, at : at + CHUNK] = gate_entry[:, at : at + CHUNK] * gate

    squares = {}

    def finish(c):
        at = c * CHUNK
        g = at // group_width
        came = jnp.concatenate([state_in[c * per + i] for i in range(per)], axis=1)
        if c == chunks - 1:
            local = jnp.concatenate([extra[i] for i in range(per)], axis=1)
            theirs = jnp.where(here == 2, unit, c_groups[g].astype(F32)).astype(BF16)
            product = dot(theirs, came) + dot(c_own[g], local)
        else:
            product = dot(c_groups[g], came)
        value = gated[:, at : at + CHUNK] + product * gate_entry[:, at : at + CHUNK]
        gated[:, at : at + CHUNK] = value
        for i in range(CHUNK // 128):
            piece = value[:, i * 128 : (i + 1) * 128]
            squares[g] = squares[g] + piece * piece if g in squares else piece * piece

    def normalize(g):
        left = g * group_width
        mean = jnp.sum(squares[g], axis=1, keepdims=True) * (1.0 / group_width)
        mamba_ref[:, left : left + group_width] = (
            gated[:, left : left + group_width]
            * lax.rsqrt(mean + EPSILON)
            * gain_ref[:, left : left + group_width]
        ).astype(BF16)

    fetches[11].wait()

    def take_keys():
        @pl.when(has_left)
        def _():
            own_k.wait_recv()
            own_v.wait_recv()

    def take_turned():
        @pl.when(middle)
        def _():
            c_back.wait_recv()
            for g in range(groups):
                theirs = c_next[g].astype(F32)
                c_ahead[g] = jnp.where(ahead, theirs, 0.0).astype(BF16)
                c_next[g] = jnp.where(ahead, theirs, unit).astype(BF16)

    def take_rest():
        for fetch in fetches[12:]:
            fetch.wait()

    held = []

    def attend_next(head):
        if not held:
            held.append(permitted_keys())
        attend(head, held[0])

    steps = {
        "l": make_local, "q": lambda c: make_ready(range(2 * c, 2 * c + 2)), "p": pass_on, "n": normalize,
        "e": lambda _: early_send(), "x": lambda _: early_pass(), "y": lambda _: late_pass(),
        "o": lambda _: first_send(chunks - 1), "r": arrive, "i": inside, "a": attend_next, "f": finish,
        "k": lambda _: take_keys(), "t": lambda _: take_turned(), "w": lambda _: take_rest(),
    }
    for name, low_end, high_end in ORDER:
        for at in range(low_end, high_end):
            steps[name](at)

    @pl.when(has_right)
    def _():
        halo_copy.wait_send()
        own_k.wait_send()
        own_v.wait_send()
        for i in range(chunks * per):
            state_copy(i).wait_send()

    @pl.when(here >= 2)
    def _():
        c_back.wait_send()


def write_out(mamba_ref, attn_ref, mamba_hbm, attn_hbm, sems):
    copies = [
        pltpu.make_async_copy(mamba_ref, mamba_hbm, sems.at[0]),
        pltpu.make_async_copy(attn_ref, attn_hbm, sems.at[1]),
    ]
    for copy in copies:
        copy.start()
    for copy in copies:
        copy.wait()


def shards(n, *args):
    (
        x_raw, bc_raw, z_gate, dt_raw, cxw, cxb, cbw, cbb, dtb, a_log, skip_d, gain, queries, keys,
        values, doc_lens,
    ) = args
    operands = (
        x_raw, bc_raw, z_gate, dt_raw.T, cxw, cxb[None], cbw, cbb[None], dtb[None], a_log[None],
        skip_d[None], gain[None], queries, keys, values, doc_lens,
    )
    rows, width = x_raw.shape
    bc_width = bc_raw.shape[1]
    chunks = width // CHUNK
    reach = max(1, n // 2)
    vmem = pl.BlockSpec(memory_space=pltpu.VMEM)
    dma = pltpu.SemaphoreType.DMA
    if n == 4 and rows == STATE and keys.shape[1] == CHUNK and width == 8 * CHUNK and (
        queries.shape[1] == 8 * ADIM
    ):
        subs = width // SUB
        state = pltpu.VMEM((subs, STATE, SUB), BF16)
        turned = pltpu.VMEM((bc_width // (2 * STATE), rows, STATE), BF16)
        body = functools.partial(packed_kernel, n)
        ready = pltpu.VMEM((subs, rows, SUB), F32)
        buffers = [pltpu.VMEM((2,) + keys.shape, BF16), state, state, turned, turned, turned, ready]
        buffers.append(pltpu.VMEM((CHUNK // SUB, STATE, SUB), BF16))
        sems = [dma((2,)), dma((2,)), dma((subs,)), dma((subs,)), dma((2,)), dma((2,))]
    else:
        state = pltpu.VMEM((chunks, STATE, CHUNK), BF16)
        body = functools.partial(relay_kernel, n, reach)
        buffers = [pltpu.VMEM((reach, 2) + keys.shape, BF16), state, state]
        sems = [dma((reach, 2)), dma((reach, 2)), dma((chunks,)), dma((chunks,))]
    results = pl.pallas_call(
        body,
        out_shape=(pltpu.VMEM((rows, width), BF16), pltpu.VMEM(queries.shape, BF16)),
        in_specs=[pl.BlockSpec(memory_space=pltpu.HBM)] * 16,
        out_specs=(vmem, vmem),
        scratch_shapes=[
            pltpu.VMEM((16, bc_width), BF16),
            pltpu.VMEM((16, bc_width), BF16),
        ]
        + buffers
        + [
            pltpu.VMEM((rows + 8, width), F32),
            pltpu.VMEM((rows + 8, bc_width), F32),
            pltpu.VMEM((rows, width), BF16),
            pltpu.VMEM((rows, width), F32),
            pltpu.VMEM((rows, width), F32),
            dma,
            dma,
        ]
        + sems
        + [dma((17,)), pltpu.VMEM((16, width), BF16)]
        + [pltpu.VMEM(a.shape, a.dtype) for a in operands[:-1]]
        + [pltpu.SMEM(doc_lens.shape, jnp.int32)],
        compiler_params=pltpu.CompilerParams(
            collective_id=0, has_side_effects=True, vmem_limit_bytes=60 * 1024 * 1024
        ),
    )(*operands)
    hbm = pl.BlockSpec(memory_space=pltpu.HBM)
    return pl.pallas_call(
        write_out,
        out_shape=(
            jax.ShapeDtypeStruct((rows, width), BF16),
            jax.ShapeDtypeStruct(queries.shape, BF16),
        ),
        in_specs=[vmem, vmem],
        out_specs=(hbm, hbm),
        scratch_shapes=[dma((2,))],
    )(*[pltpu.with_memory_space_constraint(r, pltpu.VMEM) for r in results])


def solution(mesh):
    both = P(("groups", "seq"), "dp")
    placed = (
        both, both, both, both, P(None, "dp"), P("dp"), P(None, "dp"), P("dp"), P("dp"), P("dp"),
        P("dp"), P("dp"), both, both, both, P("groups"),
    )
    return jax.shard_map(
        functools.partial(shards, mesh.shape["seq"]),
        mesh=mesh,
        in_specs=placed,
        out_specs=(both, both),
        check_vma=False,
    )
```

```python
import functools
import jax
import jax.numpy as jnp
from jax import lax
from jax.experimental import pallas as pl
from jax.experimental.pallas import tpu as pltpu
from jax.sharding import PartitionSpec as P

HDIM = 64
STATE = 128
QHEADS = 32
KVHEADS = 8
ADIM = 128
EPSILON = 1e-05
NEGATIVE = -1e30
LOG2E = 1.4426950408889634
HIGHEST = lax.Precision.HIGHEST
F32 = jnp.float32
BF16 = jnp.bfloat16
CHUNK = 256
NT = (((1,), (1,)), ((), ()))


def silu(value):
    half = 0.5 * value
    return half + half * jnp.tanh(half)


def dot(a, b):
    return jnp.dot(a, b, preferred_element_type=F32)


def wide(tile, width):
    return jnp.concatenate([tile] * (width // tile.shape[1]), axis=1)


def relay_kernel(
    n,
    reach,
    x_hbm, bc_hbm, z_hbm, dt_hbm, cxw_hbm, cxb_hbm, cbw_hbm, cbb_hbm,
    dtb_hbm, alog_hbm, skip_hbm, gain_hbm, q_hbm, k_hbm, v_hbm, lens_hbm,
    mamba_ref,
    attn_ref,
    halo_out,
    halo_in,
    kv,
    state_in,
    state_out,
    xf,
    bcf,
    xc,
    gated,
    gate_entry,
    small_send,
    small_recv,
    kv_send,
    kv_recv,
    st_send,
    st_recv,
    fetch_sem,
    x_tail,
    x_ref, bc_ref, z_ref, dt_ref, cxw_ref, cxb_ref, cbw_ref, cbb_ref,
    dtb_ref, alog_ref, skip_ref, gain_ref, q_ref, k_ref, v_ref, lens_ref,
):
    here = lax.axis_index("seq")
    rows, width = x_ref.shape
    fetches = [
        pltpu.make_async_copy(source, target, fetch_sem.at[i])
        for i, (source, target) in enumerate(
            (
                (x_hbm.at[pl.ds(rows - 16, 16), :], x_tail),
                (bc_hbm, bc_ref),
                (lens_hbm, lens_ref),
                (dt_hbm, dt_ref),
                (dtb_hbm, dtb_ref),
                (alog_hbm, alog_ref),
                (skip_hbm, skip_ref),
                (cbw_hbm, cbw_ref),
                (cbb_hbm, cbb_ref),
                (cxw_hbm, cxw_ref),
                (cxb_hbm, cxb_ref),
                (x_hbm, x_ref),
                (z_hbm, z_ref),
                (k_hbm, k_ref),
                (v_hbm, v_ref),
                (q_hbm, q_ref),
                (gain_hbm, gain_ref),
            )
        )
    ]
    for fetch in fetches:
        fetch.start()
    bc_width = bc_ref.shape[1]
    heads = dt_ref.shape[0]
    groups = bc_width // (2 * STATE)
    chunks = width // CHUNK
    group_width = width // groups
    taps = cxw_ref.shape[0]
    margin = taps - 1
    has_left = here > 0
    has_right = here < n - 1
    right = {"seq": here + 1}

    def remote(src, dst, send, recv):
        return pltpu.make_async_remote_copy(
            src_ref=src,
            dst_ref=dst,
            send_sem=send,
            recv_sem=recv,
            device_id=right,
            device_id_type=pl.DeviceIdType.MESH,
        )

    barrier = pltpu.get_barrier_semaphore()

    @pl.when(has_left)
    def _():
        pl.semaphore_signal(
            barrier, inc=1, device_id={"seq": here - 1}, device_id_type=pl.DeviceIdType.MESH
        )

    @pl.when(has_right)
    def _():
        pl.semaphore_signal(
            barrier, inc=1, device_id={"seq": here + 1}, device_id_type=pl.DeviceIdType.MESH
        )

    fetches[0].wait()
    fetches[1].wait()
    blocks = width // bc_width
    tail_x = x_tail[...].astype(F32)[16 - margin :]
    tail_bc = bc_ref[rows - 16 :, :].astype(F32)[16 - margin :]
    pieces = [tail_x[:, b * bc_width : (b + 1) * bc_width] for b in range(blocks)] + [tail_bc]
    pieces.append(jnp.zeros((16 - margin * (blocks + 1), bc_width), F32))
    halo_out[...] = jnp.concatenate(pieces, axis=0).astype(BF16)

    @pl.when(has_left & has_right)
    def _():
        pl.semaphore_wait(barrier, 2)

    @pl.when(jnp.logical_not(has_left & has_right))
    def _():
        pl.semaphore_wait(barrier, 1)

    halo_copy = remote(halo_out, halo_in, small_send, small_recv)
    own_k = remote(k_hbm, kv.at[0, 0], kv_send.at[0, 0], kv_recv.at[0, 0])
    own_v = remote(v_hbm, kv.at[0, 1], kv_send.at[0, 1], kv_recv.at[0, 1])

    @pl.when(has_right)
    def _():
        halo_copy.start()
        own_k.start()
        own_v.start()

    for fetch in fetches[2:11]:
        fetch.wait()
    first = here * rows
    starts = []
    running_start = jnp.int32(0)
    for d in range(lens_ref.shape[0]):
        starts.append(running_start)
        running_start = running_start + lens_ref[d]

    def doc_of(positions):
        total = jnp.full(positions.shape, -1, jnp.int32)
        for start in starts:
            total = total + jnp.where(start <= positions, 1, 0)
        return total

    square = (rows, 128)
    pos_i = first + lax.broadcasted_iota(jnp.int32, square, 0)
    pos_j = first + lax.broadcasted_iota(jnp.int32, (rows, rows), 1)
    doc_i = doc_of(pos_i)
    doc_j = doc_of(pos_j)
    linked = (doc_i == doc_j) & (pos_i >= pos_j)
    before = doc_of(jnp.full((1, 128), first - 1, jnp.int32))
    last = doc_of(jnp.full((1, 128), first + rows - 1, jnp.int32))
    same = [
        jnp.where(doc_of(pos_i - (margin - lag)) == doc_i, 1.0, 0.0) for lag in range(margin)
    ]

    raw = dt_ref[...].T + dtb_ref[...]
    step = jnp.maximum(raw, 0.0) + jnp.log1p(jnp.exp(-jnp.abs(raw)))
    decay = step * (jnp.exp(alog_ref[...]) * (-LOG2E))
    order_i = lax.broadcasted_iota(jnp.int32, (rows, rows), 0)
    order_j = lax.broadcasted_iota(jnp.int32, (rows, rows), 1)
    lower = jnp.where(order_i >= order_j, 1.0, 0.0)
    running = jnp.dot(lower, decay, precision=HIGHEST, preferred_element_type=F32)
    final = running[rows - 1 : rows]
    row_of = (running - jnp.log2(step)).T
    tail = jnp.where(
        (doc_i == last)[:, :heads], jnp.exp2(final - running) * step, 0.0
    )
    entry = jnp.where((doc_i == before)[:, :heads], jnp.exp2(running), 0.0)
    through = jnp.where((last == before)[:, :heads], jnp.exp2(final), 0.0)
    stack = jnp.concatenate(
        [
            tail,
            entry,
            jnp.broadcast_to(through, (8, heads)),
            jnp.broadcast_to(skip_ref[...], (8, heads)),
        ],
        axis=0,
    )
    high = stack.astype(BF16)
    low = (stack - high.astype(F32)).astype(BF16)

    @pl.when(has_left)
    def _():
        halo_copy.wait_recv()

    @pl.when(here == 0)
    def _():
        halo_in[...] = jnp.zeros_like(halo_in)
        state_in[...] = jnp.zeros_like(state_in)

    for s in range(reach):
        @pl.when(here < s + 1)
        def _(s=s):
            kv[s] = jnp.zeros_like(kv[s])

    halo = halo_in[...].astype(F32)
    for b in range(blocks):
        xf[8 - margin : 8, b * bc_width : (b + 1) * bc_width] = halo[
            b * margin : (b + 1) * margin
        ]
    bcf[8 - margin : 8, :] = halo[blocks * margin : (blocks + 1) * margin]
    bcf[8:, :] = bc_ref[...].astype(F32)

    def conv(source, weight_ref, bias_ref, at, size):
        total = source[8 : 8 + rows, at : at + size] * weight_ref[margin : margin + 1, at : at + size]
        total = total + bias_ref[:, at : at + size]
        for lag in range(margin):
            moved = source[8 - margin + lag : 8 - margin + lag + rows, at : at + size]
            total = total + moved * weight_ref[lag : lag + 1, at : at + size] * wide(
                same[lag], size
            )
        return silu(total).astype(BF16)

    b_turned, c_groups, crossed = [], [], []
    for g in range(groups):
        b_here = conv(bcf, cbw_ref, cbb_ref, 2 * g * STATE, STATE)
        c_here = conv(bcf, cbw_ref, cbb_ref, (2 * g + 1) * STATE, STATE)
        b_turned.append(b_here.astype(F32).T.astype(BF16))
        c_groups.append(c_here)
        crossed.append(lax.dot_general(c_here, b_here, NT, preferred_element_type=F32))

    def state_copy(c):
        return remote(state_out.at[c], state_in.at[c], st_send.at[c], st_recv.at[c])

    lane_head = lax.broadcasted_iota(jnp.int32, (heads, CHUNK), 1) // HDIM
    head_row = lax.broadcasted_iota(jnp.int32, (heads, CHUNK), 0)
    per_chunk = CHUNK // HDIM
    low_half = lax.broadcasted_iota(jnp.int32, (rows, 128), 1) < HDIM

    fetches[11].wait()
    carried = []
    for c in range(chunks):
        at = c * CHUNK
        g = at // group_width
        xf[8:, at : at + CHUNK] = x_ref[:, at : at + CHUNK].astype(F32)
        x_here = conv(xf, cxw_ref, cxb_ref, at, CHUNK)
        xc[:, at : at + CHUNK] = x_here
        spread = jnp.where(head_row == lane_head + c * per_chunk, 1.0, 0.0).astype(BF16)
        expanded = dot(high, spread) + dot(low, spread)
        x32 = x_here.astype(F32)
        local = dot(b_turned[g], (x32 * expanded[:rows]).astype(BF16))
        gate_entry[:, at : at + CHUNK] = expanded[rows : 2 * rows]
        gated[:, at : at + CHUNK] = x32 * expanded[2 * rows + 8 : 2 * rows + 9]
        carried.append(expanded[2 * rows : 2 * rows + 1])
        state_out[c] = local.astype(BF16)

        @pl.when(here == 0)
        def _(c=c):
            state_copy(c).start()

    for s in range(1, reach):
        @pl.when(here >= s)
        def _(s=s):
            for i in range(2):
                remote(
                    kv.at[s - 1, i], kv.at[s - 1, i], kv_send.at[s - 1, i], kv_recv.at[s - 1, i]
                ).wait_recv()

        @pl.when((here >= s) & has_right)
        def _(s=s):
            for i in range(2):
                remote(
                    kv.at[s - 1, i], kv.at[s, i], kv_send.at[s, i], kv_recv.at[s, i]
                ).start()

    for fetch in fetches[12:]:
        fetch.wait()

    kv_local = k_ref.shape[1] // ADIM
    share = q_ref.shape[1] // (ADIM * kv_local)
    scale = ADIM**-0.5 * LOG2E
    key_count = (reach + 1) * rows
    key_pos = (
        first - reach * rows + lax.broadcasted_iota(jnp.int32, (rows, key_count), 1)
    )
    key_docs = doc_of(key_pos)
    permitted = (key_docs == wide(doc_i, key_count)) & (key_pos <= wide(pos_i, key_count))

    def attend(head):
        g = head // share
        cols = slice(g * ADIM, (g + 1) * ADIM)
        keys = jnp.concatenate(
            [kv[s, 0, :, cols] for s in reversed(range(reach))] + [k_ref[:, cols]], axis=0
        )
        values = jnp.concatenate(
            [kv[s, 1, :, cols] for s in reversed(range(reach))] + [v_ref[:, cols]], axis=0
        )
        query = q_ref[:, head * ADIM : (head + 1) * ADIM]
        scores = lax.dot_general(query, keys, NT, preferred_element_type=F32)
        scores = jnp.where(permitted, scores, NEGATIVE)
        peak = jnp.max(scores, axis=1, keepdims=True)
        expo = jnp.exp2((scores - peak) * scale)
        total = jnp.sum(expo, axis=1, keepdims=True)
        summed = dot(expo.astype(BF16), values)
        attn_ref[:, head * ADIM : (head + 1) * ADIM] = (summed / total).astype(BF16)

    q_heads = kv_local * share
    early = chunks // 4
    for c in range(chunks):
        at = c * CHUNK
        g = at // group_width
        gate = silu(z_ref[:, at : at + CHUNK].astype(F32))
        for pair in range(CHUNK // 128):
            col = at + pair * 128
            head = col // HDIM
            parts = []
            for h in (head, head + 1):
                exponent = running[:, h : h + 1] - row_of[h : h + 1, :]
                parts.append(
                    (jnp.exp2(jnp.where(linked, exponent, NEGATIVE)) * crossed[g]).astype(BF16)
                )
            x_pair = xc[:, col : col + 128]
            zero = jnp.zeros_like(x_pair)
            stacked = jnp.concatenate(
                [jnp.where(low_half, x_pair, zero), jnp.where(low_half, zero, x_pair)], axis=0
            )
            inside = dot(jnp.concatenate(parts, axis=1), stacked)
            gated[:, col : col + 128] = (gated[:, col : col + 128] + inside) * gate[
                :, pair * 128 : (pair + 1) * 128
            ]
        gate_entry[:, at : at + CHUNK] = gate_entry[:, at : at + CHUNK] * gate

        @pl.when(has_left)
        def _(c=c):
            state_copy(c).wait_recv()

        @pl.when(has_left & has_right)
        def _(c=c):
            state_out[c] = (
                state_out[c].astype(F32) + state_in[c].astype(F32) * carried[c]
            ).astype(BF16)
            state_copy(c).start()

        if c == early:
            @pl.when(here >= reach)
            def _():
                for i in range(2):
                    remote(
                        kv.at[reach - 1, i],
                        kv.at[reach - 1, i],
                        kv_send.at[reach - 1, i],
                        kv_recv.at[reach - 1, i],
                    ).wait_recv()

        if early <= c < chunks - 1:
            span = chunks - early - 1
            for head in range((c - early) * q_heads // span, (c - early + 1) * q_heads // span):
                attend(head)

        gated[:, at : at + CHUNK] = (
            gated[:, at : at + CHUNK]
            + dot(c_groups[g], state_in[c]) * gate_entry[:, at : at + CHUNK]
        )
        if (at + CHUNK) % group_width == 0:
            left = at + CHUNK - group_width
            value = gated[:, left : left + group_width]
            mean = jnp.sum(value * value, axis=1, keepdims=True) * (1.0 / group_width)
            mamba_ref[:, left : left + group_width] = (
                value * lax.rsqrt(mean + EPSILON) * gain_ref[:, left : left + group_width]
            ).astype(BF16)

    @pl.when(has_right)
    def _():
        halo_copy.wait_send()
        own_k.wait_send()
        own_v.wait_send()
        for c in range(chunks):
            state_copy(c).wait_send()

    for s in range(1, reach):
        @pl.when((here >= s) & has_right)
        def _(s=s):
            for i in range(2):
                remote(
                    kv.at[s - 1, i], kv.at[s, i], kv_send.at[s, i], kv_recv.at[s, i]
                ).wait_send()


SUB = 128
EARLY = 2
ORDER = (
    ("l", 6, 7),
    ("e", 6, 7),
    ("l", 7, 8),
    ("e", 7, 8),
    ("l", 0, 6),
    ("o", 6, 8),
    ("k", 0, 1),
    ("t", 0, 1),
    ("q", 0, 4),
    ("x", 6, 8),
    ("p", 0, 1),
    ("w", 0, 1),
    ("i", 0, 4),
    ("p", 1, 2),
    ("i", 4, 8),
    ("p", 2, 3),
    ("r", 0, 2),
    ("a", 0, 3),
    ("p", 3, 4),
    ("a", 3, 6),
    ("p", 4, 5),
    ("a", 6, 8),
    ("p", 5, 6),
    ("f", 0, 2),
    ("r", 2, 3),
    ("f", 2, 3),
    ("r", 3, 4),
    ("f", 3, 4),
    ("n", 0, 1),
    ("y", 6, 8),
    ("r", 4, 5),
    ("f", 4, 5),
    ("r", 6, 7),
    ("f", 6, 7),
    ("r", 7, 8),
    ("f", 7, 8),
    ("r", 5, 6),
    ("f", 5, 6),
    ("n", 1, 2),
)


def packed_kernel(
    n,
    x_hbm, bc_hbm, z_hbm, dt_hbm, cxw_hbm, cxb_hbm, cbw_hbm, cbb_hbm,
    dtb_hbm, alog_hbm, skip_hbm, gain_hbm, q_hbm, k_hbm, v_hbm, lens_hbm,
    mamba_ref,
    attn_ref,
    halo_out,
    halo_in,
    kv,
    state_in,
    state_out,
    c_mine,
    c_next,
    c_ahead,
    ready,
    extra,
    xf,
    bcf,
    xc,
    gated,
    gate_entry,
    small_send,
    small_recv,
    kv_send,
    kv_recv,
    st_send,
    st_recv,
    c_sem,
    extra_sem,
    fetch_sem,
    x_tail,
    x_ref, bc_ref, z_ref, dt_ref, cxw_ref, cxb_ref, cbw_ref, cbb_ref,
    dtb_ref, alog_ref, skip_ref, gain_ref, q_ref, k_ref, v_ref, lens_ref,
):
    here = lax.axis_index("seq")
    has_left = here > 0
    has_right = here < n - 1
    middle = has_left & has_right
    barrier = pltpu.get_barrier_semaphore()

    @pl.when(has_left)
    def _():
        pl.semaphore_signal(
            barrier, inc=1, device_id={"seq": here - 1}, device_id_type=pl.DeviceIdType.MESH
        )

    @pl.when(has_right)
    def _():
        pl.semaphore_signal(
            barrier, inc=1, device_id={"seq": here + 1}, device_id_type=pl.DeviceIdType.MESH
        )

    rows, width = x_ref.shape
    fetches = [
        pltpu.make_async_copy(source, target, fetch_sem.at[i])
        for i, (source, target) in enumerate(
            (
                (x_hbm.at[pl.ds(rows - 16, 16), :], x_tail),
                (bc_hbm, bc_ref),
                (lens_hbm, lens_ref),
                (dt_hbm, dt_ref),
                (dtb_hbm, dtb_ref),
                (alog_hbm, alog_ref),
                (skip_hbm, skip_ref),
                (cbw_hbm, cbw_ref),
                (cbb_hbm, cbb_ref),
                (cxw_hbm, cxw_ref),
                (cxb_hbm, cxb_ref),
                (x_hbm, x_ref),
                (z_hbm, z_ref),
                (k_hbm, k_ref),
                (v_hbm, v_ref),
                (q_hbm, q_ref),
                (gain_hbm, gain_ref),
            )
        )
    ]
    for fetch in fetches:
        fetch.start()
    bc_width = bc_ref.shape[1]
    heads = dt_ref.shape[0]
    groups = bc_width // (2 * STATE)
    chunks = width // CHUNK
    per = CHUNK // SUB
    group_width = width // groups
    taps = cxw_ref.shape[0]
    margin = taps - 1

    def remote(src, dst, send, recv, to=1):
        return pltpu.make_async_remote_copy(
            src_ref=src,
            dst_ref=dst,
            send_sem=send,
            recv_sem=recv,
            device_id={"seq": here + to},
            device_id_type=pl.DeviceIdType.MESH,
        )

    fetches[0].wait()
    fetches[1].wait()
    blocks = width // bc_width
    tail_x = x_tail[...].astype(F32)[16 - margin :]
    tail_bc = bc_ref[rows - 16 :, :].astype(F32)[16 - margin :]
    pieces = [tail_x[:, b * bc_width : (b + 1) * bc_width] for b in range(blocks)] + [tail_bc]
    pieces.append(jnp.zeros((16 - margin * (blocks + 1), bc_width), F32))
    halo_out[...] = jnp.concatenate(pieces, axis=0).astype(BF16)

    @pl.when(middle)
    def _():
        pl.semaphore_wait(barrier, 2)

    @pl.when(jnp.logical_not(middle))
    def _():
        pl.semaphore_wait(barrier, 1)

    halo_copy = remote(halo_out, halo_in, small_send, small_recv)
    own_k = remote(k_hbm, kv.at[0], kv_send.at[0], kv_recv.at[0])
    own_v = remote(v_hbm, kv.at[1], kv_send.at[1], kv_recv.at[1])
    c_back = remote(c_mine, c_next, c_sem.at[0], c_sem.at[1], -1)

    @pl.when(has_right)
    def _():
        halo_copy.start()
        own_k.start()
        own_v.start()

    for fetch in fetches[2:11]:
        fetch.wait()
    first = here * rows
    starts = []
    running_start = jnp.int32(0)
    for d in range(lens_ref.shape[0]):
        starts.append(running_start)
        running_start = running_start + lens_ref[d]

    def doc_of(positions):
        total = jnp.full(positions.shape, -1, jnp.int32)
        for start in starts:
            total = total + jnp.where(start <= positions, 1, 0)
        return total

    def doc_at(position):
        return doc_of(jnp.full((1, 128), position, jnp.int32))

    square = (rows, 128)
    pos_i = first + lax.broadcasted_iota(jnp.int32, square, 0)
    pos_j = first + lax.broadcasted_iota(jnp.int32, (rows, rows), 1)
    doc_i = doc_of(pos_i)
    doc_j = doc_of(pos_j)
    linked = (doc_i == doc_j) & (pos_i >= pos_j)
    before = doc_at(first - 1)
    last = doc_at(first + rows - 1)
    same = [
        jnp.where(doc_of(pos_i - (margin - lag)) == doc_i, 1.0, 0.0) for lag in range(margin)
    ]
    ahead = doc_of(pos_i + rows) == before
    spare = (doc_at(first + rows) == before) & jnp.logical_not(ahead)
    rows_came = doc_at(first - rows - 1) == doc_at(first)

    raw = dt_ref[...].T + dtb_ref[...]
    step = jnp.maximum(raw, 0.0) + jnp.log1p(jnp.exp(-jnp.abs(raw)))
    decay = step * (jnp.exp(alog_ref[...]) * (-LOG2E))
    order_i = lax.broadcasted_iota(jnp.int32, (rows, rows), 0)
    order_j = lax.broadcasted_iota(jnp.int32, (rows, rows), 1)
    unit = jnp.where(order_i == order_j, 1.0, 0.0)
    lower = jnp.where(order_i >= order_j, 1.0, 0.0)
    running = jnp.dot(lower, decay, precision=HIGHEST, preferred_element_type=F32)
    final = running[rows - 1 : rows]
    row_of = (running - jnp.log2(step)).T
    tail = jnp.where(
        (doc_i == last)[:, :heads], jnp.exp2(final - running) * step, 0.0
    )
    entry = jnp.where((doc_i == before)[:, :heads], jnp.exp2(running), 0.0)
    through = jnp.where((last == before)[:, :heads], jnp.exp2(final), 0.0)
    stack = jnp.concatenate(
        [
            tail,
            entry,
            jnp.broadcast_to(through, (8, heads)),
            jnp.broadcast_to(skip_ref[...], (8, heads)),
        ],
        axis=0,
    )
    high = stack.astype(BF16)
    low = (stack - high.astype(F32)).astype(BF16)

    @pl.when(has_left)
    def _():
        halo_copy.wait_recv()

    @pl.when(here == 0)
    def _():
        halo_in[...] = jnp.zeros_like(halo_in)
        state_in[...] = jnp.zeros_like(state_in)
        kv[...] = jnp.zeros_like(kv)

    @pl.when(here != 2)
    def _():
        extra[...] = jnp.zeros_like(extra)

    halo = halo_in[...].astype(F32)
    for b in range(blocks):
        xf[8 - margin : 8, b * bc_width : (b + 1) * bc_width] = halo[
            b * margin : (b + 1) * margin
        ]
    bcf[8 - margin : 8, :] = halo[blocks * margin : (blocks + 1) * margin]
    bcf[8:, :] = bc_ref[...].astype(F32)

    def conv(source, weight_ref, bias_ref, at, size):
        total = source[8 : 8 + rows, at : at + size] * weight_ref[margin : margin + 1, at : at + size]
        total = total + bias_ref[:, at : at + size]
        for lag in range(margin):
            moved = source[8 - margin + lag : 8 - margin + lag + rows, at : at + size]
            total = total + moved * weight_ref[lag : lag + 1, at : at + size] * wide(
                same[lag], size
            )
        return silu(total).astype(BF16)

    b_turned, c_groups, crossed, c_own = [], [], [], []
    for g in range(groups):
        b_here = conv(bcf, cbw_ref, cbb_ref, 2 * g * STATE, STATE)
        c_here = conv(bcf, cbw_ref, cbb_ref, (2 * g + 1) * STATE, STATE)
        b_turned.append(b_here.astype(F32).T.astype(BF16))
        c_mine[g] = c_here
        c_own.append(c_here)
        c_groups.append(jnp.where(rows_came, unit, c_here.astype(F32)).astype(BF16))
        crossed.append(lax.dot_general(c_here, b_here, NT, preferred_element_type=F32))

    @pl.when(here >= 2)
    def _():
        c_back.start()

    def state_copy(i):
        return remote(state_out.at[i], state_in.at[i], st_send.at[i], st_recv.at[i])

    kv_local = k_ref.shape[1] // ADIM
    lane_head = lax.broadcasted_iota(jnp.int32, (heads, CHUNK), 1) // HDIM
    head_row = lax.broadcasted_iota(jnp.int32, (heads, CHUNK), 0)
    per_chunk = CHUNK // HDIM
    low_half = lax.broadcasted_iota(jnp.int32, (rows, 128), 1) < HDIM
    carried = {}

    def make_local(c):
        at = c * CHUNK
        g = at // group_width
        xf[8:, at : at + CHUNK] = x_ref[:, at : at + CHUNK].astype(F32)
        x_here = conv(xf, cxw_ref, cxb_ref, at, CHUNK)
        xc[:, at : at + CHUNK] = x_here
        spread = jnp.where(head_row == lane_head + c * per_chunk, 1.0, 0.0).astype(BF16)
        expanded = dot(high, spread) + dot(low, spread)
        x32 = x_here.astype(F32)
        local = dot(b_turned[g], (x32 * expanded[:rows]).astype(BF16)).astype(BF16)
        gate_entry[:, at : at + CHUNK] = expanded[rows : 2 * rows]
        gated[:, at : at + CHUNK] = x32 * expanded[2 * rows + 8 : 2 * rows + 9]
        carried[c] = expanded[2 * rows : 2 * rows + 1]
        for i in range(per):
            state_out[c * per + i] = local[:, i * SUB : (i + 1) * SUB]

        if c < chunks - EARLY:
            first_send(c)

    def first_send(c):
        @pl.when(here == 0)
        def _():
            for i in range(per):
                state_copy(c * per + i).start()

    def extra_copy(c):
        i = c - (chunks - EARLY)
        return remote(
            state_out.at[pl.ds(c * per, per)],
            extra.at[pl.ds(i * per, per)],
            extra_sem.at[0, i],
            extra_sem.at[1, i],
        )

    def early_send(c):
        @pl.when(here == 1)
        def _():
            extra_copy(c).start()

    def share(c, i):
        return carried[c][:, i * SUB : (i + 1) * SUB]

    def early_pass(c):
        g = c * CHUNK // group_width

        @pl.when(here == 2)
        def _():
            extra_copy(c).wait_recv()
            for i in range(per):
                at = c * per + i
                early = extra[at - (chunks - EARLY) * per]
                state_out[at] = (ready[at] + dot(c_ahead[g], early) * share(c, i)).astype(BF16)
                state_copy(at).start()

    def late_pass(c):
        g = c * CHUNK // group_width

        @pl.when(here == 1)
        def _():
            extra_copy(c).wait_send()
            for i in range(per):
                at = c * per + i
                state_copy(at).wait_recv()
                state_out[at] = (dot(c_ahead[g], state_in[at]) * share(c, i)).astype(BF16)
                state_copy(at).start()

    def make_ready(cs):
        @pl.when(middle)
        def _():
            for c in cs:
                g = c * CHUNK // group_width
                for i in range(per):
                    at = c * per + i
                    sent = dot(c_next[g], state_out[at])
                    if at < 2 * kv_local:
                        col = at % kv_local * ADIM
                        sent = jnp.where(
                            spare, kv[at // kv_local, :, col : col + ADIM].astype(F32), sent
                        )
                    ready[at] = sent

    def pass_on(c):
        g = c * CHUNK // group_width

        @pl.when(middle)
        def _():
            for i in range(per):
                at = c * per + i
                state_copy(at).wait_recv()
                state_out[at] = (
                    ready[at]
                    + dot(c_ahead[g], state_in[at]) * carried[c][:, i * SUB : (i + 1) * SUB]
                ).astype(BF16)
                state_copy(at).start()

    def arrive(c):
        @pl.when(here >= (2 if c >= chunks - EARLY else n - 1))
        def _():
            for i in range(per):
                state_copy(c * per + i).wait_recv()

    per_kv = q_ref.shape[1] // (ADIM * kv_local)
    scale = ADIM**-0.5 * LOG2E

    def permitted_keys():
        count = 3 * rows
        key_pos = first - 2 * rows + lax.broadcasted_iota(jnp.int32, (rows, count), 1)
        return (doc_of(key_pos) == wide(doc_i, count)) & (key_pos <= wide(pos_i, count))

    def attend(head, permitted):
        g = head // per_kv
        cols = slice(g * ADIM, (g + 1) * ADIM)
        keys = jnp.concatenate([state_in[g], kv[0, :, cols], k_ref[:, cols]], axis=0)
        values = jnp.concatenate([state_in[kv_local + g], kv[1, :, cols], v_ref[:, cols]], axis=0)
        query = q_ref[:, head * ADIM : (head + 1) * ADIM]
        scores = lax.dot_general(query, keys, NT, preferred_element_type=F32)
        scores = jnp.where(permitted, scores, NEGATIVE)
        peak = jnp.max(scores, axis=1, keepdims=True)
        expo = jnp.exp2((scores - peak) * scale)
        total = jnp.sum(expo, axis=1, keepdims=True)
        summed = dot(expo.astype(BF16), values)
        attn_ref[:, head * ADIM : (head + 1) * ADIM] = (summed / total).astype(BF16)

    def inside(c):
        at = c * CHUNK
        g = at // group_width
        gate = silu(z_ref[:, at : at + CHUNK].astype(F32))
        for pair in range(CHUNK // 128):
            col = at + pair * 128
            head = col // HDIM
            parts = []
            for h in (head, head + 1):
                exponent = running[:, h : h + 1] - row_of[h : h + 1, :]
                parts.append(
                    (jnp.exp2(jnp.where(linked, exponent, NEGATIVE)) * crossed[g]).astype(BF16)
                )
            x_pair = xc[:, col : col + 128]
            zero = jnp.zeros_like(x_pair)
            stacked = jnp.concatenate(
                [jnp.where(low_half, x_pair, zero), jnp.where(low_half, zero, x_pair)], axis=0
            )
            within = dot(jnp.concatenate(parts, axis=1), stacked)
            gated[:, col : col + 128] = (gated[:, col : col + 128] + within) * gate[
                :, pair * 128 : (pair + 1) * 128
            ]
        gate_entry[:, at : at + CHUNK] = gate_entry[:, at : at + CHUNK] * gate

    squares = {}

    def finish(c):
        at = c * CHUNK
        g = at // group_width
        came = jnp.concatenate([state_in[c * per + i] for i in range(per)], axis=1)
        if c >= chunks - EARLY:
            base = (c - (chunks - EARLY)) * per
            local = jnp.concatenate([extra[base + i] for i in range(per)], axis=1)
            theirs = jnp.where(here == 2, unit, c_groups[g].astype(F32)).astype(BF16)
            product = dot(theirs, came) + dot(c_own[g], local)
        else:
            product = dot(c_groups[g], came)
        value = gated[:, at : at + CHUNK] + product * gate_entry[:, at : at + CHUNK]
        gated[:, at : at + CHUNK] = value
        for i in range(CHUNK // 128):
            piece = value[:, i * 128 : (i + 1) * 128]
            squares[g] = squares[g] + piece * piece if g in squares else piece * piece

    def normalize(g):
        left = g * group_width
        mean = jnp.sum(squares[g], axis=1, keepdims=True) * (1.0 / group_width)
        mamba_ref[:, left : left + group_width] = (
            gated[:, left : left + group_width]
            * lax.rsqrt(mean + EPSILON)
            * gain_ref[:, left : left + group_width]
        ).astype(BF16)

    fetches[11].wait()

    def take_keys():
        @pl.when(has_left)
        def _():
            own_k.wait_recv()
            own_v.wait_recv()

    def take_turned():
        @pl.when(middle)
        def _():
            c_back.wait_recv()
            for g in range(groups):
                theirs = c_next[g].astype(F32)
                c_ahead[g] = jnp.where(ahead, theirs, 0.0).astype(BF16)
                c_next[g] = jnp.where(ahead, theirs, unit).astype(BF16)

    def take_rest():
        for fetch in fetches[12:]:
            fetch.wait()

    held = []

    def attend_next(head):
        if not held:
            held.append(permitted_keys())
        attend(head, held[0])

    steps = {
        "l": make_local, "q": lambda c: make_ready(range(2 * c, 2 * c + 2)), "p": pass_on, "n": normalize,
        "e": early_send, "x": early_pass, "y": late_pass, "o": first_send, "r": arrive, "i": inside, "a": attend_next, "f": finish,
        "k": lambda _: take_keys(), "t": lambda _: take_turned(), "w": lambda _: take_rest(),
    }
    for name, low_end, high_end in ORDER:
        for at in range(low_end, high_end):
            steps[name](at)

    @pl.when(has_right)
    def _():
        halo_copy.wait_send()
        own_k.wait_send()
        own_v.wait_send()
        for i in range(chunks * per):
            state_copy(i).wait_send()

    @pl.when(here >= 2)
    def _():
        c_back.wait_send()


def write_out(mamba_ref, attn_ref, mamba_hbm, attn_hbm, sems):
    copies = [
        pltpu.make_async_copy(mamba_ref, mamba_hbm, sems.at[0]),
        pltpu.make_async_copy(attn_ref, attn_hbm, sems.at[1]),
    ]
    for copy in copies:
        copy.start()
    for copy in copies:
        copy.wait()


def shards(n, *args):
    (
        x_raw, bc_raw, z_gate, dt_raw, cxw, cxb, cbw, cbb, dtb, a_log, skip_d, gain, queries, keys,
        values, doc_lens,
    ) = args
    operands = (
        x_raw, bc_raw, z_gate, dt_raw.T, cxw, cxb[None], cbw, cbb[None], dtb[None], a_log[None],
        skip_d[None], gain[None], queries, keys, values, doc_lens,
    )
    rows, width = x_raw.shape
    bc_width = bc_raw.shape[1]
    chunks = width // CHUNK
    reach = max(1, n // 2)
    vmem = pl.BlockSpec(memory_space=pltpu.VMEM)
    dma = pltpu.SemaphoreType.DMA
    if n == 4 and rows == STATE and keys.shape[1] == CHUNK and width == 8 * CHUNK and (
        queries.shape[1] == 8 * ADIM
    ):
        subs = width // SUB
        state = pltpu.VMEM((subs, STATE, SUB), BF16)
        turned = pltpu.VMEM((bc_width // (2 * STATE), rows, STATE), BF16)
        body = functools.partial(packed_kernel, n)
        ready = pltpu.VMEM((subs, rows, SUB), F32)
        buffers = [pltpu.VMEM((2,) + keys.shape, BF16), state, state, turned, turned, turned, ready]
        buffers.append(pltpu.VMEM((EARLY * CHUNK // SUB, STATE, SUB), BF16))
        sems = [dma((2,)), dma((2,)), dma((subs,)), dma((subs,)), dma((2,)), dma((2, EARLY))]
    else:
        state = pltpu.VMEM((chunks, STATE, CHUNK), BF16)
        body = functools.partial(relay_kernel, n, reach)
        buffers = [pltpu.VMEM((reach, 2) + keys.shape, BF16), state, state]
        sems = [dma((reach, 2)), dma((reach, 2)), dma((chunks,)), dma((chunks,))]
    results = pl.pallas_call(
        body,
        out_shape=(pltpu.VMEM((rows, width), BF16), pltpu.VMEM(queries.shape, BF16)),
        in_specs=[pl.BlockSpec(memory_space=pltpu.HBM)] * 16,
        out_specs=(vmem, vmem),
        scratch_shapes=[
            pltpu.VMEM((16, bc_width), BF16),
            pltpu.VMEM((16, bc_width), BF16),
        ]
        + buffers
        + [
            pltpu.VMEM((rows + 8, width), F32),
            pltpu.VMEM((rows + 8, bc_width), F32),
            pltpu.VMEM((rows, width), BF16),
            pltpu.VMEM((rows, width), F32),
            pltpu.VMEM((rows, width), F32),
            dma,
            dma,
        ]
        + sems
        + [dma((17,)), pltpu.VMEM((16, width), BF16)]
        + [pltpu.VMEM(a.shape, a.dtype) for a in operands[:-1]]
        + [pltpu.SMEM(doc_lens.shape, jnp.int32)],
        compiler_params=pltpu.CompilerParams(
            collective_id=0, has_side_effects=True, vmem_limit_bytes=60 * 1024 * 1024
        ),
    )(*operands)
    hbm = pl.BlockSpec(memory_space=pltpu.HBM)
    return pl.pallas_call(
        write_out,
        out_shape=(
            jax.ShapeDtypeStruct((rows, width), BF16),
            jax.ShapeDtypeStruct(queries.shape, BF16),
        ),
        in_specs=[vmem, vmem],
        out_specs=(hbm, hbm),
        scratch_shapes=[dma((2,))],
    )(*[pltpu.with_memory_space_constraint(r, pltpu.VMEM) for r in results])


def solution(mesh):
    both = P(("groups", "seq"), "dp")
    placed = (
        both, both, both, both, P(None, "dp"), P("dp"), P(None, "dp"), P("dp"), P("dp"), P("dp"),
        P("dp"), P("dp"), both, both, both, P("groups"),
    )
    return jax.shard_map(
        functools.partial(shards, mesh.shape["seq"]),
        mesh=mesh,
        in_specs=placed,
        out_specs=(both, both),
        check_vma=False,
    )
```

```python
import functools
import jax
import jax.numpy as jnp
from jax import lax
from jax.experimental import pallas as pl
from jax.experimental.pallas import tpu as pltpu
from jax.sharding import PartitionSpec as P

HDIM = 64
STATE = 128
QHEADS = 32
KVHEADS = 8
ADIM = 128
EPSILON = 1e-05
NEGATIVE = -1e30
LOG2E = 1.4426950408889634
HIGHEST = lax.Precision.HIGHEST
F32 = jnp.float32
BF16 = jnp.bfloat16
CHUNK = 256
NT = (((1,), (1,)), ((), ()))


def silu(value):
    half = 0.5 * value
    return half + half * jnp.tanh(half)


def dot(a, b):
    return jnp.dot(a, b, preferred_element_type=F32)


def wide(tile, width):
    return jnp.concatenate([tile] * (width // tile.shape[1]), axis=1)


def relay_kernel(
    n,
    reach,
    x_hbm, bc_hbm, z_hbm, dt_hbm, cxw_hbm, cxb_hbm, cbw_hbm, cbb_hbm,
    dtb_hbm, alog_hbm, skip_hbm, gain_hbm, q_hbm, k_hbm, v_hbm, lens_hbm,
    mamba_ref,
    attn_ref,
    halo_out,
    halo_in,
    kv,
    state_in,
    state_out,
    xf,
    bcf,
    xc,
    gated,
    gate_entry,
    small_send,
    small_recv,
    kv_send,
    kv_recv,
    st_send,
    st_recv,
    fetch_sem,
    x_tail,
    x_ref, bc_ref, z_ref, dt_ref, cxw_ref, cxb_ref, cbw_ref, cbb_ref,
    dtb_ref, alog_ref, skip_ref, gain_ref, q_ref, k_ref, v_ref, lens_ref,
):
    here = lax.axis_index("seq")
    rows, width = x_ref.shape
    fetches = [
        pltpu.make_async_copy(source, target, fetch_sem.at[i])
        for i, (source, target) in enumerate(
            (
                (x_hbm.at[pl.ds(rows - 16, 16), :], x_tail),
                (bc_hbm, bc_ref),
                (lens_hbm, lens_ref),
                (dt_hbm, dt_ref),
                (dtb_hbm, dtb_ref),
                (alog_hbm, alog_ref),
                (skip_hbm, skip_ref),
                (cbw_hbm, cbw_ref),
                (cbb_hbm, cbb_ref),
                (cxw_hbm, cxw_ref),
                (cxb_hbm, cxb_ref),
                (x_hbm, x_ref),
                (z_hbm, z_ref),
                (k_hbm, k_ref),
                (v_hbm, v_ref),
                (q_hbm, q_ref),
                (gain_hbm, gain_ref),
            )
        )
    ]
    for fetch in fetches:
        fetch.start()
    bc_width = bc_ref.shape[1]
    heads = dt_ref.shape[0]
    groups = bc_width // (2 * STATE)
    chunks = width // CHUNK
    group_width = width // groups
    taps = cxw_ref.shape[0]
    margin = taps - 1
    has_left = here > 0
    has_right = here < n - 1
    right = {"seq": here + 1}

    def remote(src, dst, send, recv):
        return pltpu.make_async_remote_copy(
            src_ref=src,
            dst_ref=dst,
            send_sem=send,
            recv_sem=recv,
            device_id=right,
            device_id_type=pl.DeviceIdType.MESH,
        )

    barrier = pltpu.get_barrier_semaphore()

    @pl.when(has_left)
    def _():
        pl.semaphore_signal(
            barrier, inc=1, device_id={"seq": here - 1}, device_id_type=pl.DeviceIdType.MESH
        )

    @pl.when(has_right)
    def _():
        pl.semaphore_signal(
            barrier, inc=1, device_id={"seq": here + 1}, device_id_type=pl.DeviceIdType.MESH
        )

    fetches[0].wait()
    fetches[1].wait()
    blocks = width // bc_width
    tail_x = x_tail[...].astype(F32)[16 - margin :]
    tail_bc = bc_ref[rows - 16 :, :].astype(F32)[16 - margin :]
    pieces = [tail_x[:, b * bc_width : (b + 1) * bc_width] for b in range(blocks)] + [tail_bc]
    pieces.append(jnp.zeros((16 - margin * (blocks + 1), bc_width), F32))
    halo_out[...] = jnp.concatenate(pieces, axis=0).astype(BF16)

    @pl.when(has_left & has_right)
    def _():
        pl.semaphore_wait(barrier, 2)

    @pl.when(jnp.logical_not(has_left & has_right))
    def _():
        pl.semaphore_wait(barrier, 1)

    halo_copy = remote(halo_out, halo_in, small_send, small_recv)
    own_k = remote(k_hbm, kv.at[0, 0], kv_send.at[0, 0], kv_recv.at[0, 0])
    own_v = remote(v_hbm, kv.at[0, 1], kv_send.at[0, 1], kv_recv.at[0, 1])

    @pl.when(has_right)
    def _():
        halo_copy.start()
        own_k.start()
        own_v.start()

    for fetch in fetches[2:11]:
        fetch.wait()
    first = here * rows
    starts = []
    running_start = jnp.int32(0)
    for d in range(lens_ref.shape[0]):
        starts.append(running_start)
        running_start = running_start + lens_ref[d]

    def doc_of(positions):
        total = jnp.full(positions.shape, -1, jnp.int32)
        for start in starts:
            total = total + jnp.where(start <= positions, 1, 0)
        return total

    square = (rows, 128)
    pos_i = first + lax.broadcasted_iota(jnp.int32, square, 0)
    pos_j = first + lax.broadcasted_iota(jnp.int32, (rows, rows), 1)
    doc_i = doc_of(pos_i)
    doc_j = doc_of(pos_j)
    linked = (doc_i == doc_j) & (pos_i >= pos_j)
    before = doc_of(jnp.full((1, 128), first - 1, jnp.int32))
    last = doc_of(jnp.full((1, 128), first + rows - 1, jnp.int32))
    same = [
        jnp.where(doc_of(pos_i - (margin - lag)) == doc_i, 1.0, 0.0) for lag in range(margin)
    ]

    raw = dt_ref[...].T + dtb_ref[...]
    step = jnp.maximum(raw, 0.0) + jnp.log1p(jnp.exp(-jnp.abs(raw)))
    decay = step * (jnp.exp(alog_ref[...]) * (-LOG2E))
    order_i = lax.broadcasted_iota(jnp.int32, (rows, rows), 0)
    order_j = lax.broadcasted_iota(jnp.int32, (rows, rows), 1)
    lower = jnp.where(order_i >= order_j, 1.0, 0.0)
    running = jnp.dot(lower, decay, precision=HIGHEST, preferred_element_type=F32)
    final = running[rows - 1 : rows]
    row_of = (running - jnp.log2(step)).T
    tail = jnp.where(
        (doc_i == last)[:, :heads], jnp.exp2(final - running) * step, 0.0
    )
    entry = jnp.where((doc_i == before)[:, :heads], jnp.exp2(running), 0.0)
    through = jnp.where((last == before)[:, :heads], jnp.exp2(final), 0.0)
    stack = jnp.concatenate(
        [
            tail,
            entry,
            jnp.broadcast_to(through, (8, heads)),
            jnp.broadcast_to(skip_ref[...], (8, heads)),
        ],
        axis=0,
    )
    high = stack.astype(BF16)
    low = (stack - high.astype(F32)).astype(BF16)

    @pl.when(has_left)
    def _():
        halo_copy.wait_recv()

    @pl.when(here == 0)
    def _():
        halo_in[...] = jnp.zeros_like(halo_in)
        state_in[...] = jnp.zeros_like(state_in)

    for s in range(reach):
        @pl.when(here < s + 1)
        def _(s=s):
            kv[s] = jnp.zeros_like(kv[s])

    halo = halo_in[...].astype(F32)
    for b in range(blocks):
        xf[8 - margin : 8, b * bc_width : (b + 1) * bc_width] = halo[
            b * margin : (b + 1) * margin
        ]
    bcf[8 - margin : 8, :] = halo[blocks * margin : (blocks + 1) * margin]
    bcf[8:, :] = bc_ref[...].astype(F32)

    def conv(source, weight_ref, bias_ref, at, size):
        total = source[8 : 8 + rows, at : at + size] * weight_ref[margin : margin + 1, at : at + size]
        total = total + bias_ref[:, at : at + size]
        for lag in range(margin):
            moved = source[8 - margin + lag : 8 - margin + lag + rows, at : at + size]
            total = total + moved * weight_ref[lag : lag + 1, at : at + size] * wide(
                same[lag], size
            )
        return silu(total).astype(BF16)

    b_turned, c_groups, crossed = [], [], []
    for g in range(groups):
        b_here = conv(bcf, cbw_ref, cbb_ref, 2 * g * STATE, STATE)
        c_here = conv(bcf, cbw_ref, cbb_ref, (2 * g + 1) * STATE, STATE)
        b_turned.append(b_here.astype(F32).T.astype(BF16))
        c_groups.append(c_here)
        crossed.append(lax.dot_general(c_here, b_here, NT, preferred_element_type=F32))

    def state_copy(c):
        return remote(state_out.at[c], state_in.at[c], st_send.at[c], st_recv.at[c])

    lane_head = lax.broadcasted_iota(jnp.int32, (heads, CHUNK), 1) // HDIM
    head_row = lax.broadcasted_iota(jnp.int32, (heads, CHUNK), 0)
    per_chunk = CHUNK // HDIM
    low_half = lax.broadcasted_iota(jnp.int32, (rows, 128), 1) < HDIM

    fetches[11].wait()
    carried = []
    for c in range(chunks):
        at = c * CHUNK
        g = at // group_width
        xf[8:, at : at + CHUNK] = x_ref[:, at : at + CHUNK].astype(F32)
        x_here = conv(xf, cxw_ref, cxb_ref, at, CHUNK)
        xc[:, at : at + CHUNK] = x_here
        spread = jnp.where(head_row == lane_head + c * per_chunk, 1.0, 0.0).astype(BF16)
        expanded = dot(high, spread) + dot(low, spread)
        x32 = x_here.astype(F32)
        local = dot(b_turned[g], (x32 * expanded[:rows]).astype(BF16))
        gate_entry[:, at : at + CHUNK] = expanded[rows : 2 * rows]
        gated[:, at : at + CHUNK] = x32 * expanded[2 * rows + 8 : 2 * rows + 9]
        carried.append(expanded[2 * rows : 2 * rows + 1])
        state_out[c] = local.astype(BF16)

        @pl.when(here == 0)
        def _(c=c):
            state_copy(c).start()

    for s in range(1, reach):
        @pl.when(here >= s)
        def _(s=s):
            for i in range(2):
                remote(
                    kv.at[s - 1, i], kv.at[s - 1, i], kv_send.at[s - 1, i], kv_recv.at[s - 1, i]
                ).wait_recv()

        @pl.when((here >= s) & has_right)
        def _(s=s):
            for i in range(2):
                remote(
                    kv.at[s - 1, i], kv.at[s, i], kv_send.at[s, i], kv_recv.at[s, i]
                ).start()

    for fetch in fetches[12:]:
        fetch.wait()

    kv_local = k_ref.shape[1] // ADIM
    share = q_ref.shape[1] // (ADIM * kv_local)
    scale = ADIM**-0.5 * LOG2E
    key_count = (reach + 1) * rows
    key_pos = (
        first - reach * rows + lax.broadcasted_iota(jnp.int32, (rows, key_count), 1)
    )
    key_docs = doc_of(key_pos)
    permitted = (key_docs == wide(doc_i, key_count)) & (key_pos <= wide(pos_i, key_count))

    def attend(head):
        g = head // share
        cols = slice(g * ADIM, (g + 1) * ADIM)
        keys = jnp.concatenate(
            [kv[s, 0, :, cols] for s in reversed(range(reach))] + [k_ref[:, cols]], axis=0
        )
        values = jnp.concatenate(
            [kv[s, 1, :, cols] for s in reversed(range(reach))] + [v_ref[:, cols]], axis=0
        )
        query = q_ref[:, head * ADIM : (head + 1) * ADIM]
        scores = lax.dot_general(query, keys, NT, preferred_element_type=F32)
        scores = jnp.where(permitted, scores, NEGATIVE)
        peak = jnp.max(scores, axis=1, keepdims=True)
        expo = jnp.exp2((scores - peak) * scale)
        total = jnp.sum(expo, axis=1, keepdims=True)
        summed = dot(expo.astype(BF16), values)
        attn_ref[:, head * ADIM : (head + 1) * ADIM] = (summed / total).astype(BF16)

    q_heads = kv_local * share
    early = chunks // 4
    for c in range(chunks):
        at = c * CHUNK
        g = at // group_width
        gate = silu(z_ref[:, at : at + CHUNK].astype(F32))
        for pair in range(CHUNK // 128):
            col = at + pair * 128
            head = col // HDIM
            parts = []
            for h in (head, head + 1):
                exponent = running[:, h : h + 1] - row_of[h : h + 1, :]
                parts.append(
                    (jnp.exp2(jnp.where(linked, exponent, NEGATIVE)) * crossed[g]).astype(BF16)
                )
            x_pair = xc[:, col : col + 128]
            zero = jnp.zeros_like(x_pair)
            stacked = jnp.concatenate(
                [jnp.where(low_half, x_pair, zero), jnp.where(low_half, zero, x_pair)], axis=0
            )
            inside = dot(jnp.concatenate(parts, axis=1), stacked)
            gated[:, col : col + 128] = (gated[:, col : col + 128] + inside) * gate[
                :, pair * 128 : (pair + 1) * 128
            ]
        gate_entry[:, at : at + CHUNK] = gate_entry[:, at : at + CHUNK] * gate

        @pl.when(has_left)
        def _(c=c):
            state_copy(c).wait_recv()

        @pl.when(has_left & has_right)
        def _(c=c):
            state_out[c] = (
                state_out[c].astype(F32) + state_in[c].astype(F32) * carried[c]
            ).astype(BF16)
            state_copy(c).start()

        if c == early:
            @pl.when(here >= reach)
            def _():
                for i in range(2):
                    remote(
                        kv.at[reach - 1, i],
                        kv.at[reach - 1, i],
                        kv_send.at[reach - 1, i],
                        kv_recv.at[reach - 1, i],
                    ).wait_recv()

        if early <= c < chunks - 1:
            span = chunks - early - 1
            for head in range((c - early) * q_heads // span, (c - early + 1) * q_heads // span):
                attend(head)

        gated[:, at : at + CHUNK] = (
            gated[:, at : at + CHUNK]
            + dot(c_groups[g], state_in[c]) * gate_entry[:, at : at + CHUNK]
        )
        if (at + CHUNK) % group_width == 0:
            left = at + CHUNK - group_width
            value = gated[:, left : left + group_width]
            mean = jnp.sum(value * value, axis=1, keepdims=True) * (1.0 / group_width)
            mamba_ref[:, left : left + group_width] = (
                value * lax.rsqrt(mean + EPSILON) * gain_ref[:, left : left + group_width]
            ).astype(BF16)

    @pl.when(has_right)
    def _():
        halo_copy.wait_send()
        own_k.wait_send()
        own_v.wait_send()
        for c in range(chunks):
            state_copy(c).wait_send()

    for s in range(1, reach):
        @pl.when((here >= s) & has_right)
        def _(s=s):
            for i in range(2):
                remote(
                    kv.at[s - 1, i], kv.at[s, i], kv_send.at[s, i], kv_recv.at[s, i]
                ).wait_send()


SUB = 128
EARLY = 2
ORDER = (
    ("l", 6, 7),
    ("e", 6, 7),
    ("l", 7, 8),
    ("e", 7, 8),
    ("l", 0, 6),
    ("u", 0, 1),
    ("o", 6, 8),
    ("k", 0, 1),
    ("t", 0, 1),
    ("q", 0, 4),
    ("x", 6, 8),
    ("p", 0, 1),
    ("w", 0, 1),
    ("i", 0, 4),
    ("p", 1, 2),
    ("i", 4, 8),
    ("p", 2, 3),
    ("r", 0, 1),
    ("a", 0, 3),
    ("p", 3, 4),
    ("a", 3, 6),
    ("p", 4, 5),
    ("a", 6, 8),
    ("p", 5, 6),
    ("y", 6, 7),
    ("f", 0, 1),
    ("r", 1, 2),
    ("f", 1, 2),
    ("r", 2, 3),
    ("f", 2, 3),
    ("r", 3, 4),
    ("f", 3, 4),
    ("n", 0, 1),
    ("y", 7, 8),
    ("r", 4, 5),
    ("f", 4, 5),
    ("r", 6, 7),
    ("g", 0, 8),
    ("f", 6, 7),
    ("r", 7, 8),
    ("f", 7, 8),
    ("r", 5, 6),
    ("f", 5, 6),
    ("n", 1, 2),
)


def packed_kernel(
    n,
    x_hbm, bc_hbm, z_hbm, dt_hbm, cxw_hbm, cxb_hbm, cbw_hbm, cbb_hbm,
    dtb_hbm, alog_hbm, skip_hbm, gain_hbm, q_hbm, k_hbm, v_hbm, lens_hbm,
    mamba_ref,
    attn_ref,
    halo_out,
    halo_in,
    kv,
    state_in,
    state_out,
    c_mine,
    c_next,
    c_ahead,
    ready,
    extra,
    weights,
    xf,
    bcf,
    xc,
    gated,
    gate_entry,
    small_send,
    small_recv,
    kv_send,
    kv_recv,
    st_send,
    st_recv,
    c_sem,
    extra_sem,
    fetch_sem,
    x_tail,
    x_ref, bc_ref, z_ref, dt_ref, cxw_ref, cxb_ref, cbw_ref, cbb_ref,
    dtb_ref, alog_ref, skip_ref, gain_ref, q_ref, k_ref, v_ref, lens_ref,
):
    here = lax.axis_index("seq")
    has_left = here > 0
    has_right = here < n - 1
    middle = has_left & has_right
    barrier = pltpu.get_barrier_semaphore()

    @pl.when(has_left)
    def _():
        pl.semaphore_signal(
            barrier, inc=1, device_id={"seq": here - 1}, device_id_type=pl.DeviceIdType.MESH
        )

    @pl.when(has_right)
    def _():
        pl.semaphore_signal(
            barrier, inc=1, device_id={"seq": here + 1}, device_id_type=pl.DeviceIdType.MESH
        )

    rows, width = x_ref.shape
    fetches = [
        pltpu.make_async_copy(source, target, fetch_sem.at[i])
        for i, (source, target) in enumerate(
            (
                (x_hbm.at[pl.ds(rows - 16, 16), :], x_tail),
                (bc_hbm, bc_ref),
                (lens_hbm, lens_ref),
                (dt_hbm, dt_ref),
                (dtb_hbm, dtb_ref),
                (alog_hbm, alog_ref),
                (skip_hbm, skip_ref),
                (cbw_hbm, cbw_ref),
                (cbb_hbm, cbb_ref),
                (cxw_hbm, cxw_ref),
                (cxb_hbm, cxb_ref),
                (x_hbm, x_ref),
                (z_hbm, z_ref),
                (k_hbm, k_ref),
                (v_hbm, v_ref),
                (q_hbm, q_ref),
                (gain_hbm, gain_ref),
            )
        )
    ]
    for fetch in fetches:
        fetch.start()
    bc_width = bc_ref.shape[1]
    heads = dt_ref.shape[0]
    groups = bc_width // (2 * STATE)
    chunks = width // CHUNK
    per = CHUNK // SUB
    group_width = width // groups
    taps = cxw_ref.shape[0]
    margin = taps - 1

    def remote(src, dst, send, recv, to=1):
        return pltpu.make_async_remote_copy(
            src_ref=src,
            dst_ref=dst,
            send_sem=send,
            recv_sem=recv,
            device_id={"seq": here + to},
            device_id_type=pl.DeviceIdType.MESH,
        )

    fetches[0].wait()
    fetches[1].wait()
    blocks = width // bc_width
    tail_x = x_tail[...].astype(F32)[16 - margin :]
    tail_bc = bc_ref[rows - 16 :, :].astype(F32)[16 - margin :]
    pieces = [tail_x[:, b * bc_width : (b + 1) * bc_width] for b in range(blocks)] + [tail_bc]
    pieces.append(jnp.zeros((16 - margin * (blocks + 1), bc_width), F32))
    halo_out[...] = jnp.concatenate(pieces, axis=0).astype(BF16)

    @pl.when(middle)
    def _():
        pl.semaphore_wait(barrier, 2)

    @pl.when(jnp.logical_not(middle))
    def _():
        pl.semaphore_wait(barrier, 1)

    halo_copy = remote(halo_out, halo_in, small_send, small_recv)
    own_k = remote(k_hbm, kv.at[0], kv_send.at[0], kv_recv.at[0])
    own_v = remote(v_hbm, kv.at[1], kv_send.at[1], kv_recv.at[1])
    c_back = remote(c_mine, c_next, c_sem.at[0], c_sem.at[1], -1)

    @pl.when(has_right)
    def _():
        halo_copy.start()
        own_k.start()

    @pl.when(middle)
    def _():
        own_v.start()

    for fetch in fetches[2:11]:
        fetch.wait()
    first = here * rows
    starts = []
    running_start = jnp.int32(0)
    for d in range(lens_ref.shape[0]):
        starts.append(running_start)
        running_start = running_start + lens_ref[d]

    def doc_of(positions):
        total = jnp.full(positions.shape, -1, jnp.int32)
        for start in starts:
            total = total + jnp.where(start <= positions, 1, 0)
        return total

    def doc_at(position):
        return doc_of(jnp.full((1, 128), position, jnp.int32))

    square = (rows, 128)
    pos_i = first + lax.broadcasted_iota(jnp.int32, square, 0)
    pos_j = first + lax.broadcasted_iota(jnp.int32, (rows, rows), 1)
    doc_i = doc_of(pos_i)
    doc_j = doc_of(pos_j)
    linked = (doc_i == doc_j) & (pos_i >= pos_j)
    before = doc_at(first - 1)
    last = doc_at(first + rows - 1)
    same = [
        jnp.where(doc_of(pos_i - (margin - lag)) == doc_i, 1.0, 0.0) for lag in range(margin)
    ]
    ahead = doc_of(pos_i + rows) == before
    spare = (doc_at(first + rows) == before) & jnp.logical_not(ahead)
    rows_came = doc_at(first - rows - 1) == doc_at(first)

    raw = dt_ref[...].T + dtb_ref[...]
    step = jnp.maximum(raw, 0.0) + jnp.log1p(jnp.exp(-jnp.abs(raw)))
    decay = step * (jnp.exp(alog_ref[...]) * (-LOG2E))
    order_i = lax.broadcasted_iota(jnp.int32, (rows, rows), 0)
    order_j = lax.broadcasted_iota(jnp.int32, (rows, rows), 1)
    unit = jnp.where(order_i == order_j, 1.0, 0.0)
    lower = jnp.where(order_i >= order_j, 1.0, 0.0)
    running = jnp.dot(lower, decay, precision=HIGHEST, preferred_element_type=F32)
    final = running[rows - 1 : rows]
    row_of = (running - jnp.log2(step)).T
    tail = jnp.where(
        (doc_i == last)[:, :heads], jnp.exp2(final - running) * step, 0.0
    )
    entry = jnp.where((doc_i == before)[:, :heads], jnp.exp2(running), 0.0)
    through = jnp.where((last == before)[:, :heads], jnp.exp2(final), 0.0)
    stack = jnp.concatenate(
        [
            tail,
            entry,
            jnp.broadcast_to(through, (8, heads)),
            jnp.broadcast_to(skip_ref[...], (8, heads)),
        ],
        axis=0,
    )
    high = stack.astype(BF16)
    low = (stack - high.astype(F32)).astype(BF16)

    @pl.when(has_left)
    def _():
        halo_copy.wait_recv()

    @pl.when(here == 0)
    def _():
        halo_in[...] = jnp.zeros_like(halo_in)
        state_in[...] = jnp.zeros_like(state_in)
        kv[...] = jnp.zeros_like(kv)

    @pl.when(here != 2)
    def _():
        extra[...] = jnp.zeros_like(extra)

    halo = halo_in[...].astype(F32)
    for b in range(blocks):
        xf[8 - margin : 8, b * bc_width : (b + 1) * bc_width] = halo[
            b * margin : (b + 1) * margin
        ]
    bcf[8 - margin : 8, :] = halo[blocks * margin : (blocks + 1) * margin]
    bcf[8:, :] = bc_ref[...].astype(F32)

    def conv(source, weight_ref, bias_ref, at, size):
        total = source[8 : 8 + rows, at : at + size] * weight_ref[margin : margin + 1, at : at + size]
        total = total + bias_ref[:, at : at + size]
        for lag in range(margin):
            moved = source[8 - margin + lag : 8 - margin + lag + rows, at : at + size]
            total = total + moved * weight_ref[lag : lag + 1, at : at + size] * wide(
                same[lag], size
            )
        return silu(total).astype(BF16)

    b_turned, c_groups, crossed, c_own = [], [], [], []
    for g in range(groups):
        b_here = conv(bcf, cbw_ref, cbb_ref, 2 * g * STATE, STATE)
        c_here = conv(bcf, cbw_ref, cbb_ref, (2 * g + 1) * STATE, STATE)
        b_turned.append(b_here.astype(F32).T.astype(BF16))
        c_mine[g] = c_here
        c_own.append(c_here)
        c_groups.append(jnp.where(rows_came, unit, c_here.astype(F32)).astype(BF16))
        crossed.append(lax.dot_general(c_here, b_here, NT, preferred_element_type=F32))

    @pl.when(here >= 2)
    def _():
        c_back.start()

    def state_copy(i):
        return remote(state_out.at[i], state_in.at[i], st_send.at[i], st_recv.at[i])

    kv_local = k_ref.shape[1] // ADIM
    lane_head = lax.broadcasted_iota(jnp.int32, (heads, CHUNK), 1) // HDIM
    head_row = lax.broadcasted_iota(jnp.int32, (heads, CHUNK), 0)
    per_chunk = CHUNK // HDIM
    low_half = lax.broadcasted_iota(jnp.int32, (rows, 128), 1) < HDIM
    carried = {}
    value_base = (chunks - EARLY) * per

    def make_local(c):
        at = c * CHUNK
        g = at // group_width
        xf[8:, at : at + CHUNK] = x_ref[:, at : at + CHUNK].astype(F32)
        x_here = conv(xf, cxw_ref, cxb_ref, at, CHUNK)
        xc[:, at : at + CHUNK] = x_here
        spread = jnp.where(head_row == lane_head + c * per_chunk, 1.0, 0.0).astype(BF16)
        expanded = dot(high, spread) + dot(low, spread)
        x32 = x_here.astype(F32)
        local = dot(b_turned[g], (x32 * expanded[:rows]).astype(BF16)).astype(BF16)
        gate_entry[:, at : at + CHUNK] = expanded[rows : 2 * rows]
        gated[:, at : at + CHUNK] = x32 * expanded[2 * rows + 8 : 2 * rows + 9]
        carried[c] = expanded[2 * rows : 2 * rows + 1]
        for i in range(per):
            state_out[c * per + i] = local[:, i * SUB : (i + 1) * SUB]

        if c < chunks - EARLY:
            first_send(c)

    def first_send(c):
        @pl.when(here == 0)
        def _():
            for i in range(per):
                state_copy(c * per + i).start()

    def extra_copy(c):
        i = c - (chunks - EARLY)
        return remote(
            state_out.at[pl.ds(c * per, per)],
            extra.at[pl.ds(i * per, per)],
            extra_sem.at[0, i],
            extra_sem.at[1, i],
        )

    def early_send(c):
        @pl.when(here == 1)
        def _():
            extra_copy(c).start()

    def share(c, i):
        return carried[c][:, i * SUB : (i + 1) * SUB]

    def early_pass(c):
        g = c * CHUNK // group_width

        @pl.when(here == 2)
        def _():
            extra_copy(c).wait_recv()
            for i in range(per):
                at = c * per + i
                early = extra[at - (chunks - EARLY) * per]
                state_out[at] = (ready[at] + dot(c_ahead[g], early) * share(c, i)).astype(BF16)
                state_copy(at).start()

    def late_pass(c):
        g = c * CHUNK // group_width

        @pl.when(here == 1)
        def _():
            if c == chunks - EARLY:
                own_v.wait_recv()
            extra_copy(c).wait_send()
            for i in range(per):
                at = c * per + i
                state_copy(at).wait_recv()
                sent = dot(c_ahead[g], state_in[at]) * share(c, i)
                if value_base <= at < value_base + kv_local:
                    col = (at - value_base) * ADIM
                    sent = jnp.where(spare, kv[1, :, col : col + ADIM].astype(F32), sent)
                state_out[at] = sent.astype(BF16)
                state_copy(at).start()

    def make_ready(cs):
        cs = list(cs)

        @pl.when(middle if cs[-1] < chunks - EARLY else here == 2)
        def _():
            for c in cs:
                g = c * CHUNK // group_width
                for i in range(per):
                    at = c * per + i
                    sent = dot(c_next[g], state_out[at])
                    for base, slot in ((0, 0), (value_base, 1)):
                        if base <= at < base + kv_local:
                            col = (at - base) * ADIM
                            far = kv[slot, :, col : col + ADIM].astype(F32)
                            sent = jnp.where(spare, far, sent)
                    ready[at] = sent

    def pass_on(c):
        g = c * CHUNK // group_width

        @pl.when(middle)
        def _():
            for i in range(per):
                at = c * per + i
                state_copy(at).wait_recv()
                state_out[at] = (
                    ready[at]
                    + dot(c_ahead[g], state_in[at]) * carried[c][:, i * SUB : (i + 1) * SUB]
                ).astype(BF16)
                state_copy(at).start()

    def arrive(c):
        @pl.when(here >= (2 if c >= chunks - EARLY else n - 1))
        def _():
            for i in range(per):
                state_copy(c * per + i).wait_recv()

    per_kv = q_ref.shape[1] // (ADIM * kv_local)
    scale = ADIM**-0.5 * LOG2E

    def permitted_keys():
        count = 3 * rows
        key_pos = first - 2 * rows + lax.broadcasted_iota(jnp.int32, (rows, count), 1)
        return (doc_of(key_pos) == wide(doc_i, count)) & (key_pos <= wide(pos_i, count))

    totals = []

    def weigh(head, permitted):
        g = head // per_kv
        cols = slice(g * ADIM, (g + 1) * ADIM)
        keys = jnp.concatenate([state_in[g], kv[0, :, cols], k_ref[:, cols]], axis=0)
        query = q_ref[:, head * ADIM : (head + 1) * ADIM]
        scores = lax.dot_general(query, keys, NT, preferred_element_type=F32)
        scores = jnp.where(permitted, scores, NEGATIVE)
        peak = jnp.max(scores, axis=1, keepdims=True)
        expo = jnp.exp2((scores - peak) * scale)
        totals.append(jnp.sum(expo, axis=1, keepdims=True))
        weights[head] = expo.astype(BF16)

    def gather(head):
        g = head // per_kv
        cols = slice(g * ADIM, (g + 1) * ADIM)
        values = jnp.concatenate(
            [state_in[value_base + g], kv[1, :, cols], v_ref[:, cols]], axis=0
        )
        summed = dot(weights[head], values)
        attn_ref[:, head * ADIM : (head + 1) * ADIM] = (summed / totals[head]).astype(BF16)

    def inside(c):
        at = c * CHUNK
        g = at // group_width
        gate = silu(z_ref[:, at : at + CHUNK].astype(F32))
        for pair in range(CHUNK // 128):
            col = at + pair * 128
            head = col // HDIM
            parts = []
            for h in (head, head + 1):
                exponent = running[:, h : h + 1] - row_of[h : h + 1, :]
                parts.append(
                    (jnp.exp2(jnp.where(linked, exponent, NEGATIVE)) * crossed[g]).astype(BF16)
                )
            x_pair = xc[:, col : col + 128]
            zero = jnp.zeros_like(x_pair)
            stacked = jnp.concatenate(
                [jnp.where(low_half, x_pair, zero), jnp.where(low_half, zero, x_pair)], axis=0
            )
            within = dot(jnp.concatenate(parts, axis=1), stacked)
            gated[:, col : col + 128] = (gated[:, col : col + 128] + within) * gate[
                :, pair * 128 : (pair + 1) * 128
            ]
        gate_entry[:, at : at + CHUNK] = gate_entry[:, at : at + CHUNK] * gate

    squares = {}

    def finish(c):
        at = c * CHUNK
        g = at // group_width
        came = jnp.concatenate([state_in[c * per + i] for i in range(per)], axis=1)
        if c >= chunks - EARLY:
            base = (c - (chunks - EARLY)) * per
            local = jnp.concatenate([extra[base + i] for i in range(per)], axis=1)
            theirs = jnp.where(here == 2, unit, c_groups[g].astype(F32)).astype(BF16)
            product = dot(theirs, came) + dot(c_own[g], local)
        else:
            product = dot(c_groups[g], came)
        value = gated[:, at : at + CHUNK] + product * gate_entry[:, at : at + CHUNK]
        gated[:, at : at + CHUNK] = value
        for i in range(CHUNK // 128):
            piece = value[:, i * 128 : (i + 1) * 128]
            squares[g] = squares[g] + piece * piece if g in squares else piece * piece

    def normalize(g):
        left = g * group_width
        mean = jnp.sum(squares[g], axis=1, keepdims=True) * (1.0 / group_width)
        mamba_ref[:, left : left + group_width] = (
            gated[:, left : left + group_width]
            * lax.rsqrt(mean + EPSILON)
            * gain_ref[:, left : left + group_width]
        ).astype(BF16)

    fetches[11].wait()

    def take_keys():
        @pl.when(has_left)
        def _():
            own_k.wait_recv()

        @pl.when(here >= 2)
        def _():
            own_v.wait_recv()

    def send_values():
        @pl.when(here == 0)
        def _():
            own_v.start()

    def take_turned():
        @pl.when(middle)
        def _():
            c_back.wait_recv()
            for g in range(groups):
                theirs = c_next[g].astype(F32)
                c_ahead[g] = jnp.where(ahead, theirs, 0.0).astype(BF16)
                c_next[g] = jnp.where(ahead, theirs, unit).astype(BF16)

    def take_rest():
        for fetch in fetches[12:]:
            fetch.wait()

    held = []

    def attend_next(head):
        if not held:
            held.append(permitted_keys())
        weigh(head, held[0])

    steps = {
        "l": make_local, "q": lambda c: make_ready(range(2 * c, 2 * c + 2)), "g": gather,
        "u": lambda _: send_values(), "p": pass_on, "n": normalize,
        "e": early_send, "x": early_pass, "y": late_pass, "o": first_send, "r": arrive, "i": inside, "a": attend_next, "f": finish,
        "k": lambda _: take_keys(), "t": lambda _: take_turned(), "w": lambda _: take_rest(),
    }
    for name, low_end, high_end in ORDER:
        for at in range(low_end, high_end):
            steps[name](at)

    @pl.when(has_right)
    def _():
        halo_copy.wait_send()
        own_k.wait_send()
        own_v.wait_send()
        for i in range(chunks * per):
            state_copy(i).wait_send()

    @pl.when(here >= 2)
    def _():
        c_back.wait_send()


def write_out(mamba_ref, attn_ref, mamba_hbm, attn_hbm, sems):
    copies = [
        pltpu.make_async_copy(mamba_ref, mamba_hbm, sems.at[0]),
        pltpu.make_async_copy(attn_ref, attn_hbm, sems.at[1]),
    ]
    for copy in copies:
        copy.start()
    for copy in copies:
        copy.wait()


def shards(n, *args):
    (
        x_raw, bc_raw, z_gate, dt_raw, cxw, cxb, cbw, cbb, dtb, a_log, skip_d, gain, queries, keys,
        values, doc_lens,
    ) = args
    operands = (
        x_raw, bc_raw, z_gate, dt_raw.T, cxw, cxb[None], cbw, cbb[None], dtb[None], a_log[None],
        skip_d[None], gain[None], queries, keys, values, doc_lens,
    )
    rows, width = x_raw.shape
    bc_width = bc_raw.shape[1]
    chunks = width // CHUNK
    reach = max(1, n // 2)
    vmem = pl.BlockSpec(memory_space=pltpu.VMEM)
    dma = pltpu.SemaphoreType.DMA
    if n == 4 and rows == STATE and keys.shape[1] == CHUNK and width == 8 * CHUNK and (
        queries.shape[1] == 8 * ADIM
    ):
        subs = width // SUB
        state = pltpu.VMEM((subs, STATE, SUB), BF16)
        turned = pltpu.VMEM((bc_width // (2 * STATE), rows, STATE), BF16)
        body = functools.partial(packed_kernel, n)
        ready = pltpu.VMEM((subs, rows, SUB), F32)
        buffers = [pltpu.VMEM((2,) + keys.shape, BF16), state, state, turned, turned, turned, ready]
        buffers.append(pltpu.VMEM((EARLY * CHUNK // SUB, STATE, SUB), BF16))
        buffers.append(pltpu.VMEM((queries.shape[1] // ADIM, rows, 3 * rows), BF16))
        sems = [dma((2,)), dma((2,)), dma((subs,)), dma((subs,)), dma((2,)), dma((2, EARLY))]
    else:
        state = pltpu.VMEM((chunks, STATE, CHUNK), BF16)
        body = functools.partial(relay_kernel, n, reach)
        buffers = [pltpu.VMEM((reach, 2) + keys.shape, BF16), state, state]
        sems = [dma((reach, 2)), dma((reach, 2)), dma((chunks,)), dma((chunks,))]
    results = pl.pallas_call(
        body,
        out_shape=(pltpu.VMEM((rows, width), BF16), pltpu.VMEM(queries.shape, BF16)),
        in_specs=[pl.BlockSpec(memory_space=pltpu.HBM)] * 16,
        out_specs=(vmem, vmem),
        scratch_shapes=[
            pltpu.VMEM((16, bc_width), BF16),
            pltpu.VMEM((16, bc_width), BF16),
        ]
        + buffers
        + [
            pltpu.VMEM((rows + 8, width), F32),
            pltpu.VMEM((rows + 8, bc_width), F32),
            pltpu.VMEM((rows, width), BF16),
            pltpu.VMEM((rows, width), F32),
            pltpu.VMEM((rows, width), F32),
            dma,
            dma,
        ]
        + sems
        + [dma((17,)), pltpu.VMEM((16, width), BF16)]
        + [pltpu.VMEM(a.shape, a.dtype) for a in operands[:-1]]
        + [pltpu.SMEM(doc_lens.shape, jnp.int32)],
        compiler_params=pltpu.CompilerParams(
            collective_id=0, has_side_effects=True, vmem_limit_bytes=60 * 1024 * 1024
        ),
    )(*operands)
    hbm = pl.BlockSpec(memory_space=pltpu.HBM)
    return pl.pallas_call(
        write_out,
        out_shape=(
            jax.ShapeDtypeStruct((rows, width), BF16),
            jax.ShapeDtypeStruct(queries.shape, BF16),
        ),
        in_specs=[vmem, vmem],
        out_specs=(hbm, hbm),
        scratch_shapes=[dma((2,))],
    )(*[pltpu.with_memory_space_constraint(r, pltpu.VMEM) for r in results])


def solution(mesh):
    both = P(("groups", "seq"), "dp")
    placed = (
        both, both, both, both, P(None, "dp"), P("dp"), P(None, "dp"), P("dp"), P("dp"), P("dp"),
        P("dp"), P("dp"), both, both, both, P("groups"),
    )
    return jax.shard_map(
        functools.partial(shards, mesh.shape["seq"]),
        mesh=mesh,
        in_specs=placed,
        out_specs=(both, both),
        check_vma=False,
    )
```

```python
import functools
import jax
import jax.numpy as jnp
from jax import lax
from jax.experimental import pallas as pl
from jax.experimental.pallas import tpu as pltpu
from jax.sharding import PartitionSpec as P

HDIM = 64
STATE = 128
QHEADS = 32
KVHEADS = 8
ADIM = 128
EPSILON = 1e-05
NEGATIVE = -1e30
LOG2E = 1.4426950408889634
HIGHEST = lax.Precision.HIGHEST
F32 = jnp.float32
BF16 = jnp.bfloat16
CHUNK = 256
NT = (((1,), (1,)), ((), ()))


def silu(value):
    half = 0.5 * value
    return half + half * jnp.tanh(half)


def dot(a, b):
    return jnp.dot(a, b, preferred_element_type=F32)


def wide(tile, width):
    return jnp.concatenate([tile] * (width // tile.shape[1]), axis=1)


def relay_kernel(
    n,
    reach,
    x_hbm, bc_hbm, z_hbm, dt_hbm, cxw_hbm, cxb_hbm, cbw_hbm, cbb_hbm,
    dtb_hbm, alog_hbm, skip_hbm, gain_hbm, q_hbm, k_hbm, v_hbm, lens_hbm,
    mamba_ref,
    attn_ref,
    halo_out,
    halo_in,
    kv,
    state_in,
    state_out,
    xf,
    bcf,
    xc,
    gated,
    gate_entry,
    small_send,
    small_recv,
    kv_send,
    kv_recv,
    st_send,
    st_recv,
    fetch_sem,
    x_tail,
    x_ref, bc_ref, z_ref, dt_ref, cxw_ref, cxb_ref, cbw_ref, cbb_ref,
    dtb_ref, alog_ref, skip_ref, gain_ref, q_ref, k_ref, v_ref, lens_ref,
):
    here = lax.axis_index("seq")
    rows, width = x_ref.shape
    fetches = [
        pltpu.make_async_copy(source, target, fetch_sem.at[i])
        for i, (source, target) in enumerate(
            (
                (x_hbm.at[pl.ds(rows - 16, 16), :], x_tail),
                (bc_hbm, bc_ref),
                (lens_hbm, lens_ref),
                (dt_hbm, dt_ref),
                (dtb_hbm, dtb_ref),
                (alog_hbm, alog_ref),
                (skip_hbm, skip_ref),
                (cbw_hbm, cbw_ref),
                (cbb_hbm, cbb_ref),
                (cxw_hbm, cxw_ref),
                (cxb_hbm, cxb_ref),
                (x_hbm, x_ref),
                (z_hbm, z_ref),
                (k_hbm, k_ref),
                (v_hbm, v_ref),
                (q_hbm, q_ref),
                (gain_hbm, gain_ref),
            )
        )
    ]
    for fetch in fetches:
        fetch.start()
    bc_width = bc_ref.shape[1]
    heads = dt_ref.shape[0]
    groups = bc_width // (2 * STATE)
    chunks = width // CHUNK
    group_width = width // groups
    taps = cxw_ref.shape[0]
    margin = taps - 1
    has_left = here > 0
    has_right = here < n - 1
    right = {"seq": here + 1}

    def remote(src, dst, send, recv):
        return pltpu.make_async_remote_copy(
            src_ref=src,
            dst_ref=dst,
            send_sem=send,
            recv_sem=recv,
            device_id=right,
            device_id_type=pl.DeviceIdType.MESH,
        )

    barrier = pltpu.get_barrier_semaphore()

    @pl.when(has_left)
    def _():
        pl.semaphore_signal(
            barrier, inc=1, device_id={"seq": here - 1}, device_id_type=pl.DeviceIdType.MESH
        )

    @pl.when(has_right)
    def _():
        pl.semaphore_signal(
            barrier, inc=1, device_id={"seq": here + 1}, device_id_type=pl.DeviceIdType.MESH
        )

    fetches[0].wait()
    fetches[1].wait()
    blocks = width // bc_width
    tail_x = x_tail[...].astype(F32)[16 - margin :]
    tail_bc = bc_ref[rows - 16 :, :].astype(F32)[16 - margin :]
    pieces = [tail_x[:, b * bc_width : (b + 1) * bc_width] for b in range(blocks)] + [tail_bc]
    pieces.append(jnp.zeros((16 - margin * (blocks + 1), bc_width), F32))
    halo_out[...] = jnp.concatenate(pieces, axis=0).astype(BF16)

    @pl.when(has_left & has_right)
    def _():
        pl.semaphore_wait(barrier, 2)

    @pl.when(jnp.logical_not(has_left & has_right))
    def _():
        pl.semaphore_wait(barrier, 1)

    halo_copy = remote(halo_out, halo_in, small_send, small_recv)
    own_k = remote(k_hbm, kv.at[0, 0], kv_send.at[0, 0], kv_recv.at[0, 0])
    own_v = remote(v_hbm, kv.at[0, 1], kv_send.at[0, 1], kv_recv.at[0, 1])

    @pl.when(has_right)
    def _():
        halo_copy.start()
        own_k.start()
        own_v.start()

    for fetch in fetches[2:11]:
        fetch.wait()
    first = here * rows
    starts = []
    running_start = jnp.int32(0)
    for d in range(lens_ref.shape[0]):
        starts.append(running_start)
        running_start = running_start + lens_ref[d]

    def doc_of(positions):
        total = jnp.full(positions.shape, -1, jnp.int32)
        for start in starts:
            total = total + jnp.where(start <= positions, 1, 0)
        return total

    square = (rows, 128)
    pos_i = first + lax.broadcasted_iota(jnp.int32, square, 0)
    pos_j = first + lax.broadcasted_iota(jnp.int32, (rows, rows), 1)
    doc_i = doc_of(pos_i)
    doc_j = doc_of(pos_j)
    linked = (doc_i == doc_j) & (pos_i >= pos_j)
    before = doc_of(jnp.full((1, 128), first - 1, jnp.int32))
    last = doc_of(jnp.full((1, 128), first + rows - 1, jnp.int32))
    same = [
        jnp.where(doc_of(pos_i - (margin - lag)) == doc_i, 1.0, 0.0) for lag in range(margin)
    ]

    raw = dt_ref[...].T + dtb_ref[...]
    step = jnp.maximum(raw, 0.0) + jnp.log1p(jnp.exp(-jnp.abs(raw)))
    decay = step * (jnp.exp(alog_ref[...]) * (-LOG2E))
    order_i = lax.broadcasted_iota(jnp.int32, (rows, rows), 0)
    order_j = lax.broadcasted_iota(jnp.int32, (rows, rows), 1)
    lower = jnp.where(order_i >= order_j, 1.0, 0.0)
    running = jnp.dot(lower, decay, precision=HIGHEST, preferred_element_type=F32)
    final = running[rows - 1 : rows]
    row_of = (running - jnp.log2(step)).T
    tail = jnp.where(
        (doc_i == last)[:, :heads], jnp.exp2(final - running) * step, 0.0
    )
    entry = jnp.where((doc_i == before)[:, :heads], jnp.exp2(running), 0.0)
    through = jnp.where((last == before)[:, :heads], jnp.exp2(final), 0.0)
    stack = jnp.concatenate(
        [
            tail,
            entry,
            jnp.broadcast_to(through, (8, heads)),
            jnp.broadcast_to(skip_ref[...], (8, heads)),
        ],
        axis=0,
    )
    high = stack.astype(BF16)
    low = (stack - high.astype(F32)).astype(BF16)

    @pl.when(has_left)
    def _():
        halo_copy.wait_recv()

    @pl.when(here == 0)
    def _():
        halo_in[...] = jnp.zeros_like(halo_in)
        state_in[...] = jnp.zeros_like(state_in)

    for s in range(reach):
        @pl.when(here < s + 1)
        def _(s=s):
            kv[s] = jnp.zeros_like(kv[s])

    halo = halo_in[...].astype(F32)
    for b in range(blocks):
        xf[8 - margin : 8, b * bc_width : (b + 1) * bc_width] = halo[
            b * margin : (b + 1) * margin
        ]
    bcf[8 - margin : 8, :] = halo[blocks * margin : (blocks + 1) * margin]
    bcf[8:, :] = bc_ref[...].astype(F32)

    def conv(source, weight_ref, bias_ref, at, size):
        total = source[8 : 8 + rows, at : at + size] * weight_ref[margin : margin + 1, at : at + size]
        total = total + bias_ref[:, at : at + size]
        for lag in range(margin):
            moved = source[8 - margin + lag : 8 - margin + lag + rows, at : at + size]
            total = total + moved * weight_ref[lag : lag + 1, at : at + size] * wide(
                same[lag], size
            )
        return silu(total).astype(BF16)

    b_turned, c_groups, crossed = [], [], []
    for g in range(groups):
        b_here = conv(bcf, cbw_ref, cbb_ref, 2 * g * STATE, STATE)
        c_here = conv(bcf, cbw_ref, cbb_ref, (2 * g + 1) * STATE, STATE)
        b_turned.append(b_here.astype(F32).T.astype(BF16))
        c_groups.append(c_here)
        crossed.append(lax.dot_general(c_here, b_here, NT, preferred_element_type=F32))

    def state_copy(c):
        return remote(state_out.at[c], state_in.at[c], st_send.at[c], st_recv.at[c])

    lane_head = lax.broadcasted_iota(jnp.int32, (heads, CHUNK), 1) // HDIM
    head_row = lax.broadcasted_iota(jnp.int32, (heads, CHUNK), 0)
    per_chunk = CHUNK // HDIM
    low_half = lax.broadcasted_iota(jnp.int32, (rows, 128), 1) < HDIM

    fetches[11].wait()
    carried = []
    for c in range(chunks):
        at = c * CHUNK
        g = at // group_width
        xf[8:, at : at + CHUNK] = x_ref[:, at : at + CHUNK].astype(F32)
        x_here = conv(xf, cxw_ref, cxb_ref, at, CHUNK)
        xc[:, at : at + CHUNK] = x_here
        spread = jnp.where(head_row == lane_head + c * per_chunk, 1.0, 0.0).astype(BF16)
        expanded = dot(high, spread) + dot(low, spread)
        x32 = x_here.astype(F32)
        local = dot(b_turned[g], (x32 * expanded[:rows]).astype(BF16))
        gate_entry[:, at : at + CHUNK] = expanded[rows : 2 * rows]
        gated[:, at : at + CHUNK] = x32 * expanded[2 * rows + 8 : 2 * rows + 9]
        carried.append(expanded[2 * rows : 2 * rows + 1])
        state_out[c] = local.astype(BF16)

        @pl.when(here == 0)
        def _(c=c):
            state_copy(c).start()

    for s in range(1, reach):
        @pl.when(here >= s)
        def _(s=s):
            for i in range(2):
                remote(
                    kv.at[s - 1, i], kv.at[s - 1, i], kv_send.at[s - 1, i], kv_recv.at[s - 1, i]
                ).wait_recv()

        @pl.when((here >= s) & has_right)
        def _(s=s):
            for i in range(2):
                remote(
                    kv.at[s - 1, i], kv.at[s, i], kv_send.at[s, i], kv_recv.at[s, i]
                ).start()

    for fetch in fetches[12:]:
        fetch.wait()

    kv_local = k_ref.shape[1] // ADIM
    share = q_ref.shape[1] // (ADIM * kv_local)
    scale = ADIM**-0.5 * LOG2E
    key_count = (reach + 1) * rows
    key_pos = (
        first - reach * rows + lax.broadcasted_iota(jnp.int32, (rows, key_count), 1)
    )
    key_docs = doc_of(key_pos)
    permitted = (key_docs == wide(doc_i, key_count)) & (key_pos <= wide(pos_i, key_count))

    def attend(head):
        g = head // share
        cols = slice(g * ADIM, (g + 1) * ADIM)
        keys = jnp.concatenate(
            [kv[s, 0, :, cols] for s in reversed(range(reach))] + [k_ref[:, cols]], axis=0
        )
        values = jnp.concatenate(
            [kv[s, 1, :, cols] for s in reversed(range(reach))] + [v_ref[:, cols]], axis=0
        )
        query = q_ref[:, head * ADIM : (head + 1) * ADIM]
        scores = lax.dot_general(query, keys, NT, preferred_element_type=F32)
        scores = jnp.where(permitted, scores, NEGATIVE)
        peak = jnp.max(scores, axis=1, keepdims=True)
        expo = jnp.exp2((scores - peak) * scale)
        total = jnp.sum(expo, axis=1, keepdims=True)
        summed = dot(expo.astype(BF16), values)
        attn_ref[:, head * ADIM : (head + 1) * ADIM] = (summed / total).astype(BF16)

    q_heads = kv_local * share
    early = chunks // 4
    for c in range(chunks):
        at = c * CHUNK
        g = at // group_width
        gate = silu(z_ref[:, at : at + CHUNK].astype(F32))
        for pair in range(CHUNK // 128):
            col = at + pair * 128
            head = col // HDIM
            parts = []
            for h in (head, head + 1):
                exponent = running[:, h : h + 1] - row_of[h : h + 1, :]
                parts.append(
                    (jnp.exp2(jnp.where(linked, exponent, NEGATIVE)) * crossed[g]).astype(BF16)
                )
            x_pair = xc[:, col : col + 128]
            zero = jnp.zeros_like(x_pair)
            stacked = jnp.concatenate(
                [jnp.where(low_half, x_pair, zero), jnp.where(low_half, zero, x_pair)], axis=0
            )
            inside = dot(jnp.concatenate(parts, axis=1), stacked)
            gated[:, col : col + 128] = (gated[:, col : col + 128] + inside) * gate[
                :, pair * 128 : (pair + 1) * 128
            ]
        gate_entry[:, at : at + CHUNK] = gate_entry[:, at : at + CHUNK] * gate

        @pl.when(has_left)
        def _(c=c):
            state_copy(c).wait_recv()

        @pl.when(has_left & has_right)
        def _(c=c):
            state_out[c] = (
                state_out[c].astype(F32) + state_in[c].astype(F32) * carried[c]
            ).astype(BF16)
            state_copy(c).start()

        if c == early:
            @pl.when(here >= reach)
            def _():
                for i in range(2):
                    remote(
                        kv.at[reach - 1, i],
                        kv.at[reach - 1, i],
                        kv_send.at[reach - 1, i],
                        kv_recv.at[reach - 1, i],
                    ).wait_recv()

        if early <= c < chunks - 1:
            span = chunks - early - 1
            for head in range((c - early) * q_heads // span, (c - early + 1) * q_heads // span):
                attend(head)

        gated[:, at : at + CHUNK] = (
            gated[:, at : at + CHUNK]
            + dot(c_groups[g], state_in[c]) * gate_entry[:, at : at + CHUNK]
        )
        if (at + CHUNK) % group_width == 0:
            left = at + CHUNK - group_width
            value = gated[:, left : left + group_width]
            mean = jnp.sum(value * value, axis=1, keepdims=True) * (1.0 / group_width)
            mamba_ref[:, left : left + group_width] = (
                value * lax.rsqrt(mean + EPSILON) * gain_ref[:, left : left + group_width]
            ).astype(BF16)

    @pl.when(has_right)
    def _():
        halo_copy.wait_send()
        own_k.wait_send()
        own_v.wait_send()
        for c in range(chunks):
            state_copy(c).wait_send()

    for s in range(1, reach):
        @pl.when((here >= s) & has_right)
        def _(s=s):
            for i in range(2):
                remote(
                    kv.at[s - 1, i], kv.at[s, i], kv_send.at[s, i], kv_recv.at[s, i]
                ).wait_send()


SUB = 128
EARLY = 2
ORDER = (
    ("l", 6, 7),
    ("e", 6, 7),
    ("l", 7, 8),
    ("e", 7, 8),
    ("l", 0, 6),
    ("u", 0, 1),
    ("o", 6, 8),
    ("k", 0, 1),
    ("t", 0, 1),
    ("q", 0, 4),
    ("x", 6, 8),
    ("p", 0, 1),
    ("w", 0, 1),
    ("i", 0, 4),
    ("p", 1, 2),
    ("i", 4, 8),
    ("p", 2, 3),
    ("r", 0, 1),
    ("a", 0, 3),
    ("p", 3, 4),
    ("a", 3, 6),
    ("p", 4, 6),
    ("a", 6, 8),
    ("y", 6, 7),
    ("f", 0, 1),
    ("r", 1, 2),
    ("f", 1, 2),
    ("r", 2, 3),
    ("f", 2, 3),
    ("r", 3, 4),
    ("f", 3, 4),
    ("n", 0, 1),
    ("y", 7, 8),
    ("r", 4, 5),
    ("f", 4, 5),
    ("r", 6, 7),
    ("g", 0, 8),
    ("f", 6, 7),
    ("r", 7, 8),
    ("f", 7, 8),
    ("r", 5, 6),
    ("f", 5, 6),
    ("n", 1, 2),
)


def packed_kernel(
    n,
    x_hbm, bc_hbm, z_hbm, dt_hbm, cxw_hbm, cxb_hbm, cbw_hbm, cbb_hbm,
    dtb_hbm, alog_hbm, skip_hbm, gain_hbm, q_hbm, k_hbm, v_hbm, lens_hbm,
    mamba_ref,
    attn_ref,
    halo_out,
    halo_in,
    kv,
    state_in,
    state_out,
    c_mine,
    c_next,
    c_ahead,
    ready,
    extra,
    weights,
    xf,
    bcf,
    xc,
    gated,
    gate_entry,
    small_send,
    small_recv,
    kv_send,
    kv_recv,
    st_send,
    st_recv,
    c_sem,
    extra_sem,
    fetch_sem,
    x_tail,
    x_ref, bc_ref, z_ref, dt_ref, cxw_ref, cxb_ref, cbw_ref, cbb_ref,
    dtb_ref, alog_ref, skip_ref, gain_ref, q_ref, k_ref, v_ref, lens_ref,
):
    here = lax.axis_index("seq")
    has_left = here > 0
    has_right = here < n - 1
    middle = has_left & has_right
    barrier = pltpu.get_barrier_semaphore()

    @pl.when(has_left)
    def _():
        pl.semaphore_signal(
            barrier, inc=1, device_id={"seq": here - 1}, device_id_type=pl.DeviceIdType.MESH
        )

    @pl.when(has_right)
    def _():
        pl.semaphore_signal(
            barrier, inc=1, device_id={"seq": here + 1}, device_id_type=pl.DeviceIdType.MESH
        )

    rows, width = x_ref.shape
    fetches = [
        pltpu.make_async_copy(source, target, fetch_sem.at[i])
        for i, (source, target) in enumerate(
            (
                (x_hbm.at[pl.ds(rows - 16, 16), :], x_tail),
                (bc_hbm, bc_ref),
                (lens_hbm, lens_ref),
                (dt_hbm, dt_ref),
                (dtb_hbm, dtb_ref),
                (alog_hbm, alog_ref),
                (skip_hbm, skip_ref),
                (cbw_hbm, cbw_ref),
                (cbb_hbm, cbb_ref),
                (cxw_hbm, cxw_ref),
                (cxb_hbm, cxb_ref),
                (x_hbm, x_ref),
                (z_hbm, z_ref),
                (k_hbm, k_ref),
                (v_hbm, v_ref),
                (q_hbm, q_ref),
                (gain_hbm, gain_ref),
            )
        )
    ]
    for fetch in fetches:
        fetch.start()
    bc_width = bc_ref.shape[1]
    heads = dt_ref.shape[0]
    groups = bc_width // (2 * STATE)
    chunks = width // CHUNK
    per = CHUNK // SUB
    group_width = width // groups
    taps = cxw_ref.shape[0]
    margin = taps - 1

    def remote(src, dst, send, recv, to=1):
        return pltpu.make_async_remote_copy(
            src_ref=src,
            dst_ref=dst,
            send_sem=send,
            recv_sem=recv,
            device_id={"seq": here + to},
            device_id_type=pl.DeviceIdType.MESH,
        )

    fetches[0].wait()
    fetches[1].wait()
    blocks = width // bc_width
    tail_x = x_tail[...].astype(F32)[16 - margin :]
    tail_bc = bc_ref[rows - 16 :, :].astype(F32)[16 - margin :]
    pieces = [tail_x[:, b * bc_width : (b + 1) * bc_width] for b in range(blocks)] + [tail_bc]
    pieces.append(jnp.zeros((16 - margin * (blocks + 1), bc_width), F32))
    halo_out[...] = jnp.concatenate(pieces, axis=0).astype(BF16)

    @pl.when(middle)
    def _():
        pl.semaphore_wait(barrier, 2)

    @pl.when(jnp.logical_not(middle))
    def _():
        pl.semaphore_wait(barrier, 1)

    halo_copy = remote(halo_out, halo_in, small_send, small_recv)
    own_k = remote(k_hbm, kv.at[0], kv_send.at[0], kv_recv.at[0])
    own_v = remote(v_hbm, kv.at[1], kv_send.at[1], kv_recv.at[1])
    c_back = remote(c_mine, c_next, c_sem.at[0], c_sem.at[1], -1)

    @pl.when(has_right)
    def _():
        halo_copy.start()
        own_k.start()

    @pl.when(middle)
    def _():
        own_v.start()

    for fetch in fetches[2:11]:
        fetch.wait()
    first = here * rows
    starts = []
    running_start = jnp.int32(0)
    for d in range(lens_ref.shape[0]):
        starts.append(running_start)
        running_start = running_start + lens_ref[d]

    def doc_of(positions):
        total = jnp.full(positions.shape, -1, jnp.int32)
        for start in starts:
            total = total + jnp.where(start <= positions, 1, 0)
        return total

    def doc_at(position):
        return doc_of(jnp.full((1, 128), position, jnp.int32))

    square = (rows, 128)
    pos_i = first + lax.broadcasted_iota(jnp.int32, square, 0)
    pos_j = first + lax.broadcasted_iota(jnp.int32, (rows, rows), 1)
    doc_i = doc_of(pos_i)
    doc_j = doc_of(pos_j)
    linked = (doc_i == doc_j) & (pos_i >= pos_j)
    before = doc_at(first - 1)
    last = doc_at(first + rows - 1)
    same = [
        jnp.where(doc_of(pos_i - (margin - lag)) == doc_i, 1.0, 0.0) for lag in range(margin)
    ]
    ahead = doc_of(pos_i + rows) == before
    spare = (doc_at(first + rows) == before) & jnp.logical_not(ahead)
    rows_came = doc_at(first - rows - 1) == doc_at(first)

    raw = dt_ref[...].T + dtb_ref[...]
    step = jnp.maximum(raw, 0.0) + jnp.log1p(jnp.exp(-jnp.abs(raw)))
    decay = step * (jnp.exp(alog_ref[...]) * (-LOG2E))
    order_i = lax.broadcasted_iota(jnp.int32, (rows, rows), 0)
    order_j = lax.broadcasted_iota(jnp.int32, (rows, rows), 1)
    unit = jnp.where(order_i == order_j, 1.0, 0.0)
    lower = jnp.where(order_i >= order_j, 1.0, 0.0)
    running = jnp.dot(lower, decay, precision=HIGHEST, preferred_element_type=F32)
    final = running[rows - 1 : rows]
    row_of = (running - jnp.log2(step)).T
    tail = jnp.where(
        (doc_i == last)[:, :heads], jnp.exp2(final - running) * step, 0.0
    )
    entry = jnp.where((doc_i == before)[:, :heads], jnp.exp2(running), 0.0)
    through = jnp.where((last == before)[:, :heads], jnp.exp2(final), 0.0)
    stack = jnp.concatenate(
        [
            tail,
            entry,
            jnp.broadcast_to(through, (8, heads)),
            jnp.broadcast_to(skip_ref[...], (8, heads)),
        ],
        axis=0,
    )
    high = stack.astype(BF16)
    low = (stack - high.astype(F32)).astype(BF16)

    @pl.when(has_left)
    def _():
        halo_copy.wait_recv()

    @pl.when(here == 0)
    def _():
        halo_in[...] = jnp.zeros_like(halo_in)
        state_in[...] = jnp.zeros_like(state_in)
        kv[...] = jnp.zeros_like(kv)

    @pl.when(here != 2)
    def _():
        extra[...] = jnp.zeros_like(extra)

    halo = halo_in[...].astype(F32)
    for b in range(blocks):
        xf[8 - margin : 8, b * bc_width : (b + 1) * bc_width] = halo[
            b * margin : (b + 1) * margin
        ]
    bcf[8 - margin : 8, :] = halo[blocks * margin : (blocks + 1) * margin]
    bcf[8:, :] = bc_ref[...].astype(F32)

    def conv(source, weight_ref, bias_ref, at, size):
        total = source[8 : 8 + rows, at : at + size] * weight_ref[margin : margin + 1, at : at + size]
        total = total + bias_ref[:, at : at + size]
        for lag in range(margin):
            moved = source[8 - margin + lag : 8 - margin + lag + rows, at : at + size]
            total = total + moved * weight_ref[lag : lag + 1, at : at + size] * wide(
                same[lag], size
            )
        return silu(total).astype(BF16)

    b_turned, c_groups, crossed, c_own = [], [], [], []
    for g in range(groups):
        b_here = conv(bcf, cbw_ref, cbb_ref, 2 * g * STATE, STATE)
        c_here = conv(bcf, cbw_ref, cbb_ref, (2 * g + 1) * STATE, STATE)
        b_turned.append(b_here.astype(F32).T.astype(BF16))
        c_mine[g] = c_here
        c_own.append(c_here)
        c_groups.append(jnp.where(rows_came, unit, c_here.astype(F32)).astype(BF16))
        crossed.append(lax.dot_general(c_here, b_here, NT, preferred_element_type=F32))

    @pl.when(here >= 2)
    def _():
        c_back.start()

    def state_copy(i):
        return remote(state_out.at[i], state_in.at[i], st_send.at[i], st_recv.at[i])

    kv_local = k_ref.shape[1] // ADIM
    lane_head = lax.broadcasted_iota(jnp.int32, (heads, CHUNK), 1) // HDIM
    head_row = lax.broadcasted_iota(jnp.int32, (heads, CHUNK), 0)
    per_chunk = CHUNK // HDIM
    low_half = lax.broadcasted_iota(jnp.int32, (rows, 128), 1) < HDIM
    carried = {}
    value_base = (chunks - EARLY) * per

    def make_local(c):
        at = c * CHUNK
        g = at // group_width
        xf[8:, at : at + CHUNK] = x_ref[:, at : at + CHUNK].astype(F32)
        x_here = conv(xf, cxw_ref, cxb_ref, at, CHUNK)
        xc[:, at : at + CHUNK] = x_here
        spread = jnp.where(head_row == lane_head + c * per_chunk, 1.0, 0.0).astype(BF16)
        expanded = dot(high, spread) + dot(low, spread)
        x32 = x_here.astype(F32)
        local = dot(b_turned[g], (x32 * expanded[:rows]).astype(BF16)).astype(BF16)
        gate_entry[:, at : at + CHUNK] = expanded[rows : 2 * rows]
        gated[:, at : at + CHUNK] = x32 * expanded[2 * rows + 8 : 2 * rows + 9]
        carried[c] = expanded[2 * rows : 2 * rows + 1]
        for i in range(per):
            state_out[c * per + i] = local[:, i * SUB : (i + 1) * SUB]

        if c < chunks - EARLY:
            first_send(c)

    def first_send(c):
        @pl.when(here == 0)
        def _():
            for i in range(per):
                state_copy(c * per + i).start()

    def extra_copy(c):
        i = c - (chunks - EARLY)
        return remote(
            state_out.at[pl.ds(c * per, per)],
            extra.at[pl.ds(i * per, per)],
            extra_sem.at[0, i],
            extra_sem.at[1, i],
        )

    def early_send(c):
        @pl.when(here == 1)
        def _():
            extra_copy(c).start()

    def share(c, i):
        return carried[c][:, i * SUB : (i + 1) * SUB]

    def early_pass(c):
        g = c * CHUNK // group_width

        @pl.when(here == 2)
        def _():
            extra_copy(c).wait_recv()
            for i in range(per):
                at = c * per + i
                early = extra[at - (chunks - EARLY) * per]
                state_out[at] = (ready[at] + dot(c_ahead[g], early) * share(c, i)).astype(BF16)
                state_copy(at).start()

    def late_pass(c):
        g = c * CHUNK // group_width

        @pl.when(here == 1)
        def _():
            if c == chunks - EARLY:
                own_v.wait_recv()
            extra_copy(c).wait_send()
            for i in range(per):
                at = c * per + i
                state_copy(at).wait_recv()
                sent = dot(c_ahead[g], state_in[at]) * share(c, i)
                if value_base <= at < value_base + kv_local:
                    col = (at - value_base) * ADIM
                    sent = jnp.where(spare, kv[1, :, col : col + ADIM].astype(F32), sent)
                state_out[at] = sent.astype(BF16)
                state_copy(at).start()

    def make_ready(cs):
        cs = list(cs)

        @pl.when(middle if cs[-1] < chunks - EARLY else here == 2)
        def _():
            for c in cs:
                g = c * CHUNK // group_width
                for i in range(per):
                    at = c * per + i
                    sent = dot(c_next[g], state_out[at])
                    for base, slot in ((0, 0), (value_base, 1)):
                        if base <= at < base + kv_local:
                            col = (at - base) * ADIM
                            far = kv[slot, :, col : col + ADIM].astype(F32)
                            sent = jnp.where(spare, far, sent)
                    ready[at] = sent

    def pass_on(c):
        g = c * CHUNK // group_width

        @pl.when(middle)
        def _():
            for i in range(per):
                at = c * per + i
                state_copy(at).wait_recv()
                state_out[at] = (
                    ready[at]
                    + dot(c_ahead[g], state_in[at]) * carried[c][:, i * SUB : (i + 1) * SUB]
                ).astype(BF16)
                state_copy(at).start()

    def arrive(c):
        @pl.when(here >= (2 if c >= chunks - EARLY else n - 1))
        def _():
            for i in range(per):
                state_copy(c * per + i).wait_recv()

    per_kv = q_ref.shape[1] // (ADIM * kv_local)
    scale = ADIM**-0.5 * LOG2E

    def permitted_keys():
        count = 3 * rows
        key_pos = first - 2 * rows + lax.broadcasted_iota(jnp.int32, (rows, count), 1)
        return (doc_of(key_pos) == wide(doc_i, count)) & (key_pos <= wide(pos_i, count))

    totals = []

    def weigh(head, permitted):
        g = head // per_kv
        cols = slice(g * ADIM, (g + 1) * ADIM)
        keys = jnp.concatenate([state_in[g], kv[0, :, cols], k_ref[:, cols]], axis=0)
        query = q_ref[:, head * ADIM : (head + 1) * ADIM]
        scores = lax.dot_general(query, keys, NT, preferred_element_type=F32)
        scores = jnp.where(permitted, scores, NEGATIVE)
        peak = jnp.max(scores, axis=1, keepdims=True)
        expo = jnp.exp2((scores - peak) * scale)
        totals.append(jnp.sum(expo, axis=1, keepdims=True))
        weights[head] = expo.astype(BF16)

    def gather(head):
        g = head // per_kv
        cols = slice(g * ADIM, (g + 1) * ADIM)
        values = jnp.concatenate(
            [state_in[value_base + g], kv[1, :, cols], v_ref[:, cols]], axis=0
        )
        summed = dot(weights[head], values)
        attn_ref[:, head * ADIM : (head + 1) * ADIM] = (summed / totals[head]).astype(BF16)

    def inside(c):
        at = c * CHUNK
        g = at // group_width
        gate = silu(z_ref[:, at : at + CHUNK].astype(F32))
        for pair in range(CHUNK // 128):
            col = at + pair * 128
            head = col // HDIM
            parts = []
            for h in (head, head + 1):
                exponent = running[:, h : h + 1] - row_of[h : h + 1, :]
                parts.append(
                    (jnp.exp2(jnp.where(linked, exponent, NEGATIVE)) * crossed[g]).astype(BF16)
                )
            x_pair = xc[:, col : col + 128]
            zero = jnp.zeros_like(x_pair)
            stacked = jnp.concatenate(
                [jnp.where(low_half, x_pair, zero), jnp.where(low_half, zero, x_pair)], axis=0
            )
            within = dot(jnp.concatenate(parts, axis=1), stacked)
            gated[:, col : col + 128] = (gated[:, col : col + 128] + within) * gate[
                :, pair * 128 : (pair + 1) * 128
            ]
        gate_entry[:, at : at + CHUNK] = gate_entry[:, at : at + CHUNK] * gate

    squares = {}

    def finish(c):
        at = c * CHUNK
        g = at // group_width
        came = jnp.concatenate([state_in[c * per + i] for i in range(per)], axis=1)
        if c >= chunks - EARLY:
            base = (c - (chunks - EARLY)) * per
            local = jnp.concatenate([extra[base + i] for i in range(per)], axis=1)
            theirs = jnp.where(here == 2, unit, c_groups[g].astype(F32)).astype(BF16)
            product = dot(theirs, came) + dot(c_own[g], local)
        else:
            product = dot(c_groups[g], came)
        value = gated[:, at : at + CHUNK] + product * gate_entry[:, at : at + CHUNK]
        gated[:, at : at + CHUNK] = value
        for i in range(CHUNK // 128):
            piece = value[:, i * 128 : (i + 1) * 128]
            squares[g] = squares[g] + piece * piece if g in squares else piece * piece

    def normalize(g):
        left = g * group_width
        mean = jnp.sum(squares[g], axis=1, keepdims=True) * (1.0 / group_width)
        mamba_ref[:, left : left + group_width] = (
            gated[:, left : left + group_width]
            * lax.rsqrt(mean + EPSILON)
            * gain_ref[:, left : left + group_width]
        ).astype(BF16)

    fetches[11].wait()

    def take_keys():
        @pl.when(has_left)
        def _():
            own_k.wait_recv()

        @pl.when(here >= 2)
        def _():
            own_v.wait_recv()

    def send_values():
        @pl.when(here == 0)
        def _():
            own_v.start()

    def take_turned():
        @pl.when(middle)
        def _():
            c_back.wait_recv()
            for g in range(groups):
                theirs = c_next[g].astype(F32)
                c_ahead[g] = jnp.where(ahead, theirs, 0.0).astype(BF16)
                c_next[g] = jnp.where(ahead, theirs, unit).astype(BF16)

    def take_rest():
        for fetch in fetches[12:]:
            fetch.wait()

    held = []

    def attend_next(head):
        if not held:
            held.append(permitted_keys())
        weigh(head, held[0])

    steps = {
        "l": make_local, "q": lambda c: make_ready(range(2 * c, 2 * c + 2)), "g": gather,
        "u": lambda _: send_values(), "p": pass_on, "n": normalize,
        "e": early_send, "x": early_pass, "y": late_pass, "o": first_send, "r": arrive, "i": inside, "a": attend_next, "f": finish,
        "k": lambda _: take_keys(), "t": lambda _: take_turned(), "w": lambda _: take_rest(),
    }
    for name, low_end, high_end in ORDER:
        for at in range(low_end, high_end):
            steps[name](at)

    @pl.when(has_right)
    def _():
        halo_copy.wait_send()
        own_k.wait_send()
        own_v.wait_send()
        for i in range(chunks * per):
            state_copy(i).wait_send()

    @pl.when(here >= 2)
    def _():
        c_back.wait_send()


def write_out(mamba_ref, attn_ref, mamba_hbm, attn_hbm, sems):
    copies = [
        pltpu.make_async_copy(mamba_ref, mamba_hbm, sems.at[0]),
        pltpu.make_async_copy(attn_ref, attn_hbm, sems.at[1]),
    ]
    for copy in copies:
        copy.start()
    for copy in copies:
        copy.wait()


def shards(n, *args):
    (
        x_raw, bc_raw, z_gate, dt_raw, cxw, cxb, cbw, cbb, dtb, a_log, skip_d, gain, queries, keys,
        values, doc_lens,
    ) = args
    operands = (
        x_raw, bc_raw, z_gate, dt_raw.T, cxw, cxb[None], cbw, cbb[None], dtb[None], a_log[None],
        skip_d[None], gain[None], queries, keys, values, doc_lens,
    )
    rows, width = x_raw.shape
    bc_width = bc_raw.shape[1]
    chunks = width // CHUNK
    reach = max(1, n // 2)
    vmem = pl.BlockSpec(memory_space=pltpu.VMEM)
    dma = pltpu.SemaphoreType.DMA
    if n == 4 and rows == STATE and keys.shape[1] == CHUNK and width == 8 * CHUNK and (
        queries.shape[1] == 8 * ADIM
    ):
        subs = width // SUB
        state = pltpu.VMEM((subs, STATE, SUB), BF16)
        turned = pltpu.VMEM((bc_width // (2 * STATE), rows, STATE), BF16)
        body = functools.partial(packed_kernel, n)
        ready = pltpu.VMEM((subs, rows, SUB), F32)
        buffers = [pltpu.VMEM((2,) + keys.shape, BF16), state, state, turned, turned, turned, ready]
        buffers.append(pltpu.VMEM((EARLY * CHUNK // SUB, STATE, SUB), BF16))
        buffers.append(pltpu.VMEM((queries.shape[1] // ADIM, rows, 3 * rows), BF16))
        sems = [dma((2,)), dma((2,)), dma((subs,)), dma((subs,)), dma((2,)), dma((2, EARLY))]
    else:
        state = pltpu.VMEM((chunks, STATE, CHUNK), BF16)
        body = functools.partial(relay_kernel, n, reach)
        buffers = [pltpu.VMEM((reach, 2) + keys.shape, BF16), state, state]
        sems = [dma((reach, 2)), dma((reach, 2)), dma((chunks,)), dma((chunks,))]
    results = pl.pallas_call(
        body,
        out_shape=(pltpu.VMEM((rows, width), BF16), pltpu.VMEM(queries.shape, BF16)),
        in_specs=[pl.BlockSpec(memory_space=pltpu.HBM)] * 16,
        out_specs=(vmem, vmem),
        scratch_shapes=[
            pltpu.VMEM((16, bc_width), BF16),
            pltpu.VMEM((16, bc_width), BF16),
        ]
        + buffers
        + [
            pltpu.VMEM((rows + 8, width), F32),
            pltpu.VMEM((rows + 8, bc_width), F32),
            pltpu.VMEM((rows, width), BF16),
            pltpu.VMEM((rows, width), F32),
            pltpu.VMEM((rows, width), F32),
            dma,
            dma,
        ]
        + sems
        + [dma((17,)), pltpu.VMEM((16, width), BF16)]
        + [pltpu.VMEM(a.shape, a.dtype) for a in operands[:-1]]
        + [pltpu.SMEM(doc_lens.shape, jnp.int32)],
        compiler_params=pltpu.CompilerParams(
            collective_id=0, has_side_effects=True, vmem_limit_bytes=60 * 1024 * 1024
        ),
    )(*operands)
    hbm = pl.BlockSpec(memory_space=pltpu.HBM)
    return pl.pallas_call(
        write_out,
        out_shape=(
            jax.ShapeDtypeStruct((rows, width), BF16),
            jax.ShapeDtypeStruct(queries.shape, BF16),
        ),
        in_specs=[vmem, vmem],
        out_specs=(hbm, hbm),
        scratch_shapes=[dma((2,))],
    )(*[pltpu.with_memory_space_constraint(r, pltpu.VMEM) for r in results])


def solution(mesh):
    both = P(("groups", "seq"), "dp")
    placed = (
        both, both, both, both, P(None, "dp"), P("dp"), P(None, "dp"), P("dp"), P("dp"), P("dp"),
        P("dp"), P("dp"), both, both, both, P("groups"),
    )
    return jax.shard_map(
        functools.partial(shards, mesh.shape["seq"]),
        mesh=mesh,
        in_specs=placed,
        out_specs=(both, both),
        check_vma=False,
    )
```
